32 devices in a mesh: seq: 8 (over z, y), dp: 4 (over x, core).
Axes of the slice: x: 2, y: 2, z: 4, core: 2. Of those that a mesh axis runs over, the one named last changes fastest.
Arguments:
- queries: bfloat16 [4, 1024, 1024], P('dp', 'seq'), may hold values from -150 to 150
- key_states: bfloat16 [4, 1024, 1024], P('dp', 'seq'), may hold values from -6 to 6
- values: bfloat16 [4, 1024, 1024], P('dp', 'seq'), may hold values from -6 to 6
- w_out: bfloat16 [1024, 1024], replicated, may hold values from -0.1875 to 0.1875
- cotangent: bfloat16 [4, 1024, 1024], P('dp', 'seq'), may hold values from -6 to 6
- neighbours: int32 [4, 8, 2], P('dp', 'seq'), may hold values from 0 to 7, as said below
- counts: int32 [4, 8], P('dp', 'seq'), may hold values from 1 to 2
Outputs:
- output: bfloat16 [4, 1024, 1024], P('dp', 'seq')
- grad_queries: bfloat16 [4, 1024, 1024], P('dp', 'seq')
- grad_keys: bfloat16 [4, 1024, 1024], P('dp', 'seq')
- grad_values: bfloat16 [4, 1024, 1024], P('dp', 'seq')
- grad_w_out: float32 [1024, 1024], P(('seq', 'dp'))
The draws below stay inside these ranges and needn't reach their ends.
Inputs may be any that keep to these rules, and one draw needn't show every extreme that they name: `neighbours`: entries j < counts[s, p] of patch p's list are distinct patches other than p, at most 1 patches away from p; the later entries equal p.
All inputs are finite; a program needn't handle non-finite values.
Results may differ from the reference program's by a relative error of at most 0.029.
Values may be sent and summed in bfloat16 or wider, within the bound.
No kernel may reach another device: no remote copies, remote signals or barrier semaphores. Data moves between devices by JAX's collectives and lax.ppermute only.
A program may use at most 64 MiB of HBM per device.

```python
import math
import jax
import jax.numpy as jnp
from jax import lax

PATCH = 128
HEADS = 8
HD = 128
DW = 1024
NB = 2
REACH = 1
HW = 1024
NPATCH = 8
SEQLEN = 1024
SAMPLES = 4


def query_key_pair(key):
    base_key = jax.random.fold_in(key, 7)
    draw_one, draw_two = jax.random.split(base_key, 2)
    full_shape = (SAMPLES, SEQLEN, HEADS * HD)
    drawn_keys = jnp.clip(jax.random.normal(draw_one, full_shape, jnp.float32), -5.0, 5.0)
    key_out = drawn_keys
    query_out = 2.0 * jnp.clip(jax.random.normal(draw_two, full_shape, jnp.float32), -5.0, 5.0)
    return (query_out, key_out)


def draw_queries(key, part):
    return query_key_pair(key)[0].astype(jnp.bfloat16)


def draw_key_states(key, part):
    return query_key_pair(key)[1].astype(jnp.bfloat16)


def neighbour_table(key):
    base_key = jax.random.fold_in(key, 11)
    draw_one, draw_two = jax.random.split(base_key, 2)
    patch_ids = jnp.arange(NPATCH, dtype=jnp.int32)[None, :, None]
    steps_away = jnp.concatenate([jnp.arange(-REACH, 0, dtype=jnp.int32), jnp.arange(1, REACH + 1, dtype=jnp.int32)])
    targets = patch_ids + steps_away[None, None, :]
    inside = (targets >= 0) & (targets < NPATCH)
    ranking = jax.random.randint(draw_one, (SAMPLES, NPATCH, 2 * REACH), 0, 4096, dtype=jnp.int32) * 16
    ranking = ranking + jnp.arange(2 * REACH, dtype=jnp.int32)[None, None, :] + jnp.where(inside, 0, 1 << 20).astype(jnp.int32)
    ranked_order = jnp.argsort(ranking, axis=-1)
    picked = jnp.take_along_axis(jnp.broadcast_to(targets, ranking.shape), ranked_order, axis=-1)[:, :, :NB]
    capacity = jnp.minimum(jnp.sum(inside.astype(jnp.int32), axis=-1), NB)
    raw_count = jax.random.randint(draw_two, (SAMPLES, NPATCH), 0, 1 << 16, dtype=jnp.int32) % capacity + 1
    middle = (jnp.arange(NPATCH) == NPATCH // 2)[None, :]
    live_count = jnp.where(middle, NB, raw_count).astype(jnp.int32)
    slot_ids = jnp.arange(NB, dtype=jnp.int32)
    neighbour_ids = jnp.where(slot_ids[None, None, :] < live_count[:, :, None], picked, patch_ids)
    return (neighbour_ids.astype(jnp.int32), live_count)


def draw_neighbours(key, part):
    return neighbour_table(key)[0]


def draw_counts(key, part):
    return neighbour_table(key)[1]


def steps_of(stream_key, dims, pieces, low, largest):
    def one(dim, blocks):
        draws = jax.random.uniform(jax.random.fold_in(jax.random.fold_in(stream_key, 6), dim), (blocks,), jnp.float32, low / len(pieces), largest / len(pieces))
        return jnp.repeat(jnp.exp(draws), dims[dim] // blocks).reshape((-1,) + (1,) * (len(dims) - dim - 1))

    loudness = one(*pieces[0])
    for cut in pieces[1:]:
        loudness = loudness * one(*cut)
    return loudness


def noise(key, dims, scale, most, cuts=(), kind=jnp.bfloat16):
    entries = jax.random.normal(key, dims, jnp.float32) * scale
    if len(cuts) > 0:
        entries = steps_of(key, dims, cuts, -0.22, 0.18) * entries
    return jnp.clip(entries, min=-most, max=most).astype(kind)


def setup_inputs(seed: int = 0) -> dict:
    arg_keys = jax.random.split(jax.random.key(seed), 8)
    return {
        "queries": draw_queries(jax.random.fold_in(arg_keys[7], 71), 0),
        "key_states": draw_key_states(jax.random.fold_in(arg_keys[7], 71), 0),
        "values": noise(arg_keys[2], (SAMPLES, SEQLEN, HW), 1.0, 6.0, ((0, 4), (1, 8))),
        "w_out": noise(arg_keys[3], (HW, DW), HW ** -0.5, 0.1875),
        "cotangent": noise(arg_keys[4], (SAMPLES, SEQLEN, DW), 1.0, 6.0, ((0, 4), (1, 8))),
        "neighbours": draw_neighbours(jax.random.fold_in(arg_keys[7], 71), 0),
        "counts": draw_counts(jax.random.fold_in(arg_keys[7], 71), 0),
    }


def to_low(array):
    return lax.optimization_barrier(array.astype(jnp.bfloat16)).astype(jnp.float32)

def patch_terms(query_rows, key_window, value_window, allowed, w_out, cot_rows):
    score_scale = 1.0 / math.sqrt(HD)
    high = lax.Precision.HIGHEST
    query_heads = query_rows.astype(jnp.float32).reshape(PATCH, HEADS, HD)
    key_heads = key_window.astype(jnp.float32).reshape(-1, HEADS, HD)
    value_heads = value_window.astype(jnp.float32).reshape(-1, HEADS, HD)
    scores = jnp.einsum('qhd,khd->hqk', query_heads, key_heads, precision=high) * score_scale
    scores = jnp.where(allowed[None, None, :], scores, -jnp.inf)
    row_max = lax.optimization_barrier(jnp.max(scores, axis=-1, keepdims=True))
    log_total = row_max + jnp.log(lax.optimization_barrier(jnp.sum(jnp.exp(scores - row_max), axis=-1, keepdims=True)))
    attn_probs = jnp.exp(scores - log_total)
    probs_low = to_low(attn_probs)
    attended = jnp.einsum('hqk,khd->qhd', probs_low, value_heads, precision=high)
    attended = attended.reshape(PATCH, HEADS * HD).astype(jnp.bfloat16)
    output = jnp.dot(attended, w_out, preferred_element_type=jnp.float32).astype(jnp.bfloat16)
    grad_attended = jnp.dot(cot_rows, w_out.T, preferred_element_type=jnp.float32).astype(jnp.bfloat16)
    grad_heads = grad_attended.astype(jnp.float32).reshape(PATCH, HEADS, HD)
    attn_heads = attended.astype(jnp.float32).reshape(PATCH, HEADS, HD)
    row_delta = lax.optimization_barrier(jnp.sum(grad_heads * attn_heads, axis=-1)).T[:, :, None]
    grad_probs = jnp.einsum('qhd,khd->hqk', grad_heads, value_heads, precision=high)
    grad_scores = to_low(attn_probs * (grad_probs - row_delta))
    grad_query = jnp.einsum('hqk,khd->qhd', grad_scores, key_heads, precision=high) * score_scale
    grad_query = grad_query.reshape(PATCH, HEADS * HD).astype(jnp.bfloat16)
    key_parts = jnp.einsum('hqk,qhd->khd', grad_scores, query_heads, precision=high) * score_scale
    key_parts = key_parts.reshape(-1, PATCH, HEADS * HD).astype(jnp.bfloat16)
    value_parts = jnp.einsum('hqk,qhd->khd', probs_low, grad_heads, precision=high)
    value_parts = value_parts.reshape(-1, PATCH, HEADS * HD).astype(jnp.bfloat16)
    weight_term = to_low(jnp.dot(attended.T, cot_rows, preferred_element_type=jnp.float32))
    return (output, grad_query, key_parts, value_parts, weight_term)

def collect(parts):
    span = 2 * REACH + 1
    summed = jnp.zeros((NPATCH, PATCH, HEADS * HD), jnp.float32)
    for position in range(span):
        offset = position - REACH
        padded = jnp.pad(parts[:, position].astype(jnp.float32), ((REACH, REACH), (0, 0), (0, 0)))
        summed = summed + padded[REACH - offset:REACH - offset + NPATCH]
    return summed.astype(jnp.bfloat16).reshape(SEQLEN, HEADS * HD)

def reference(queries, key_states, values, w_out, cotangent, neighbours, counts):
    span = 2 * REACH + 1

    def one_sample(inputs):
        query_all, key_all, value_all, cot_all, neighbour_ids, live_counts = inputs
        key_pad = jnp.pad(key_all.reshape(NPATCH, PATCH, HEADS * HD), ((REACH, REACH), (0, 0), (0, 0)))
        value_pad = jnp.pad(value_all.reshape(NPATCH, PATCH, HEADS * HD), ((REACH, REACH), (0, 0), (0, 0)))
        offsets = jnp.arange(-REACH, REACH + 1, dtype=jnp.int32)
        slot_ids = jnp.arange(NB, dtype=jnp.int32)

        def one_patch(patch_id):
            first_row = (patch_id * PATCH).astype(jnp.int32)
            query_rows = lax.dynamic_slice_in_dim(query_all, first_row, PATCH, 0)
            cot_rows = lax.dynamic_slice_in_dim(cot_all, first_row, PATCH, 0)
            key_window = lax.dynamic_slice_in_dim(key_pad, patch_id, span, 0).reshape(span * PATCH, HEADS * HD)
            value_window = lax.dynamic_slice_in_dim(value_pad, patch_id, span, 0).reshape(span * PATCH, HEADS * HD)
            matches = (neighbour_ids[patch_id][None, :] == patch_id + offsets[:, None]) & (slot_ids[None, :] < live_counts[patch_id])
            live_slots = jnp.any(matches, axis=1) | (offsets == 0)
            allowed = jnp.repeat(live_slots, PATCH)
            return patch_terms(query_rows, key_window, value_window, allowed, w_out, cot_rows)
        output, grad_query, key_parts, value_parts, weight_terms = lax.map(one_patch, jnp.arange(NPATCH, dtype=jnp.int32))
        return (output.reshape(SEQLEN, DW), grad_query.reshape(SEQLEN, HEADS * HD), collect(key_parts), collect(value_parts), lax.optimization_barrier(jnp.sum(weight_terms, axis=0)))
    output, grad_queries, grad_keys, grad_values, weight_sums = lax.map(one_sample, (queries, key_states, values, cotangent, neighbours, counts))
    grad_w_out = lax.optimization_barrier(jnp.sum(weight_sums, axis=0))
    return (output, grad_queries, grad_keys, grad_values, grad_w_out)
```

```python
import functools
import math

import jax
import jax.numpy as jnp
from jax import lax
from jax.experimental import pallas as pl
from jax.experimental.pallas import tpu as pltpu
from jax.sharding import PartitionSpec as P

HD = 128
VMEM_LIMIT = 32 * 1024 * 1024
F32 = jnp.float32
BF16 = jnp.bfloat16


def dot(a, b, ca, cb):
    return lax.dot_general(a, b, (((ca,), (cb,)), ((), ())), preferred_element_type=F32)


def bit_reversed(index, bits):
    out = 0
    for b in range(bits):
        out = (out << 1) | ((index >> b) & 1)
    return out


def attention_kernel(direct, n_dp, flags, q, k0, v0, ky, vy, kz, vz, ga, att, att_t, dq, dk0, dv0, dky, dvy, dkz, dvz):
    scale = 1.0 / math.sqrt(HD)
    heads = q.shape[1] // HD
    ks, vs = (k0, ky, kz), (v0, vy, vz)
    dks, dvs = (dk0, dky, dkz), (dv0, dvy, dvz)
    bits = (heads - 1).bit_length()
    for h in range(heads):
        cols = slice(h * HD, (h + 1) * HD)
        qh, gh = q[:, cols], ga[:, cols]
        kh = [k[:, cols] for k in ks]
        vh = [v[:, cols] for v in vs]
        s = [dot(k, qh, 1, 1) * scale for k in kh]
        s[1] = jnp.where(flags[0] > 0, s[1], -jnp.inf)
        s[2] = jnp.where(flags[1] > 0, s[2], -jnp.inf)
        top = jnp.max(jnp.maximum(jnp.maximum(s[0], s[1]), s[2]), axis=0, keepdims=True)
        e = [jnp.exp(x - top) for x in s]
        total = jnp.sum(e[0] + e[1] + e[2], axis=0, keepdims=True)
        inv = 1.0 / total
        p = [x * inv for x in e]
        low = [x.astype(BF16) for x in p]
        o_t = dot(vh[0], low[0], 0, 0) + dot(vh[1], low[1], 0, 0) + dot(vh[2], low[2], 0, 0)
        att[:, cols] = o_t.T.astype(BF16)
        o_low = o_t.astype(BF16)
        if direct:
            rows = HD // n_dp
            slot = flags[2] ^ h
            place = 0
            for b in range(bits):
                place = place * 2 + ((slot >> b) & 1)
            start = pl.multiple_of(place * rows, rows)
            for d in range(n_dp):
                att_t[d, pl.ds(start, rows), :] = o_low[d * rows : (d + 1) * rows, :]
        else:
            att_t[cols, :] = o_low
        g = [dot(v, gh, 1, 1) for v in vh]
        delta = jnp.sum(p[0] * g[0] + p[1] * g[1] + p[2] * g[2], axis=0, keepdims=True)
        ds = [(p[i] * (g[i] - delta)).astype(BF16) for i in range(3)]
        dq[:, cols] = (
            (dot(ds[0], kh[0], 0, 0) + dot(ds[1], kh[1], 0, 0) + dot(ds[2], kh[2], 0, 0)) * scale
        ).astype(BF16)
        for i in range(3):
            dks[i][:, cols] = (dot(ds[i], qh, 1, 0) * scale).astype(BF16)
            dvs[i][:, cols] = dot(low[i], gh, 1, 0).astype(BF16)


def attention(flags, q, k0, v0, ky, vy, kz, vz, ga, n_seq, n_dp):
    tokens, features = q.shape
    heads = features // HD
    direct = n_seq == heads and HD % n_dp == 0 and (HD // n_dp) % 16 == 0
    vmem = pl.BlockSpec(memory_space=pltpu.VMEM)
    block = jax.ShapeDtypeStruct((tokens, features), BF16)
    turned = (n_dp, features // n_dp, tokens) if direct else (features, tokens)
    result = pl.pallas_call(
        functools.partial(attention_kernel, direct, n_dp),
        out_shape=(block, jax.ShapeDtypeStruct(turned, BF16)) + (block,) * 7,
        in_specs=[pl.BlockSpec(memory_space=pltpu.SMEM)] + [vmem] * 8,
        out_specs=(vmem,) * 9,
        compiler_params=pltpu.CompilerParams(vmem_limit_bytes=VMEM_LIMIT),
        cost_estimate=pl.CostEstimate(
            flops=6 * 2 * tokens * 3 * tokens * features,
            bytes_accessed=17 * tokens * features * 2,
            transcendentals=heads * tokens * tokens * 3,
        ),
        name="patch_attention",
    )(flags, q, k0, v0, ky, vy, kz, vz, ga)
    if not direct:
        bits = (n_seq - 1).bit_length()
        order = jnp.array([bit_reversed(i, bits) for i in range(n_seq)], jnp.int32) ^ flags[2]
        turned = result[1].reshape(n_seq, n_dp, features // (n_seq * n_dp), tokens)
        turned = jnp.take(turned, order, axis=0).transpose(1, 0, 2, 3)
        turned = turned.reshape(n_dp, features // n_dp, tokens)
        result = (result[0], turned) + tuple(result[2:])
    return result


def weight_kernel(n, *refs):
    att_refs, cot_refs, (keep, send) = refs[:n], refs[n : 2 * n], refs[2 * n :]
    half = keep.shape[0]
    for target, start in ((send, half), (keep, 0)):
        total = dot(att_refs[0][start : start + half, :], cot_refs[0][...], 1, 0)
        for i in range(1, n):
            total += dot(att_refs[i][start : start + half, :], cot_refs[i][...], 1, 0)
        target[...] = total.astype(target.dtype)


def weight_terms(att_parts, cot_parts):
    n = len(att_parts)
    rows = att_parts[0].shape[0]
    tokens, width = cot_parts[0].shape
    vmem = pl.BlockSpec(memory_space=pltpu.VMEM)
    return pl.pallas_call(
        functools.partial(weight_kernel, n),
        out_shape=(
            jax.ShapeDtypeStruct((rows // 2, width), F32),
            jax.ShapeDtypeStruct((rows // 2, width), BF16),
        ),
        in_specs=[vmem] * (2 * n),
        out_specs=(vmem, vmem),
        compiler_params=pltpu.CompilerParams(vmem_limit_bytes=VMEM_LIMIT),
        cost_estimate=pl.CostEstimate(
            flops=2 * rows * n * tokens * width,
            bytes_accessed=n * (rows + width) * tokens * 2 + rows * width * 3,
            transcendentals=0,
        ),
        name="weight_terms",
    )(*att_parts, *cot_parts)


def on_device(queries, key_states, values, w_out, cotangent, neighbours, counts):
    q, k0, v0, cot = queries[0], key_states[0], values[0], cotangent[0]
    n_seq, n_dp = lax.axis_size("seq"), lax.axis_size("dp")
    me, my_dp = lax.axis_index("seq"), lax.axis_index("dp")

    swap = [(i, i ^ 1) for i in range(n_seq)]
    onward = [(i, i + 2) for i in range(0, n_seq, 2) if i + 2 < n_seq]
    onward += [(i, i - 2) for i in range(1, n_seq, 2) if i - 2 >= 0]
    backward = [(b, a) for a, b in onward]
    send = lambda x, pairs: lax.ppermute(x, "seq", pairs)

    ky, vy = send(k0, swap), send(v0, swap)
    kz, vz = send(ky, onward), send(vy, onward)
    across = lambda x, k: lax.ppermute(x, "dp", [(i, i ^ k) for i in range(n_dp)])
    cots = [cot] + [across(cot, k) for k in range(1, n_dp)]
    ga = dot(cot, w_out, 1, 1).astype(BF16)

    listed, live = neighbours[0, 0], counts[0, 0]
    used = jnp.arange(listed.shape[0], dtype=jnp.int32) < live
    near = me ^ 1
    far = jnp.where(me % 2 == 0, me - 1, me + 1)
    flag = lambda patch: jnp.any((listed == patch) & used).astype(jnp.int32)
    flags = jnp.stack([flag(near), flag(far), me.astype(jnp.int32)])

    att, att_t, dq, dk0, dv0, dky, dvy, dkz, dvz = attention(
        flags, q, k0, v0, ky, vy, kz, vz, ga, n_seq, n_dp
    )

    add = lambda a, b: (a.astype(F32) + b.astype(F32)).astype(BF16)
    dk_near = add(dky, send(dkz, backward))
    dv_near = add(dvy, send(dvz, backward))
    dk = add(dk0, send(dk_near, swap))
    dv = add(dv0, send(dv_near, swap))

    pieces = [lax.dynamic_index_in_dim(att_t, my_dp ^ k, 0, keepdims=False) for k in range(n_dp)]
    parts = [pieces[0]] + [across(pieces[k], k) for k in range(1, n_dp)]
    keep, out = weight_terms(parts, cots)
    step = 1
    while True:
        total = keep + send(out, [(i, i ^ step) for i in range(n_seq)]).astype(F32)
        step *= 2
        if step == n_seq:
            break
        half = total.shape[0] // 2
        keep, out = total[:half], total[half:].astype(BF16)

    output = dot(att, w_out, 1, 0).astype(BF16)
    return (output[None], dq[None], dk[None], dv[None], total)


def solution(mesh):
    placed = (
        P("dp", "seq", None),
        P("dp", "seq", None),
        P("dp", "seq", None),
        P(),
        P("dp", "seq", None),
        P("dp", "seq", None),
        P("dp", "seq"),
    )
    return jax.shard_map(
        on_device,
        mesh=mesh,
        in_specs=placed,
        out_specs=(
            P("dp", "seq", None),
            P("dp", "seq", None),
            P("dp", "seq", None),
            P("dp", "seq", None),
            P(("seq", "dp"), None),
        ),
        check_vma=False,
    )
```

```python
import functools
import math

import jax
import jax.numpy as jnp
from jax import lax
from jax.experimental import pallas as pl
from jax.experimental.pallas import tpu as pltpu
from jax.sharding import PartitionSpec as P

HD = 128
VMEM_LIMIT = 32 * 1024 * 1024
F32 = jnp.float32
BF16 = jnp.bfloat16
VMEM = pl.BlockSpec(memory_space=pltpu.VMEM)
SMEM = pl.BlockSpec(memory_space=pltpu.SMEM)
ANY = pl.BlockSpec(memory_space=pl.ANY)


def dot(a, b, ca, cb):
    return lax.dot_general(a, b, (((ca,), (cb,)), ((), ())), preferred_element_type=F32)


def bit_reversed(index, bits):
    out = 0
    for b in range(bits):
        out = out * 2 + ((index >> b) & 1)
    return out


def shape_of(*dims, dtype=BF16):
    return jax.ShapeDtypeStruct(dims, dtype)


def call(body, out_shape, in_specs, name, flops=0, moved=0, exps=0, scratch=()):
    return pl.pallas_call(
        body,
        out_shape=out_shape,
        in_specs=in_specs,
        out_specs=(VMEM,) * len(out_shape),
        scratch_shapes=list(scratch),
        compiler_params=pltpu.CompilerParams(vmem_limit_bytes=VMEM_LIMIT),
        cost_estimate=pl.CostEstimate(flops=flops, bytes_accessed=moved, transcendentals=exps),
        name=name,
    )


def head_cols(pair, parity):
    return pl.ds(pl.multiple_of((2 * pair + parity) * HD, HD), HD)


def pack_kernel(me, q, k, v, kv_send, kv_keep, q_send, q_keep, sems):
    mine = me[0] & 1
    pairs = q_send.shape[1] // HD
    copies = []
    for parity, kv_to, q_to in ((1 - mine, kv_send, q_send), (mine, kv_keep, q_keep)):
        for source, target in ((k, kv_to.at[0]), (v, kv_to.at[1]), (q, q_to)):
            for j in range(pairs):
                copies.append(
                    pltpu.make_async_copy(
                        source.at[:, head_cols(j, parity)],
                        target.at[:, j * HD : (j + 1) * HD],
                        sems.at[len(copies)],
                    )
                )
    for copy in copies:
        copy.start()
    for copy in copies:
        copy.wait()


def pack(me, q, k, v):
    tokens, features = q.shape
    both, one = shape_of(2, tokens, features // 2), shape_of(tokens, features // 2)
    return call(
        pack_kernel,
        (both, both, one, one),
        [SMEM, ANY, ANY, ANY],
        "pack_heads",
        moved=6 * tokens * features * 2,
        scratch=[pltpu.SemaphoreType.DMA((3 * features // HD,))],
    )(me, q, k, v)


def attention_kernel(
    direct, n_dp, flags, q_own, q_par, own, par, far_own, far_par, cot_own, cot_par, w,
    att_own, dq_own, back, att_t, d_own, d_par, d_far_own, d_far_par,
):
    rate = math.log2(math.e) / math.sqrt(HD)
    scale = 1.0 / math.sqrt(HD)
    tokens = q_own.shape[0]
    pairs = q_own.shape[1] // HD
    me = flags[4]
    left = lax.broadcasted_iota(jnp.int32, (1, 2 * tokens), 1) < tokens
    barred = lambda i: jnp.where(flags[i] > 0, 0.0, -jnp.inf)
    bias = (
        jnp.where(left, 0.0, barred(2)),
        jnp.where(left, barred(0), 0.0),
        jnp.where(left, barred(1), barred(3)),
    )
    for j in range(pairs):
        cols = slice(j * HD, (j + 1) * HD)
        wh = w[head_cols(j, me & 1), :]
        ga_own = dot(cot_own[...], wh, 1, 1).astype(BF16)
        ga_par = dot(cot_par[...], wh, 1, 1).astype(BF16)
        ga = jnp.concatenate([ga_own, ga_par], axis=0)
        qo, qp = q_own[:, cols], q_par[:, cols]
        q = jnp.concatenate([qo, qp], axis=0)
        k = jnp.concatenate([own[0, :, cols], par[0, :, cols]], axis=0)
        v = jnp.concatenate([own[1, :, cols], par[1, :, cols]], axis=0)
        kfo, kfp = far_own[0, :, cols], far_par[0, :, cols]
        vfo, vfp = far_own[1, :, cols], far_par[1, :, cols]
        near = dot(k, q, 1, 1)
        far = jnp.concatenate([dot(kfo, qo, 1, 1), dot(kfp, qp, 1, 1)], axis=1)
        s = [near[:tokens] + bias[0], near[tokens:] + bias[1], far + bias[2]]
        top = jnp.max(jnp.maximum(jnp.maximum(s[0], s[1]), s[2]), axis=0, keepdims=True)
        e = [jnp.exp2((x - top) * rate) for x in s]
        inv = 1.0 / jnp.sum(e[0] + e[1] + e[2], axis=0, keepdims=True)
        p = [x * inv for x in e]
        low = jnp.concatenate([p[0], p[1]], axis=0).astype(BF16)
        low_far = p[2].astype(BF16)
        lfo, lfp = low_far[:, :tokens], low_far[:, tokens:]
        o_t = dot(v, low, 0, 0) + jnp.concatenate([dot(vfo, lfo, 0, 0), dot(vfp, lfp, 0, 0)], axis=1)
        o = o_t.T.astype(BF16)
        att_own[:, cols] = o[:tokens]
        back[0, :, cols] = o[tokens:]
        o_low = o_t.astype(BF16)
        if direct:
            rows = HD // n_dp
            bits = (pairs - 1).bit_length()
            start = pl.multiple_of(bit_reversed(j ^ (me >> 1), bits) * rows, rows)
            for d in range(n_dp):
                att_t[d, pl.ds(start, rows), :] = o_low[d * rows : (d + 1) * rows, :]
        else:
            att_t[cols, :] = o_low
        gn = dot(v, ga, 1, 1)
        g = [
            gn[:tokens],
            gn[tokens:],
            jnp.concatenate([dot(vfo, ga_own, 1, 1), dot(vfp, ga_par, 1, 1)], axis=1),
        ]
        delta = jnp.sum(p[0] * g[0] + p[1] * g[1] + p[2] * g[2], axis=0, keepdims=True)
        ds = [p[i] * (g[i] - delta) for i in range(3)]
        dsn = jnp.concatenate([ds[0], ds[1]], axis=0).astype(BF16)
        dsf = ds[2].astype(BF16)
        dfo, dfp = dsf[:, :tokens], dsf[:, tokens:]
        dq = dot(dsn, k, 0, 0) + jnp.concatenate([dot(dfo, kfo, 0, 0), dot(dfp, kfp, 0, 0)], axis=0)
        dq = (dq * scale).astype(BF16)
        dq_own[:, cols] = dq[:tokens]
        back[1, :, cols] = dq[tokens:]
        dk = (dot(dsn, q, 1, 0) * scale).astype(BF16)
        dv = dot(low, ga, 1, 0).astype(BF16)
        d_own[0, :, cols] = dk[:tokens]
        d_par[0, :, cols] = dk[tokens:]
        d_own[1, :, cols] = dv[:tokens]
        d_par[1, :, cols] = dv[tokens:]
        d_far_own[0, :, cols] = (dot(dfo, qo, 1, 0) * scale).astype(BF16)
        d_far_par[0, :, cols] = (dot(dfp, qp, 1, 0) * scale).astype(BF16)
        d_far_own[1, :, cols] = dot(lfo, ga_own, 1, 0).astype(BF16)
        d_far_par[1, :, cols] = dot(lfp, ga_par, 1, 0).astype(BF16)


def attention(flags, q_own, q_par, own, par, far_own, far_par, cot_own, cot_par, w, n_seq, n_dp):
    tokens, features = cot_own.shape[0], w.shape[0]
    heads = features // HD
    direct = n_seq == heads and HD % n_dp == 0 and (HD // n_dp) % 16 == 0
    one, both = shape_of(tokens, features // 2), shape_of(2, tokens, features // 2)
    if direct:
        turned = shape_of(n_dp, features // 2 // n_dp, 2 * tokens)
    else:
        turned = shape_of(features // 2, 2 * tokens)
    result = call(
        functools.partial(attention_kernel, direct, n_dp),
        (one, one, both, turned, both, both, both, both),
        [SMEM] + [VMEM] * 9,
        "patch_attention",
        flops=2 * tokens * features * (18 * tokens + 1024),
        moved=24 * tokens * features,
        exps=heads * tokens * tokens * 3,
    )(flags, q_own, q_par, own, par, far_own, far_par, cot_own, cot_par, w)
    turned = result[3]
    if not direct:
        me = flags[4]
        bits = (n_seq - 1).bit_length()
        order = jnp.array([bit_reversed(i, bits) for i in range(n_seq)], jnp.int32) ^ me
        full = jnp.zeros((heads // 2, 2, HD, 2 * tokens), BF16)
        full = lax.dynamic_update_slice(
            full, turned.reshape(heads // 2, 1, HD, 2 * tokens), (0, me & 1, 0, 0)
        )
        full = full.reshape(n_seq, n_dp, features // (n_seq * n_dp), 2 * tokens)
        full = jnp.take(full, order, axis=0).transpose(1, 0, 2, 3)
        turned = full.reshape(n_dp, features // n_dp, 2 * tokens)
    return result[:3] + (turned, 2 if direct else 1) + result[4:]


def weight_kernel(n, *refs):
    att_refs, own_refs, par_refs = refs[:n], refs[n : 2 * n], refs[2 * n : 3 * n]
    keep, send = refs[3 * n :]
    half = keep.shape[0]
    tokens = own_refs[0].shape[0]
    for target, start in ((send, half), (keep, 0)):
        rows = slice(start, start + half)
        total = jnp.zeros(target.shape, F32)
        for i in range(n):
            total += dot(att_refs[i][rows, :tokens], own_refs[i][...], 1, 0)
            total += dot(att_refs[i][rows, tokens:], par_refs[i][...], 1, 0)
        target[...] = total.astype(target.dtype)


def weight_terms(att_parts, own_parts, par_parts):
    n = len(att_parts)
    rows = att_parts[0].shape[0]
    tokens, width = own_parts[0].shape
    return call(
        functools.partial(weight_kernel, n),
        (shape_of(rows // 2, width, dtype=F32), shape_of(rows // 2, width)),
        [VMEM] * (3 * n),
        "weight_terms",
        flops=4 * rows * n * tokens * width,
        moved=n * (rows + width) * tokens * 4 + rows * width * 3,
    )(*att_parts, *own_parts, *par_parts)


def query_kernel(me, att_own, dq_own, back, w, out, dq, att):
    mine = me[0] & 1
    for j in range(att_own.shape[1] // HD):
        cols = slice(j * HD, (j + 1) * HD)
        att[:, head_cols(j, mine)] = att_own[:, cols]
        att[:, head_cols(j, 1 - mine)] = back[0, :, cols]
        dq[:, head_cols(j, mine)] = dq_own[:, cols]
        dq[:, head_cols(j, 1 - mine)] = back[1, :, cols]
    out[...] = dot(att[...], w[...], 1, 0).astype(BF16)


def finish_queries(me, att_own, dq_own, back, w):
    tokens = att_own.shape[0]
    return call(
        query_kernel,
        (shape_of(tokens, w.shape[1]), shape_of(tokens, w.shape[0])),
        [SMEM] + [VMEM] * 4,
        "finish_queries",
        flops=2 * tokens * w.size,
        moved=2 * w.size + 8 * tokens * w.shape[0],
        scratch=[pltpu.VMEM((tokens, w.shape[0]), BF16)],
    )(me, att_own, dq_own, back, w)


def key_kernel(me, own, far, home, dk, dv):
    mine = me[0] & 1
    for i, target in ((0, dk), (1, dv)):
        for j in range(own.shape[2] // HD):
            cols = slice(j * HD, (j + 1) * HD)
            total = own[i, :, cols].astype(F32) + far[i, :, cols].astype(F32)
            target[:, head_cols(j, mine)] = total.astype(BF16)
            target[:, head_cols(j, 1 - mine)] = home[i, :, cols]


def finish_keys(me, own, far, home):
    tokens, half = own.shape[1:]
    return call(
        key_kernel,
        (shape_of(tokens, 2 * half), shape_of(tokens, 2 * half)),
        [SMEM] + [VMEM] * 3,
        "finish_keys",
        moved=10 * tokens * 2 * half,
    )(me, own, far, home)


def on_device(queries, key_states, values, w_out, cotangent, neighbours, counts):
    n_seq, n_dp = lax.axis_size("seq"), lax.axis_size("dp")
    me, my_dp = lax.axis_index("seq").astype(jnp.int32), lax.axis_index("dp")
    whoami = me.reshape(1)
    cot = cotangent[0]

    swap = [(i, i ^ 1) for i in range(n_seq)]
    relay = [(i, i + 2) for i in range(0, n_seq, 2) if i + 2 < n_seq]
    relay += [(i, i - 2) for i in range(1, n_seq, 2) if i - 2 >= 0]
    outer = [(b, a) for a, b in relay]
    send = lambda x, pairs: lax.ppermute(x, "seq", pairs)
    across = lambda x, k: lax.ppermute(x, "dp", [(i, i ^ k) for i in range(n_dp)])

    kv_send, own, q_send, q_own = pack(whoami, queries[0], key_states[0], values[0])
    par = send(kv_send, swap)
    far_par = send(own, outer)
    q_par = send(q_send, swap)
    cot_par = send(cot, swap)
    far_own = send(par, relay)

    listed, live = neighbours[0, 0], counts[0, 0]
    used = jnp.arange(listed.shape[0], dtype=jnp.int32) < live
    far_patch = jnp.where(me % 2 == 0, me - 1, me + 1)
    flag = lambda patch: jnp.any((listed == patch) & used).astype(jnp.int32)
    here = jnp.stack([flag(me ^ 1), flag(far_patch)])
    flags = jnp.concatenate([here, send(here, swap), whoami])

    def gathered(x):
        held = {0: x}
        bit = n_dp // 2
        while bit:
            for k in list(held):
                held[k | bit] = across(held[k], bit)
            bit //= 2
        return [held[k] for k in range(n_dp)]

    cots, cots_par = gathered(cot), gathered(cot_par)

    att_own, dq_own, back, att_t, step, d_own, d_par, d_far_own, d_far_par = attention(
        flags, q_own, q_par, own, par, far_own, far_par, cot, cot_par, w_out, n_seq, n_dp
    )

    returned = send(d_far_own, outer)
    pieces = [lax.dynamic_index_in_dim(att_t, my_dp ^ k, 0, keepdims=False) for k in range(n_dp)]
    parts = [pieces[0]] + [across(pieces[k], k) for k in range(1, n_dp)]
    back = send(back, swap)
    d_far = send(d_far_par, relay)
    home = send((d_par.astype(F32) + returned.astype(F32)).astype(BF16), swap)

    keep, out = weight_terms(parts, cots, cots_par)
    while True:
        total = keep + send(out, [(i, i ^ step) for i in range(n_seq)]).astype(F32)
        step *= 2
        if step == n_seq:
            break
        half = total.shape[0] // 2
        keep, out = total[:half], total[half:].astype(BF16)

    output, dq = finish_queries(whoami, att_own, dq_own, back, w_out)
    dk, dv = finish_keys(whoami, d_own, d_far, home)
    return (output[None], dq[None], dk[None], dv[None], total)


def solution(mesh):
    placed = (
        P("dp", "seq", None),
        P("dp", "seq", None),
        P("dp", "seq", None),
        P(),
        P("dp", "seq", None),
        P("dp", "seq", None),
        P("dp", "seq"),
    )
    return jax.shard_map(
        on_device,
        mesh=mesh,
        in_specs=placed,
        out_specs=(
            P("dp", "seq", None),
            P("dp", "seq", None),
            P("dp", "seq", None),
            P("dp", "seq", None),
            P(("seq", "dp"), None),
        ),
        check_vma=False,
    )
```

```python
import functools
import math

import jax
import jax.numpy as jnp
from jax import lax
from jax.experimental import pallas as pl
from jax.experimental.pallas import tpu as pltpu
from jax.sharding import PartitionSpec as P

HD = 128
VMEM_LIMIT = 32 * 1024 * 1024
F32 = jnp.float32
BF16 = jnp.bfloat16
VMEM = pl.BlockSpec(memory_space=pltpu.VMEM)
SMEM = pl.BlockSpec(memory_space=pltpu.SMEM)
HBM = pl.BlockSpec(memory_space=pltpu.HBM)
FLAG_ROWS = 16


def dot(a, b, ca, cb):
    return lax.dot_general(a, b, (((ca,), (cb,)), ((), ())), preferred_element_type=F32)


def bit_reversed(index, bits):
    out = 0
    for b in range(bits):
        out = out * 2 + ((index >> b) & 1)
    return out


def shape_of(*dims, dtype=BF16):
    return jax.ShapeDtypeStruct(dims, dtype)


def call(body, out_shape, in_specs, name, flops=0, moved=0, exps=0, scratch=()):
    return pl.pallas_call(
        body,
        out_shape=out_shape,
        in_specs=in_specs,
        out_specs=(VMEM,) * len(out_shape),
        scratch_shapes=list(scratch),
        compiler_params=pltpu.CompilerParams(vmem_limit_bytes=VMEM_LIMIT),
        cost_estimate=pl.CostEstimate(flops=flops, bytes_accessed=moved, transcendentals=exps),
        name=name,
    )


def head_cols(pair, parity):
    return pl.ds(pl.multiple_of((2 * pair + parity) * HD, HD), HD)


def listed_flags(me, listed, live):
    far_patch = jnp.where(me % 2 == 0, me - 1, me + 1)
    near, far = jnp.int32(0), jnp.int32(0)
    for slot in range(listed.shape[1]):
        used = slot < live[0, 0]
        near = jnp.where(used & (listed[0, slot] == (me ^ 1)), 1, near)
        far = jnp.where(used & (listed[0, slot] == far_patch), 1, far)
    return near, far


def pack_kernel(me, listed, live, q, k, v, cot, kv_send, kv_keep, cq_send, q_keep, sems):
    mine = me[0] & 1
    tokens, half = q_keep.shape
    pairs = half // HD
    copies = []

    def copy(source, target):
        copies.append(pltpu.make_async_copy(source, target, sems.at[len(copies)]))
        copies[-1].start()

    for kv, q_to, q_row, parity in ((kv_send, cq_send, 2 * tokens, 1 - mine), (kv_keep, q_keep, 0, mine)):
        for source, target, row in ((k, kv, 0), (v, kv, tokens), (q, q_to, q_row)):
            for j in range(pairs):
                copy(
                    source.at[:, head_cols(j, parity)],
                    target.at[row : row + tokens, j * HD : (j + 1) * HD],
                )
    for i in range(2):
        copy(cot.at[:, i * half : (i + 1) * half], cq_send.at[i * tokens : (i + 1) * tokens, :])
    near, far = listed_flags(me[0], listed, live)
    left = lax.broadcasted_iota(jnp.int32, (FLAG_ROWS, half), 1) < half // 2
    flags = jnp.where(left, near, far).astype(F32).astype(BF16)
    cq_send[3 * tokens : 3 * tokens + FLAG_ROWS, :] = flags
    for item in copies:
        item.wait()


def pack(me, listed, live, q, k, v, cot):
    tokens, features = q.shape
    half = features // 2
    kv, one = shape_of(2 * tokens, half), shape_of(tokens, half)
    return call(
        pack_kernel,
        (kv, kv, shape_of(3 * tokens + FLAG_ROWS, half), one),
        [SMEM] * 3 + [HBM] * 4,
        "pack_heads",
        moved=8 * tokens * features * 2,
        scratch=[pltpu.SemaphoreType.DMA((3 * features // HD + 2,))],
    )(me, listed, live, q, k, v, cot)


def turn_kernel(me, cot, w, ga, w_half, cot_in, sems):
    pairs = ga.shape[1] // HD
    first = pltpu.make_async_copy(cot, cot_in, sems.at[pairs])
    first.start()
    rows = [
        pltpu.make_async_copy(
            w.at[head_cols(j, me[0] & 1), :], w_half.at[j * HD : (j + 1) * HD, :], sems.at[j]
        )
        for j in range(pairs)
    ]
    for item in rows:
        item.start()
    first.wait()
    for j in range(pairs):
        cols = slice(j * HD, (j + 1) * HD)
        rows[j].wait()
        ga[:, cols] = dot(cot_in[...], w_half[cols, :], 1, 1).astype(BF16)


def turn_own(me, cot, w):
    tokens, width = cot.shape
    half = w.shape[0] // 2
    return call(
        turn_kernel,
        (shape_of(tokens, half), shape_of(half, width)),
        [SMEM, HBM, HBM],
        "grad_attended_own",
        flops=2 * tokens * width * half,
        moved=4 * half * width,
        scratch=[pltpu.VMEM((tokens, width), BF16), pltpu.SemaphoreType.DMA((half // HD + 1,))],
    )(me, cot, w)


def score_kernel(
    me, listed, live, q_own, cq, own, par, far_own, far_par, ga_own, w_half,
    probs, grads, ga_par, d_far_own, d_far_par,
):
    rate = math.log2(math.e) / math.sqrt(HD)
    scale = 1.0 / math.sqrt(HD)
    tokens, half = q_own.shape
    near_flag, far_flag = listed_flags(me[0], listed, live)
    barred = lambda x: jnp.where(x > 0, 0.0, -jnp.inf)
    theirs = cq[3 * tokens : 3 * tokens + FLAG_ROWS, :].astype(F32)[:1]
    left = lax.broadcasted_iota(jnp.int32, (1, 2 * tokens), 1) < tokens
    near_par = barred(jnp.broadcast_to(theirs[:, :1], (1, 2 * tokens)))
    far_par_bias = barred(jnp.broadcast_to(theirs[:, half - 1 :], (1, 2 * tokens)))
    bias = (
        jnp.where(left, 0.0, near_par),
        jnp.where(left, barred(near_flag), 0.0),
        jnp.where(left, barred(far_flag), far_par_bias),
    )
    for j in range(half // HD):
        cols = slice(j * HD, (j + 1) * HD)
        gp = dot(cq[:tokens, :], w_half[cols, :half], 1, 1)
        gp = (gp + dot(cq[tokens : 2 * tokens, :], w_half[cols, half:], 1, 1)).astype(BF16)
        ga_par[:, cols] = gp
        go = ga_own[:, cols]
        ga = jnp.concatenate([go, gp], axis=0)
        qo, qp = q_own[:, cols], cq[2 * tokens : 3 * tokens, cols]
        q = jnp.concatenate([qo, qp], axis=0)
        k = jnp.concatenate([own[:tokens, cols], par[:tokens, cols]], axis=0)
        v = jnp.concatenate([own[tokens:, cols], par[tokens:, cols]], axis=0)
        kfo, kfp = far_own[:tokens, cols], far_par[:tokens, cols]
        vfo, vfp = far_own[tokens:, cols], far_par[tokens:, cols]
        near = dot(k, q, 1, 1)
        far = jnp.concatenate([dot(kfo, qo, 1, 1), dot(kfp, qp, 1, 1)], axis=1)
        s = [near[:tokens] + bias[0], near[tokens:] + bias[1], far + bias[2]]
        top = jnp.max(jnp.maximum(jnp.maximum(s[0], s[1]), s[2]), axis=0, keepdims=True)
        e = [jnp.exp2((x - top) * rate) for x in s]
        inv = 1.0 / jnp.sum(e[0] + e[1] + e[2], axis=0, keepdims=True)
        p = [x * inv for x in e]
        gn = dot(v, ga, 1, 1)
        g = [
            gn[:tokens],
            gn[tokens:],
            jnp.concatenate([dot(vfo, go, 1, 1), dot(vfp, gp, 1, 1)], axis=1),
        ]
        delta = jnp.sum(p[0] * g[0] + p[1] * g[1] + p[2] * g[2], axis=0, keepdims=True)
        for i in range(3):
            probs[j, i * tokens : (i + 1) * tokens, :] = p[i].astype(BF16)
            grads[j, i * tokens : (i + 1) * tokens, :] = (p[i] * (g[i] - delta)).astype(BF16)
        last = slice(2 * tokens, 3 * tokens)
        first, second = slice(0, tokens), slice(tokens, 2 * tokens)
        d_far_own[first, cols] = (dot(grads[j, last, :tokens], qo, 1, 0) * scale).astype(BF16)
        d_far_par[first, cols] = (dot(grads[j, last, tokens:], qp, 1, 0) * scale).astype(BF16)
        d_far_own[second, cols] = dot(probs[j, last, :tokens], go, 1, 0).astype(BF16)
        d_far_par[second, cols] = dot(probs[j, last, tokens:], gp, 1, 0).astype(BF16)


def scores(me, listed, live, q_own, cq, own, par, far_own, far_par, ga_own, w_half):
    tokens, half = q_own.shape
    pairs = half // HD
    square = shape_of(pairs, 3 * tokens, 2 * tokens)
    kv = shape_of(2 * tokens, half)
    return call(
        score_kernel,
        (square, square, shape_of(tokens, half), kv, kv),
        [SMEM] * 3 + [VMEM] * 8,
        "patch_scores",
        flops=2 * tokens * half * (16 * tokens + 1024),
        moved=40 * tokens * half,
        exps=pairs * tokens * tokens * 6,
    )(me, listed, live, q_own, cq, own, par, far_own, far_par, ga_own, w_half)


def gradient_kernel(
    direct, n_dp, who, q_own, cq, own, par, far_own, far_par, ga_own, ga_par, probs, grads,
    att_own, dq_own, back, att_t, d_own, d_par,
):
    scale = 1.0 / math.sqrt(HD)
    tokens, half = q_own.shape
    pairs = half // HD
    me = who[0]
    near, last = slice(0, 2 * tokens), slice(2 * tokens, 3 * tokens)
    for j in range(pairs):
        cols = slice(j * HD, (j + 1) * HD)
        ga = jnp.concatenate([ga_own[:, cols], ga_par[:, cols]], axis=0)
        q = jnp.concatenate([q_own[:, cols], cq[2 * tokens : 3 * tokens, cols]], axis=0)
        k = jnp.concatenate([own[:tokens, cols], par[:tokens, cols]], axis=0)
        v = jnp.concatenate([own[tokens:, cols], par[tokens:, cols]], axis=0)
        kfo, kfp = far_own[:tokens, cols], far_par[:tokens, cols]
        vfo, vfp = far_own[tokens:, cols], far_par[tokens:, cols]
        low, dsn = probs[j, near, :], grads[j, near, :]
        lfo, lfp = probs[j, last, :tokens], probs[j, last, tokens:]
        dfo, dfp = grads[j, last, :tokens], grads[j, last, tokens:]
        o_t = dot(v, low, 0, 0) + jnp.concatenate([dot(vfo, lfo, 0, 0), dot(vfp, lfp, 0, 0)], axis=1)
        o = o_t.T.astype(BF16)
        att_own[:, cols] = o[:tokens]
        back[:tokens, cols] = o[tokens:]
        o_low = o_t.astype(BF16)
        if direct:
            rows = HD // n_dp
            bits = (pairs - 1).bit_length()
            start = pl.multiple_of(bit_reversed(j ^ (me >> 1), bits) * rows, rows)
            for d in range(n_dp):
                att_t[d, pl.ds(start, rows), :] = o_low[d * rows : (d + 1) * rows, :]
        else:
            att_t[cols, :] = o_low
        dq = dot(dsn, k, 0, 0) + jnp.concatenate([dot(dfo, kfo, 0, 0), dot(dfp, kfp, 0, 0)], axis=0)
        dq = (dq * scale).astype(BF16)
        dq_own[:, cols] = dq[:tokens]
        back[tokens:, cols] = dq[tokens:]
        dk = (dot(dsn, q, 1, 0) * scale).astype(BF16)
        dv = dot(low, ga, 1, 0).astype(BF16)
        d_own[:tokens, cols] = dk[:tokens]
        d_par[:tokens, cols] = dk[tokens:]
        d_own[tokens:, cols] = dv[:tokens]
        d_par[tokens:, cols] = dv[tokens:]


def gradients(me, q_own, cq, own, par, far_own, far_par, ga_own, ga_par, probs, grads, n_seq, n_dp):
    tokens, half = q_own.shape
    features = 2 * half
    heads = features // HD
    direct = n_seq == heads and HD % n_dp == 0 and (HD // n_dp) % 16 == 0
    one, kv = shape_of(tokens, half), shape_of(2 * tokens, half)
    turned = shape_of(n_dp, half // n_dp, 2 * tokens) if direct else shape_of(half, 2 * tokens)
    result = call(
        functools.partial(gradient_kernel, direct, n_dp),
        (one, one, kv, turned, kv, kv),
        [SMEM] + [VMEM] * 10,
        "patch_gradients",
        flops=2 * tokens * half * 20 * tokens,
        moved=40 * tokens * half,
    )(me, q_own, cq, own, par, far_own, far_par, ga_own, ga_par, probs, grads)
    turned = result[3]
    if not direct:
        here = me[0]
        bits = (n_seq - 1).bit_length()
        order = jnp.array([bit_reversed(i, bits) for i in range(n_seq)], jnp.int32) ^ here
        full = jnp.zeros((heads // 2, 2, HD, 2 * tokens), BF16)
        full = lax.dynamic_update_slice(
            full, turned.reshape(heads // 2, 1, HD, 2 * tokens), (0, here & 1, 0, 0)
        )
        full = full.reshape(n_seq, n_dp, features // (n_seq * n_dp), 2 * tokens)
        full = jnp.take(full, order, axis=0).transpose(1, 0, 2, 3)
        turned = full.reshape(n_dp, features // n_dp, 2 * tokens)
    return result[:3] + (turned, 2 if direct else 1) + result[4:]


def weight_kernel(n, *refs):
    att_refs, own_refs, par_refs = refs[:n], refs[n : 2 * n], refs[2 * n : 3 * n]
    keep, send = refs[3 * n :]
    size = keep.shape[0]
    tokens = own_refs[0].shape[0]
    half = par_refs[0].shape[1]
    for target, start in ((send, size), (keep, 0)):
        rows = slice(start, start + size)
        for side in range(2):
            cols = slice(side * half, (side + 1) * half)
            total = jnp.zeros((size, half), F32)
            for i in range(n):
                total += dot(att_refs[i][rows, :tokens], own_refs[i][:, cols], 1, 0)
                theirs = par_refs[i][side * tokens : (side + 1) * tokens, :]
                total += dot(att_refs[i][rows, tokens:], theirs, 1, 0)
            target[:, cols] = total.astype(target.dtype)


def weight_terms(att_parts, own_parts, par_parts):
    n = len(att_parts)
    rows = att_parts[0].shape[0]
    tokens, width = own_parts[0].shape
    return call(
        functools.partial(weight_kernel, n),
        (shape_of(rows // 2, width, dtype=F32), shape_of(rows // 2, width)),
        [VMEM] * (3 * n),
        "weight_terms",
        flops=4 * rows * n * tokens * width,
        moved=n * (rows + width) * tokens * 4 + rows * width * 3,
    )(*att_parts, *own_parts, *par_parts)


def query_kernel(me, att_own, dq_own, back, w, out, dq, att):
    mine = me[0] & 1
    for j in range(att_own.shape[1] // HD):
        cols = slice(j * HD, (j + 1) * HD)
        att[:, head_cols(j, mine)] = att_own[:, cols]
        att[:, head_cols(j, 1 - mine)] = back[: att_own.shape[0], cols]
        dq[:, head_cols(j, mine)] = dq_own[:, cols]
        dq[:, head_cols(j, 1 - mine)] = back[att_own.shape[0] :, cols]
    out[...] = dot(att[...], w[...], 1, 0).astype(BF16)


def finish_queries(me, att_own, dq_own, back, w):
    tokens = att_own.shape[0]
    return call(
        query_kernel,
        (shape_of(tokens, w.shape[1]), shape_of(tokens, w.shape[0])),
        [SMEM] + [VMEM] * 4,
        "finish_queries",
        flops=2 * tokens * w.size,
        moved=2 * w.size + 8 * tokens * w.shape[0],
        scratch=[pltpu.VMEM((tokens, w.shape[0]), BF16)],
    )(me, att_own, dq_own, back, w)


def key_kernel(me, own, far, home, dk, dv):
    mine = me[0] & 1
    tokens = dk.shape[0]
    for i, target in ((0, dk), (1, dv)):
        rows = slice(i * tokens, (i + 1) * tokens)
        for j in range(own.shape[1] // HD):
            cols = slice(j * HD, (j + 1) * HD)
            total = own[rows, cols].astype(F32) + far[rows, cols].astype(F32)
            target[:, head_cols(j, mine)] = total.astype(BF16)
            target[:, head_cols(j, 1 - mine)] = home[rows, cols]


def finish_keys(me, own, far, home):
    tokens, half = own.shape[0] // 2, own.shape[1]
    return call(
        key_kernel,
        (shape_of(tokens, 2 * half), shape_of(tokens, 2 * half)),
        [SMEM] + [VMEM] * 3,
        "finish_keys",
        moved=10 * tokens * 2 * half,
    )(me, own, far, home)


def on_device(queries, key_states, values, w_out, cotangent, neighbours, counts):
    n_seq, n_dp = lax.axis_size("seq"), lax.axis_size("dp")
    me, my_dp = lax.axis_index("seq").astype(jnp.int32), lax.axis_index("dp")
    who = me.reshape(1)
    cot = cotangent[0]
    tokens = cot.shape[0]

    swap = [(i, i ^ 1) for i in range(n_seq)]
    relay = [(i, i + 2) for i in range(0, n_seq, 2) if i + 2 < n_seq]
    relay += [(i, i - 2) for i in range(1, n_seq, 2) if i - 2 >= 0]
    outer = [(b, a) for a, b in relay]
    send = lambda x, pairs: lax.ppermute(x, "seq", pairs)
    across = lambda x, k: lax.ppermute(x, "dp", [(i, i ^ k) for i in range(n_dp)])

    kv_send, own, cq_send, q_own = pack(
        who, neighbours[0], counts, queries[0], key_states[0], values[0], cot
    )
    par = send(kv_send, swap)
    cq = send(cq_send, swap)
    far_par = send(own, outer)
    far_own = send(par, relay)
    ga_own, w_half = turn_own(who, cot, w_out)

    def gathered(x):
        held = {0: x}
        bit = n_dp // 2
        while bit:
            for k in list(held):
                held[k | bit] = across(held[k], bit)
            bit //= 2
        return [held[k] for k in range(n_dp)]

    cots, cots_par = gathered(cot), gathered(cq[: 2 * tokens])

    inputs = (q_own, cq, own, par, far_own, far_par, ga_own)
    probs, grads, ga_par, d_far_own, d_far_par = scores(
        who, neighbours[0], counts, *inputs, w_half
    )
    returned = send(d_far_own, outer)
    att_own, dq_own, back, att_t, step, d_own, d_par = gradients(
        who, *inputs, ga_par, probs, grads, n_seq, n_dp
    )

    pieces = [lax.dynamic_index_in_dim(att_t, my_dp ^ k, 0, keepdims=False) for k in range(n_dp)]
    parts = [pieces[0]] + [across(pieces[k], k) for k in range(1, n_dp)]
    back = send(back, swap)
    d_far = send(d_far_par, relay)
    home = send((d_par.astype(F32) + returned.astype(F32)).astype(BF16), swap)

    keep, out = weight_terms(parts, cots, cots_par)
    while True:
        total = keep + send(out, [(i, i ^ step) for i in range(n_seq)]).astype(F32)
        step *= 2
        if step == n_seq:
            break
        rows = total.shape[0] // 2
        keep, out = total[:rows], total[rows:].astype(BF16)

    output, dq = finish_queries(who, att_own, dq_own, back, w_out)
    dk, dv = finish_keys(who, d_own, d_far, home)
    return (output[None], dq[None], dk[None], dv[None], total)


def solution(mesh):
    placed = (
        P("dp", "seq", None),
        P("dp", "seq", None),
        P("dp", "seq", None),
        P(),
        P("dp", "seq", None),
        P("dp", "seq", None),
        P("dp", "seq"),
    )
    return jax.shard_map(
        on_device,
        mesh=mesh,
        in_specs=placed,
        out_specs=(
            P("dp", "seq", None),
            P("dp", "seq", None),
            P("dp", "seq", None),
            P("dp", "seq", None),
            P(("seq", "dp"), None),
        ),
        check_vma=False,
    )
```

```python
import functools
import math

import jax
import jax.numpy as jnp
from jax import lax
from jax.experimental import pallas as pl
from jax.experimental.pallas import tpu as pltpu
from jax.sharding import PartitionSpec as P

HD = 128
VMEM_LIMIT = 32 * 1024 * 1024
F32 = jnp.float32
BF16 = jnp.bfloat16
VMEM = pl.BlockSpec(memory_space=pltpu.VMEM)
SMEM = pl.BlockSpec(memory_space=pltpu.SMEM)
HBM = pl.BlockSpec(memory_space=pltpu.HBM)
FLAG_ROWS = 16


def dot(a, b, ca, cb):
    return lax.dot_general(a, b, (((ca,), (cb,)), ((), ())), preferred_element_type=F32)


def bit_reversed(index, bits):
    out = 0
    for b in range(bits):
        out = out * 2 + ((index >> b) & 1)
    return out


def shape_of(*dims, dtype=BF16):
    return jax.ShapeDtypeStruct(dims, dtype)


def call(body, out_shape, in_specs, name, flops=0, moved=0, exps=0, scratch=()):
    return pl.pallas_call(
        body,
        out_shape=out_shape,
        in_specs=in_specs,
        out_specs=(VMEM,) * len(out_shape),
        scratch_shapes=list(scratch),
        compiler_params=pltpu.CompilerParams(vmem_limit_bytes=VMEM_LIMIT),
        cost_estimate=pl.CostEstimate(flops=flops, bytes_accessed=moved, transcendentals=exps),
        name=name,
    )


def head_cols(pair, parity):
    return pl.ds(pl.multiple_of((2 * pair + parity) * HD, HD), HD)


def listed_flags(me, listed, live):
    far_patch = jnp.where(me % 2 == 0, me - 1, me + 1)
    near, far = jnp.int32(0), jnp.int32(0)
    for slot in range(listed.shape[1]):
        used = slot < live[0, 0]
        near = jnp.where(used & (listed[0, slot] == (me ^ 1)), 1, near)
        far = jnp.where(used & (listed[0, slot] == far_patch), 1, far)
    return near, far


def pack_kv_kernel(who, k, v, kv_send, kv_keep, sems):
    mine = who[0] & 1
    tokens, half = kv_send.shape[0] // 2, kv_send.shape[1]
    copies = []
    for target, parity in ((kv_send, 1 - mine), (kv_keep, mine)):
        for source, row in ((k, 0), (v, tokens)):
            for j in range(half // HD):
                item = pltpu.make_async_copy(
                    source.at[:, head_cols(j, parity)],
                    target.at[row : row + tokens, j * HD : (j + 1) * HD],
                    sems.at[len(copies)],
                )
                item.start()
                copies.append(item)
    for item in copies:
        item.wait()


def in_hbm(x):
    return pltpu.with_memory_space_constraint(x, pltpu.HBM)


def pack_kv(who, k, v):
    tokens, features = k.shape
    kv = shape_of(2 * tokens, features // 2)
    return call(
        pack_kv_kernel,
        (kv, kv),
        [SMEM, HBM, HBM],
        "pack_keys_values",
        moved=8 * tokens * features,
        scratch=[pltpu.SemaphoreType.DMA((2 * features // HD,))],
    )(who, in_hbm(k), in_hbm(v))


def pack_q_kernel(who, listed, live, q, q_send, q_keep):
    mine = who[0] & 1
    tokens, half = q_keep.shape
    for j in range(half // HD):
        cols = slice(j * HD, (j + 1) * HD)
        q_keep[:, cols] = q[:, head_cols(j, mine)]
        q_send[:tokens, cols] = q[:, head_cols(j, 1 - mine)]
    near, far = listed_flags(who[0], listed, live)
    left = lax.broadcasted_iota(jnp.int32, (FLAG_ROWS, half), 1) < half // 2
    q_send[tokens : tokens + FLAG_ROWS, :] = jnp.where(left, near, far).astype(F32).astype(BF16)


def pack_q(who, listed, live, q):
    tokens, features = q.shape
    return call(
        pack_q_kernel,
        (shape_of(tokens + FLAG_ROWS, features // 2), shape_of(tokens, features // 2)),
        [SMEM] * 3 + [VMEM],
        "pack_queries",
        moved=4 * tokens * features,
    )(who, listed, live, q)


def far_slot(me):
    return 1 - ((me & 1) ^ ((me >> 1) & 1))


def score_kernel(
    who, listed, live, q_own, q_par, own, par, far_own, far_par, ga_full, cot_par, w,
    probs, grads, ga, edge_a, edge_b,
):
    rate = math.log2(math.e) / math.sqrt(HD)
    scale = 1.0 / math.sqrt(HD)
    tokens, half = q_own.shape
    near_flag, far_flag = listed_flags(who[0], listed, live)
    barred = lambda x: jnp.where(x > 0, 0.0, -jnp.inf)
    theirs = q_par[tokens : tokens + FLAG_ROWS, :].astype(F32)[:1]
    left = lax.broadcasted_iota(jnp.int32, (1, 2 * tokens), 1) < tokens
    near_par = barred(jnp.broadcast_to(theirs[:, :1], (1, 2 * tokens)))
    far_par_bias = barred(jnp.broadcast_to(theirs[:, half - 1 :], (1, 2 * tokens)))
    bias = (
        jnp.where(left, 0.0, near_par),
        jnp.where(left, barred(near_flag), 0.0),
        jnp.where(left, barred(far_flag), far_par_bias),
    )
    slot = far_slot(who[0])
    for j in range(half // HD):
        cols = slice(j * HD, (j + 1) * HD)
        mine = head_cols(j, who[0] & 1)
        go = ga_full[:, mine]
        gp = dot(cot_par[...], w[mine, :], 1, 1).astype(BF16)
        g_both = jnp.concatenate([go, gp], axis=0)
        ga[:, cols] = g_both
        qo, qp = q_own[:, cols], q_par[:tokens, cols]
        q = jnp.concatenate([qo, qp], axis=0)
        k = jnp.concatenate([own[:tokens, cols], par[:tokens, cols]], axis=0)
        v = jnp.concatenate([own[tokens:, cols], par[tokens:, cols]], axis=0)
        kfo, kfp = far_own[:tokens, cols], far_par[:tokens, cols]
        vfo, vfp = far_own[tokens:, cols], far_par[tokens:, cols]
        near = dot(k, q, 1, 1)
        far = jnp.concatenate([dot(kfo, qo, 1, 1), dot(kfp, qp, 1, 1)], axis=1)
        s = [near[:tokens] + bias[0], near[tokens:] + bias[1], far + bias[2]]
        top = jnp.max(jnp.maximum(jnp.maximum(s[0], s[1]), s[2]), axis=0, keepdims=True)
        e = [jnp.exp2((x - top) * rate) for x in s]
        inv = 1.0 / jnp.sum(e[0] + e[1] + e[2], axis=0, keepdims=True)
        p = [x * inv for x in e]
        gn = dot(v, g_both, 1, 1)
        g = [
            gn[:tokens],
            gn[tokens:],
            jnp.concatenate([dot(vfo, go, 1, 1), dot(vfp, gp, 1, 1)], axis=1),
        ]
        delta = jnp.sum(p[0] * g[0] + p[1] * g[1] + p[2] * g[2], axis=0, keepdims=True)
        for i in range(3):
            probs[j, i * tokens : (i + 1) * tokens, :] = p[i].astype(BF16)
            grads[j, i * tokens : (i + 1) * tokens, :] = (p[i] * (g[i] - delta)).astype(BF16)
        last = slice(2 * tokens, 3 * tokens)
        own_far = jnp.concatenate(
            [dot(grads[j, last, :tokens], qo, 1, 0) * scale, dot(probs[j, last, :tokens], go, 1, 0)], axis=0
        ).astype(BF16)
        par_far = jnp.concatenate(
            [dot(grads[j, last, tokens:], qp, 1, 0) * scale, dot(probs[j, last, tokens:], gp, 1, 0)], axis=0
        ).astype(BF16)
        edge_a[:, cols] = jnp.where(slot == 0, own_far, par_far)
        edge_b[:, cols] = jnp.where(slot == 0, par_far, own_far)


def scores(who, listed, live, q_own, q_par, own, par, far_own, far_par, ga_full, cot_par, w):
    tokens, half = q_own.shape
    pairs = half // HD
    square = shape_of(pairs, 3 * tokens, 2 * tokens)
    return call(
        score_kernel,
        (square, square) + (shape_of(2 * tokens, half),) * 3,
        [SMEM] * 3 + [VMEM] * 9,
        "patch_scores",
        flops=2 * tokens * half * (16 * tokens + 1024),
        moved=40 * tokens * half,
        exps=pairs * tokens * tokens * 6,
    )(who, listed, live, q_own, q_par, own, par, far_own, far_par, ga_full, cot_par, w)


def gradient_kernel(
    direct, n_dp, who, q_own, q_par, own, par, far_own, far_par, ga, probs, grads,
    att_own, dq_own, back, att_t, d_own, d_par,
):
    scale = 1.0 / math.sqrt(HD)
    tokens, half = q_own.shape
    pairs = half // HD
    me = who[0]
    near, last = slice(0, 2 * tokens), slice(2 * tokens, 3 * tokens)
    for j in range(pairs):
        cols = slice(j * HD, (j + 1) * HD)
        q = jnp.concatenate([q_own[:, cols], q_par[:tokens, cols]], axis=0)
        k = jnp.concatenate([own[:tokens, cols], par[:tokens, cols]], axis=0)
        v = jnp.concatenate([own[tokens:, cols], par[tokens:, cols]], axis=0)
        kfo, kfp = far_own[:tokens, cols], far_par[:tokens, cols]
        vfo, vfp = far_own[tokens:, cols], far_par[tokens:, cols]
        low, dsn = probs[j, near, :], grads[j, near, :]
        lfo, lfp = probs[j, last, :tokens], probs[j, last, tokens:]
        dfo, dfp = grads[j, last, :tokens], grads[j, last, tokens:]
        o_t = dot(v, low, 0, 0) + jnp.concatenate([dot(vfo, lfo, 0, 0), dot(vfp, lfp, 0, 0)], axis=1)
        o = o_t.T.astype(BF16)
        att_own[:, cols] = o[:tokens]
        back[:tokens, cols] = o[tokens:]
        o_low = o_t.astype(BF16)
        if direct:
            rows = HD // n_dp
            bits = (pairs - 1).bit_length()
            place = bit_reversed(j ^ (me >> 1), bits)
            for d in range(n_dp):
                block = bit_reversed((d ^ who[1]) >> 1, (n_dp // 2 - 1).bit_length())
                start = pl.multiple_of((block * pairs + place) * rows, rows)
                att_t[(d ^ who[1]) & 1, pl.ds(start, rows), :] = o_low[d * rows : (d + 1) * rows, :]
        else:
            att_t[cols, :] = o_low
        dq = dot(dsn, k, 0, 0) + jnp.concatenate([dot(dfo, kfo, 0, 0), dot(dfp, kfp, 0, 0)], axis=0)
        dq = (dq * scale).astype(BF16)
        dq_own[:, cols] = dq[:tokens]
        back[tokens:, cols] = dq[tokens:]
        dk = (dot(dsn, q, 1, 0) * scale).astype(BF16)
        dv = dot(low, ga[:, cols], 1, 0).astype(BF16)
        d_own[:tokens, cols] = dk[:tokens]
        d_par[:tokens, cols] = dk[tokens:]
        d_own[tokens:, cols] = dv[:tokens]
        d_par[tokens:, cols] = dv[tokens:]


def gradients(who, q_own, q_par, own, par, far_own, far_par, ga, probs, grads, n_seq, n_dp):
    tokens, half = q_own.shape
    features = 2 * half
    heads = features // HD
    direct = n_seq == heads and HD % n_dp == 0 and (HD // n_dp) % 16 == 0
    one, kv = shape_of(tokens, half), shape_of(2 * tokens, half)
    turned = shape_of(2, half // 2, 2 * tokens) if direct else shape_of(half, 2 * tokens)
    result = call(
        functools.partial(gradient_kernel, direct, n_dp),
        (one, one, kv, turned, kv, kv),
        [SMEM] + [VMEM] * 9,
        "patch_gradients",
        flops=2 * tokens * half * 20 * tokens,
        moved=40 * tokens * half,
    )(who, q_own, q_par, own, par, far_own, far_par, ga, probs, grads)
    turned = result[3]
    if not direct:
        here = who[0]
        bits, d_bits = (n_seq - 1).bit_length(), (n_dp // 2 - 1).bit_length()
        order = jnp.array([bit_reversed(i, bits) for i in range(n_seq)], jnp.int32) ^ here
        d_order = [bit_reversed(i, d_bits) * 2 + c for c in range(2) for i in range(n_dp // 2)]
        full = jnp.zeros((heads // 2, 2, HD, 2 * tokens), BF16)
        full = lax.dynamic_update_slice(
            full, turned.reshape(heads // 2, 1, HD, 2 * tokens), (0, here & 1, 0, 0)
        )
        full = full.reshape(n_seq, n_dp, features // (n_seq * n_dp), 2 * tokens)
        full = jnp.take(full, order, axis=0)
        full = jnp.take(full, jnp.array(d_order, jnp.int32) ^ who[1], axis=1).transpose(1, 0, 2, 3)
        turned = full.reshape(2, features // 2, 2 * tokens)
    return result[:3] + (turned, 2 if direct else 1) + result[4:]


def weight_kernel(att_keep, att_core, own, par, core_own, core_par, keep, send):
    size = keep.shape[0]
    tokens = own.shape[0]
    for target, start in ((send, size), (keep, 0)):
        rows = slice(start, start + size)
        total = dot(att_keep[rows, :tokens], own[...], 1, 0)
        total += dot(att_keep[rows, tokens:], par[...], 1, 0)
        total += dot(att_core[rows, :tokens], core_own[...], 1, 0)
        total += dot(att_core[rows, tokens:], core_par[...], 1, 0)
        target[...] = total.astype(target.dtype)


def weight_terms(*operands):
    rows = operands[0].shape[0]
    tokens, width = operands[2].shape
    return call(
        weight_kernel,
        (shape_of(rows // 2, width, dtype=F32), shape_of(rows // 2, width)),
        [VMEM] * 6,
        "weight_terms",
        flops=8 * rows * tokens * width,
        moved=8 * (rows + width) * tokens + rows * width * 3,
    )(*operands)


def query_kernel(me, att_own, dq_own, back, w, out, dq, att):
    mine = me[0] & 1
    for j in range(att_own.shape[1] // HD):
        cols = slice(j * HD, (j + 1) * HD)
        att[:, head_cols(j, mine)] = att_own[:, cols]
        att[:, head_cols(j, 1 - mine)] = back[: att_own.shape[0], cols]
        dq[:, head_cols(j, mine)] = dq_own[:, cols]
        dq[:, head_cols(j, 1 - mine)] = back[att_own.shape[0] :, cols]
    out[...] = dot(att[...], w[...], 1, 0).astype(BF16)


def finish_queries(me, att_own, dq_own, back, w):
    tokens = att_own.shape[0]
    return call(
        query_kernel,
        (shape_of(tokens, w.shape[1]), shape_of(tokens, w.shape[0])),
        [SMEM] + [VMEM] * 4,
        "finish_queries",
        flops=2 * tokens * w.size,
        moved=2 * w.size + 8 * tokens * w.shape[0],
        scratch=[pltpu.VMEM((tokens, w.shape[0]), BF16)],
    )(me, att_own, dq_own, back, w)


def key_kernel(me, own, far, home, dk, dv):
    mine = me[0] & 1
    tokens = dk.shape[0]
    for i, target in ((0, dk), (1, dv)):
        rows = slice(i * tokens, (i + 1) * tokens)
        for j in range(own.shape[1] // HD):
            cols = slice(j * HD, (j + 1) * HD)
            total = own[rows, cols].astype(F32) + far[rows, cols].astype(F32)
            target[:, head_cols(j, mine)] = total.astype(BF16)
            target[:, head_cols(j, 1 - mine)] = home[rows, cols]


def finish_keys(me, own, far, home):
    tokens, half = own.shape[0] // 2, own.shape[1]
    return call(
        key_kernel,
        (shape_of(tokens, 2 * half), shape_of(tokens, 2 * half)),
        [SMEM] + [VMEM] * 3,
        "finish_keys",
        moved=10 * tokens * 2 * half,
    )(me, own, far, home)


def on_device(queries, key_states, values, w_out, cotangent, neighbours, counts):
    n_seq, n_dp = lax.axis_size("seq"), lax.axis_size("dp")
    me, my_dp = lax.axis_index("seq").astype(jnp.int32), lax.axis_index("dp").astype(jnp.int32)
    who = jnp.stack([me, my_dp])
    cot = cotangent[0]

    swap = [(i, i ^ 1) for i in range(n_seq)]
    relay = [(i, i + 2) for i in range(0, n_seq, 2) if i + 2 < n_seq]
    relay += [(i, i - 2) for i in range(1, n_seq, 2) if i - 2 >= 0]
    outer = [(b, a) for a, b in relay]
    edges = [[], []]
    for i in range(n_seq):
        edges[0].append((i, i ^ 2))
        other = i + 2 if (i >> 1) & 1 else i - 2
        if 0 <= other < n_seq:
            edges[1].append((i, other))
    send = lambda x, pairs: lax.ppermute(x, "seq", pairs)
    across = lambda x, k: lax.ppermute(x, "dp", [(i, i ^ k) for i in range(n_dp)])

    kv_send, own = pack_kv(who, key_states[0], values[0])
    q_send, q_own = pack_q(who, neighbours[0], counts, queries[0])
    par = send(kv_send, swap)
    far_par = send(own, outer)
    core_own = across(cot, 1)
    ga_full = dot(cot, w_out, 1, 1).astype(BF16)
    par, q_send, late_cot = lax.optimization_barrier((par, q_send, cot))
    q_par = send(q_send, swap)
    cot_par = send(late_cot, swap)
    far_own = send(par, relay)
    core_par = across(cot_par, 1)

    inputs = (q_own, q_par, own, par, far_own, far_par)
    probs, grads, ga, *leaving = scores(
        who, neighbours[0], counts, *inputs, ga_full, cot_par, w_out
    )
    far = [send(leaving[i], edges[i]) for i in range(2)]
    att_own, dq_own, back, att_t, step, d_own, d_par = gradients(
        who, *inputs, ga, probs, grads, n_seq, n_dp
    )

    back = send(back, swap)
    att_core = across(att_t[1], 1)
    slot = far_slot(me)
    keep, out = weight_terms(att_t[0], att_core, cot, cot_par, core_own, core_par)
    out, *far = lax.optimization_barrier((out, *far))
    returned = jnp.where(slot == 0, far[1], far[0])
    d_far_own = jnp.where(slot == 0, far[0], far[1])
    home = send((d_par.astype(F32) + returned.astype(F32)).astype(BF16), swap)

    hops = []
    bit = 2
    while bit < n_dp:
        hops.append(("dp", n_dp, bit))
        bit *= 2
    while step < n_seq:
        hops.append(("seq", n_seq, step))
        step *= 2
    for place, (axis, count, bit) in enumerate(hops):
        total = keep + lax.ppermute(out, axis, [(i, i ^ bit) for i in range(count)]).astype(F32)
        rows = total.shape[0] // 2
        if place + 1 < len(hops):
            keep, out = total[:rows], total[rows:].astype(BF16)

    output, dq = finish_queries(who, att_own, dq_own, back, w_out)
    dk, dv = finish_keys(who, d_own, d_far_own, home)
    return (output[None], dq[None], dk[None], dv[None], total)


def solution(mesh):
    placed = (
        P("dp", "seq", None),
        P("dp", "seq", None),
        P("dp", "seq", None),
        P(),
        P("dp", "seq", None),
        P("dp", "seq", None),
        P("dp", "seq"),
    )
    return jax.shard_map(
        on_device,
        mesh=mesh,
        in_specs=placed,
        out_specs=(
            P("dp", "seq", None),
            P("dp", "seq", None),
            P("dp", "seq", None),
            P("dp", "seq", None),
            P(("seq", "dp"), None),
        ),
        check_vma=False,
    )
```

```python
import functools
import math

import jax
import jax.numpy as jnp
from jax import lax
from jax.experimental import pallas as pl
from jax.experimental.pallas import tpu as pltpu
from jax.sharding import PartitionSpec as P

HD = 128
VMEM_LIMIT = 12 * 1024 * 1024
F32 = jnp.float32
BF16 = jnp.bfloat16
VMEM = pl.BlockSpec(memory_space=pltpu.VMEM)
SMEM = pl.BlockSpec(memory_space=pltpu.SMEM)
HBM = pl.BlockSpec(memory_space=pltpu.HBM)
ANY = pl.BlockSpec(memory_space=pl.ANY)
FLAG_ROWS = 16


def dot(a, b, ca, cb):
    return lax.dot_general(a, b, (((ca,), (cb,)), ((), ())), preferred_element_type=F32)


def bit_reversed(index, bits):
    out = 0
    for b in range(bits):
        out = out * 2 + ((index >> b) & 1)
    return out


def shape_of(*dims, dtype=BF16):
    return jax.ShapeDtypeStruct(dims, dtype)


def call(body, out_shape, in_specs, name, scratch=()):
    return pl.pallas_call(
        body,
        out_shape=out_shape,
        in_specs=in_specs,
        out_specs=(VMEM,) * len(out_shape),
        scratch_shapes=list(scratch),
        compiler_params=pltpu.CompilerParams(vmem_limit_bytes=VMEM_LIMIT),
        cost_estimate=pl.CostEstimate(flops=0, bytes_accessed=0, transcendentals=0),
        name=name,
    )


def head_cols(pair, parity):
    return pl.ds(pl.multiple_of((2 * pair + parity) * HD, HD), HD)


def listed_flags(me, listed, live):
    far_patch = jnp.where(me % 2 == 0, me - 1, me + 1)
    near, far = jnp.int32(0), jnp.int32(0)
    for slot in range(listed.shape[1]):
        used = slot < live[0, 0]
        near = jnp.where(used & (listed[0, slot] == (me ^ 1)), 1, near)
        far = jnp.where(used & (listed[0, slot] == far_patch), 1, far)
    return near, far


def pack_kv_kernel(who, k, v, kv_send, kv_keep, sems):
    mine = who[0] & 1
    tokens, half = kv_send.shape[0] // 2, kv_send.shape[1]
    copies = []
    for target, parity in ((kv_send, 1 - mine), (kv_keep, mine)):
        for source, row in ((k, 0), (v, tokens)):
            for j in range(half // HD):
                item = pltpu.make_async_copy(
                    source.at[:, head_cols(j, parity)],
                    target.at[row : row + tokens, j * HD : (j + 1) * HD],
                    sems.at[len(copies)],
                )
                item.start()
                copies.append(item)
    for item in copies:
        item.wait()


def in_hbm(x):
    return pltpu.with_memory_space_constraint(x, pltpu.HBM)


def pack_kv(who, k, v):
    tokens, features = k.shape
    kv = shape_of(2 * tokens, features // 2)
    return call(
        pack_kv_kernel,
        (kv, kv),
        [SMEM, HBM, HBM],
        "pack_keys_values",
        scratch=[pltpu.SemaphoreType.DMA((2 * features // HD,))],
    )(who, in_hbm(k), in_hbm(v))


def pack_q_kernel(who, listed, live, q, q_send, q_keep):
    mine = who[0] & 1
    tokens, half = q_keep.shape
    for j in range(half // HD):
        cols = slice(j * HD, (j + 1) * HD)
        q_keep[:, cols] = q[:, head_cols(j, mine)]
        q_send[:tokens, cols] = q[:, head_cols(j, 1 - mine)]
    near, far = listed_flags(who[0], listed, live)
    left = lax.broadcasted_iota(jnp.int32, (FLAG_ROWS, half), 1) < half // 2
    q_send[tokens : tokens + FLAG_ROWS, :] = jnp.where(left, near, far).astype(F32).astype(BF16)


def pack_q(who, listed, live, q):
    tokens, features = q.shape
    return call(
        pack_q_kernel,
        (shape_of(tokens + FLAG_ROWS, features // 2), shape_of(tokens, features // 2)),
        [SMEM] * 3 + [VMEM],
        "pack_queries",
    )(who, listed, live, q)


def far_slot(me):
    return 1 - ((me & 1) ^ ((me >> 1) & 1))


def forward_kernel(
    direct, n_dp, who, listed, live, q_own, q_par, own, par, far_own, far_par, after,
    probs, att_own, att_back, att_t,
):
    rate = math.log2(math.e) / math.sqrt(HD)
    tokens, half = q_own.shape
    pairs = half // HD
    me = who[0]
    near_flag, far_flag = listed_flags(me, listed, live)
    barred = lambda x: jnp.where(x > 0, 0.0, -jnp.inf)
    theirs = q_par[tokens : tokens + FLAG_ROWS, :].astype(F32)[:1]
    left = lax.broadcasted_iota(jnp.int32, (1, 2 * tokens), 1) < tokens
    near_par = barred(jnp.broadcast_to(theirs[:, :1], (1, 2 * tokens)))
    far_par_bias = barred(jnp.broadcast_to(theirs[:, half - 1 :], (1, 2 * tokens)))
    bias = (
        jnp.where(left, 0.0, near_par),
        jnp.where(left, barred(near_flag), 0.0),
        jnp.where(left, barred(far_flag), far_par_bias),
    )
    for j in range(pairs):
        cols = slice(j * HD, (j + 1) * HD)
        qo, qp = q_own[:, cols], q_par[:tokens, cols]
        q = jnp.concatenate([qo, qp], axis=0)
        k = jnp.concatenate([own[:tokens, cols], par[:tokens, cols]], axis=0)
        v = jnp.concatenate([own[tokens:, cols], par[tokens:, cols]], axis=0)
        near = dot(k, q, 1, 1)
        far = jnp.concatenate(
            [dot(far_own[:tokens, cols], qo, 1, 1), dot(far_par[:tokens, cols], qp, 1, 1)], axis=1
        )
        s = [near[:tokens] + bias[0], near[tokens:] + bias[1], far + bias[2]]
        top = jnp.max(jnp.maximum(jnp.maximum(s[0], s[1]), s[2]), axis=0, keepdims=True)
        e = [jnp.exp2((x - top) * rate) for x in s]
        inv = 1.0 / jnp.sum(e[0] + e[1] + e[2], axis=0, keepdims=True)
        low = [(x * inv).astype(BF16) for x in e]
        for i in range(3):
            probs[j, i * tokens : (i + 1) * tokens, :] = low[i]
        vfo, vfp = far_own[tokens:, cols], far_par[tokens:, cols]
        o_t = dot(v, jnp.concatenate(low[:2], axis=0), 0, 0)
        o_t += jnp.concatenate(
            [dot(vfo, low[2][:, :tokens], 0, 0), dot(vfp, low[2][:, tokens:], 0, 0)], axis=1
        )
        o = o_t.T.astype(BF16)
        att_own[:, cols] = o[:tokens]
        att_back[:, cols] = o[tokens:]
        o_low = o_t.astype(BF16)
        if direct:
            rows = HD // n_dp
            place = bit_reversed(j ^ (me >> 1), (pairs - 1).bit_length())
            for d in range(n_dp):
                block = bit_reversed((d ^ who[1]) >> 1, (n_dp // 2 - 1).bit_length())
                start = pl.multiple_of((block * pairs + place) * rows, rows)
                att_t[(d ^ who[1]) & 1, pl.ds(start, rows), :] = o_low[d * rows : (d + 1) * rows, :]
        else:
            att_t[cols, :] = o_low


def forward(who, listed, live, inputs, after, n_seq, n_dp):
    tokens, half = inputs[0].shape
    features = 2 * half
    heads, pairs = features // HD, half // HD
    direct = n_seq == heads and HD % n_dp == 0 and (HD // n_dp) % 16 == 0
    one = shape_of(tokens, half)
    turned = shape_of(2, half // 2, 2 * tokens) if direct else shape_of(half, 2 * tokens)
    probs, att_own, att_back, turned = call(
        functools.partial(forward_kernel, direct, n_dp),
        (shape_of(pairs, 3 * tokens, 2 * tokens), one, one, turned),
        [SMEM] * 3 + [VMEM] * 6 + [ANY],
        "patch_forward",
    )(who, listed, live, *inputs, after)
    if not direct:
        here = who[0]
        bits, d_bits = (n_seq - 1).bit_length(), (n_dp // 2 - 1).bit_length()
        order = jnp.array([bit_reversed(i, bits) for i in range(n_seq)], jnp.int32) ^ here
        d_order = [bit_reversed(i, d_bits) * 2 + c for c in range(2) for i in range(n_dp // 2)]
        full = jnp.zeros((heads // 2, 2, HD, 2 * tokens), BF16)
        full = lax.dynamic_update_slice(
            full, turned.reshape(heads // 2, 1, HD, 2 * tokens), (0, here & 1, 0, 0)
        )
        full = full.reshape(n_seq, n_dp, features // (n_seq * n_dp), 2 * tokens)
        full = jnp.take(full, order, axis=0)
        full = jnp.take(full, jnp.array(d_order, jnp.int32) ^ who[1], axis=1).transpose(1, 0, 2, 3)
        turned = full.reshape(2, features // 2, 2 * tokens)
    return probs, att_own, att_back, turned, 2 if direct else 1


def backward_kernel(
    who, q_own, q_par, own, par, far_own, far_par, ga_full, cot_par, w, probs,
    grads, ga, edge_a, edge_b,
):
    scale = 1.0 / math.sqrt(HD)
    tokens, half = q_own.shape
    slot = far_slot(who[0])
    last = slice(2 * tokens, 3 * tokens)
    for j in range(half // HD):
        cols = slice(j * HD, (j + 1) * HD)
        mine = head_cols(j, who[0] & 1)
        go = ga_full[:, mine]
        gp = dot(cot_par[...], w[mine, :], 1, 1).astype(BF16)
        g_both = jnp.concatenate([go, gp], axis=0)
        ga[:, cols] = g_both
        qo, qp = q_own[:, cols], q_par[:tokens, cols]
        v = jnp.concatenate([own[tokens:, cols], par[tokens:, cols]], axis=0)
        vfo, vfp = far_own[tokens:, cols], far_par[tokens:, cols]
        gn = dot(v, g_both, 1, 1)
        g = [
            gn[:tokens],
            gn[tokens:],
            jnp.concatenate([dot(vfo, go, 1, 1), dot(vfp, gp, 1, 1)], axis=1),
        ]
        p = [probs[j, i * tokens : (i + 1) * tokens, :].astype(F32) for i in range(3)]
        delta = jnp.sum(p[0] * g[0] + p[1] * g[1] + p[2] * g[2], axis=0, keepdims=True)
        ds = [(p[i] * (g[i] - delta)).astype(BF16) for i in range(3)]
        for i in range(3):
            grads[j, i * tokens : (i + 1) * tokens, :] = ds[i]
        dfo, dfp = ds[2][:, :tokens], ds[2][:, tokens:]
        own_far = jnp.concatenate(
            [dot(dfo, qo, 1, 0) * scale, dot(probs[j, last, :tokens], go, 1, 0)], axis=0
        ).astype(BF16)
        par_far = jnp.concatenate(
            [dot(dfp, qp, 1, 0) * scale, dot(probs[j, last, tokens:], gp, 1, 0)], axis=0
        ).astype(BF16)
        edge_a[:, cols] = jnp.where(slot == 0, own_far, par_far)
        edge_b[:, cols] = jnp.where(slot == 0, par_far, own_far)


def backward(who, inputs, ga_full, cot_par, w, probs):
    tokens, half = inputs[0].shape
    return call(
        backward_kernel,
        (shape_of(*probs.shape),) + (shape_of(2 * tokens, half),) * 3,
        [SMEM] + [VMEM] * 10,
        "patch_backward",
    )(who, *inputs, ga_full, cot_par, w, probs)


def gradient_kernel(
    q_own, q_par, own, par, far_own, far_par, ga, probs, grads, dq_own, dq_back, d_own, d_par
):
    scale = 1.0 / math.sqrt(HD)
    tokens, half = q_own.shape
    near, last = slice(0, 2 * tokens), slice(2 * tokens, 3 * tokens)
    for j in range(half // HD):
        cols = slice(j * HD, (j + 1) * HD)
        q = jnp.concatenate([q_own[:, cols], q_par[:tokens, cols]], axis=0)
        k = jnp.concatenate([own[:tokens, cols], par[:tokens, cols]], axis=0)
        kfo, kfp = far_own[:tokens, cols], far_par[:tokens, cols]
        low, dsn = probs[j, near, :], grads[j, near, :]
        dfo, dfp = grads[j, last, :tokens], grads[j, last, tokens:]
        dq = dot(dsn, k, 0, 0) + jnp.concatenate([dot(dfo, kfo, 0, 0), dot(dfp, kfp, 0, 0)], axis=0)
        dq = (dq * scale).astype(BF16)
        dq_own[:, cols] = dq[:tokens]
        dq_back[:, cols] = dq[tokens:]
        dk = (dot(dsn, q, 1, 0) * scale).astype(BF16)
        dv = dot(low, ga[:, cols], 1, 0).astype(BF16)
        d_own[:tokens, cols] = dk[:tokens]
        d_par[:tokens, cols] = dk[tokens:]
        d_own[tokens:, cols] = dv[:tokens]
        d_par[tokens:, cols] = dv[tokens:]


def gradients(inputs, ga, probs, grads):
    tokens, half = inputs[0].shape
    one, kv = shape_of(tokens, half), shape_of(2 * tokens, half)
    return call(
        gradient_kernel, (one, one, kv, kv), [VMEM] * 9, "patch_gradients"
    )(*inputs, ga, probs, grads)


def weight_kernel(att_keep, att_core, own, par, core_own, core_par, keep, send):
    size = keep.shape[0]
    tokens = own.shape[0]
    for target, start in ((send, size), (keep, 0)):
        rows = slice(start, start + size)
        total = dot(att_keep[rows, :tokens], own[...], 1, 0)
        total += dot(att_keep[rows, tokens:], par[...], 1, 0)
        total += dot(att_core[rows, :tokens], core_own[...], 1, 0)
        total += dot(att_core[rows, tokens:], core_par[...], 1, 0)
        target[...] = total.astype(target.dtype)


def weight_terms(*operands):
    rows = operands[0].shape[0]
    tokens, width = operands[2].shape
    return call(
        weight_kernel,
        (shape_of(rows // 2, width, dtype=F32), shape_of(rows // 2, width)),
        [VMEM] * 6,
        "weight_terms",
    )(*operands)


def output_kernel(who, att_own, att_back, w, out, att):
    mine = who[0] & 1
    for j in range(att_own.shape[1] // HD):
        cols = slice(j * HD, (j + 1) * HD)
        att[:, head_cols(j, mine)] = att_own[:, cols]
        att[:, head_cols(j, 1 - mine)] = att_back[:, cols]
    out[...] = dot(att[...], w[...], 1, 0).astype(BF16)


def finish_output(who, att_own, att_back, w):
    tokens = att_own.shape[0]
    return call(
        output_kernel,
        (shape_of(tokens, w.shape[1]),),
        [SMEM] + [VMEM] * 3,
        "finish_output",
        scratch=[pltpu.VMEM((tokens, w.shape[0]), BF16)],
    )(who, att_own, att_back, w)[0]


def final_kernel(who, dq_own, dq_back, own, far_a, far_b, home, dq, dk, dv):
    mine = who[0] & 1
    slot = far_slot(who[0])
    tokens = dk.shape[0]
    for j in range(own.shape[1] // HD):
        cols = slice(j * HD, (j + 1) * HD)
        dq[:, head_cols(j, mine)] = dq_own[:, cols]
        dq[:, head_cols(j, 1 - mine)] = dq_back[:, cols]
        for i, target in ((0, dk), (1, dv)):
            rows = slice(i * tokens, (i + 1) * tokens)
            far = jnp.where(slot == 0, far_a[rows, cols].astype(F32), far_b[rows, cols].astype(F32))
            target[:, head_cols(j, mine)] = (own[rows, cols].astype(F32) + far).astype(BF16)
            target[:, head_cols(j, 1 - mine)] = home[rows, cols]


def finish_gradients(who, dq_own, dq_back, own, far, home):
    tokens, half = dq_own.shape
    return call(
        final_kernel,
        (shape_of(tokens, 2 * half),) * 3,
        [SMEM] + [VMEM] * 6,
        "finish_gradients",
    )(who, dq_own, dq_back, own, *far, home)


def on_device(queries, key_states, values, w_out, cotangent, neighbours, counts):
    n_seq, n_dp = lax.axis_size("seq"), lax.axis_size("dp")
    me, my_dp = lax.axis_index("seq").astype(jnp.int32), lax.axis_index("dp").astype(jnp.int32)
    who = jnp.stack([me, my_dp])
    cot = cotangent[0]

    swap = [(i, i ^ 1) for i in range(n_seq)]
    relay = [(i, i + 2) for i in range(0, n_seq, 2) if i + 2 < n_seq]
    relay += [(i, i - 2) for i in range(1, n_seq, 2) if i - 2 >= 0]
    outer = [(b, a) for a, b in relay]
    edges = [[], []]
    for i in range(n_seq):
        edges[0].append((i, i ^ 2))
        other = i + 2 if (i >> 1) & 1 else i - 2
        if 0 <= other < n_seq:
            edges[1].append((i, other))
    send = lambda x, pairs: lax.ppermute(x, "seq", pairs)
    across = lambda x, k: lax.ppermute(x, "dp", [(i, i ^ k) for i in range(n_dp)])

    kv_send, own = pack_kv(who, key_states[0], values[0])
    q_send, q_own = pack_q(who, neighbours[0], counts, queries[0])
    par = send(kv_send, swap)
    far_par = send(own, outer)
    core_own = across(cot, 1)
    ga_full = dot(cot, w_out, 1, 1).astype(BF16)
    cot_par = send(cot, swap)
    q_par = send(q_send, swap)
    far_own = send(par, relay)
    core_par = across(cot_par, 1)

    inputs = (q_own, q_par, own, par, far_own, far_par)
    probs, att_own, att_back, att_t, step = forward(
        who, neighbours[0], counts, inputs, ga_full, n_seq, n_dp
    )
    att_core = across(att_t[1], 1)
    att_back = send(att_back, swap)
    grads, ga, *leaving = backward(who, inputs, ga_full, cot_par, w_out, probs)
    far = [send(leaving[i], edges[i]) for i in range(2)]
    keep, out = weight_terms(att_t[0], att_core, cot, cot_par, core_own, core_par)
    dq_own, dq_back, d_own, d_par = gradients(inputs, ga, probs, grads)
    dq_back = send(dq_back, swap)
    returned = jnp.where(far_slot(me) == 0, far[1], far[0])
    home = send((d_par.astype(F32) + returned.astype(F32)).astype(BF16), swap)

    hops = []
    bit = 2
    while bit < n_dp:
        hops.append(("dp", n_dp, bit))
        bit *= 2
    while step < n_seq:
        hops.append(("seq", n_seq, step))
        step *= 2
    for place, (axis, count, bit) in enumerate(hops):
        total = keep + lax.ppermute(out, axis, [(i, i ^ bit) for i in range(count)]).astype(F32)
        rows = total.shape[0] // 2
        if place + 1 < len(hops):
            keep, out = total[:rows], total[rows:].astype(BF16)

    output = finish_output(who, att_own, att_back, w_out)
    dq, dk, dv = finish_gradients(who, dq_own, dq_back, d_own, far, home)
    return (output[None], dq[None], dk[None], dv[None], total)


def solution(mesh):
    placed = (
        P("dp", "seq", None),
        P("dp", "seq", None),
        P("dp", "seq", None),
        P(),
        P("dp", "seq", None),
        P("dp", "seq", None),
        P("dp", "seq"),
    )
    return jax.shard_map(
        on_device,
        mesh=mesh,
        in_specs=placed,
        out_specs=(
            P("dp", "seq", None),
            P("dp", "seq", None),
            P("dp", "seq", None),
            P("dp", "seq", None),
            P(("seq", "dp"), None),
        ),
        check_vma=False,
    )
```

```python
import functools
import math

import jax
import jax.numpy as jnp
from jax import lax
from jax.experimental import pallas as pl
from jax.experimental.pallas import tpu as pltpu
from jax.sharding import PartitionSpec as P

HD = 128
VMEM_LIMIT = 12 * 1024 * 1024
F32 = jnp.float32
BF16 = jnp.bfloat16
VMEM = pl.BlockSpec(memory_space=pltpu.VMEM)
SMEM = pl.BlockSpec(memory_space=pltpu.SMEM)
HBM = pl.BlockSpec(memory_space=pltpu.HBM)
ANY = pl.BlockSpec(memory_space=pl.ANY)
FLAG_ROWS = 16


def dot(a, b, ca, cb):
    return lax.dot_general(a, b, (((ca,), (cb,)), ((), ())), preferred_element_type=F32)


def bit_reversed(index, bits):
    out = 0
    for b in range(bits):
        out = out * 2 + ((index >> b) & 1)
    return out


def shape_of(*dims, dtype=BF16):
    return jax.ShapeDtypeStruct(dims, dtype)


def call(body, out_shape, in_specs, name, scratch=()):
    return pl.pallas_call(
        body,
        out_shape=out_shape,
        in_specs=in_specs,
        out_specs=(VMEM,) * len(out_shape),
        scratch_shapes=list(scratch),
        compiler_params=pltpu.CompilerParams(vmem_limit_bytes=VMEM_LIMIT),
        cost_estimate=pl.CostEstimate(flops=0, bytes_accessed=0, transcendentals=0),
        name=name,
    )


def head_cols(pair, parity):
    return pl.ds(pl.multiple_of((2 * pair + parity) * HD, HD), HD)


def listed_flags(me, listed, live):
    far_patch = jnp.where(me % 2 == 0, me - 1, me + 1)
    near, far = jnp.int32(0), jnp.int32(0)
    for slot in range(listed.shape[1]):
        used = slot < live[0, 0]
        near = jnp.where(used & (listed[0, slot] == (me ^ 1)), 1, near)
        far = jnp.where(used & (listed[0, slot] == far_patch), 1, far)
    return near, far


def pack_kv_kernel(who, k, v, kv_send, kv_keep, sems):
    mine = who[0] & 1
    tokens, half = kv_send.shape[0] // 2, kv_send.shape[1]
    copies = []
    for target, parity in ((kv_send, 1 - mine), (kv_keep, mine)):
        for source, row in ((k, 0), (v, tokens)):
            for j in range(half // HD):
                item = pltpu.make_async_copy(
                    source.at[:, head_cols(j, parity)],
                    target.at[row : row + tokens, j * HD : (j + 1) * HD],
                    sems.at[len(copies)],
                )
                item.start()
                copies.append(item)
    for item in copies:
        item.wait()


def in_hbm(x):
    return pltpu.with_memory_space_constraint(x, pltpu.HBM)


def pack_kv(who, k, v):
    tokens, features = k.shape
    kv = shape_of(2 * tokens, features // 2)
    return call(
        pack_kv_kernel,
        (kv, kv),
        [SMEM, HBM, HBM],
        "pack_keys_values",
        scratch=[pltpu.SemaphoreType.DMA((2 * features // HD,))],
    )(who, in_hbm(k), in_hbm(v))


def pack_q_kernel(who, listed, live, q, q_send, q_keep):
    mine = who[0] & 1
    tokens, half = q_keep.shape
    for j in range(half // HD):
        cols = slice(j * HD, (j + 1) * HD)
        q_keep[:, cols] = q[:, head_cols(j, mine)]
        q_send[:tokens, cols] = q[:, head_cols(j, 1 - mine)]
    near, far = listed_flags(who[0], listed, live)
    left = lax.broadcasted_iota(jnp.int32, (FLAG_ROWS, half), 1) < half // 2
    q_send[tokens : tokens + FLAG_ROWS, :] = jnp.where(left, near, far).astype(F32).astype(BF16)


def pack_q(who, listed, live, q):
    tokens, features = q.shape
    return call(
        pack_q_kernel,
        (shape_of(tokens + FLAG_ROWS, features // 2), shape_of(tokens, features // 2)),
        [SMEM] * 3 + [VMEM],
        "pack_queries",
    )(who, listed, live, q)


def far_slot(me):
    return 1 - ((me & 1) ^ ((me >> 1) & 1))


def forward_kernel(
    direct, n_dp, who, listed, live, q_own, q_par, own, par, far_own, far_par, after,
    probs, att_own, att_back, att_t,
):
    rate = math.log2(math.e) / math.sqrt(HD)
    tokens, half = q_own.shape
    pairs = half // HD
    me = who[0]
    near_flag, far_flag = listed_flags(me, listed, live)
    barred = lambda x: jnp.where(x > 0, 0.0, -jnp.inf)
    theirs = q_par[tokens : tokens + FLAG_ROWS, :].astype(F32)[:1]
    left = lax.broadcasted_iota(jnp.int32, (1, 2 * tokens), 1) < tokens
    near_par = barred(jnp.broadcast_to(theirs[:, :1], (1, 2 * tokens)))
    far_par_bias = barred(jnp.broadcast_to(theirs[:, half - 1 :], (1, 2 * tokens)))
    bias = (
        jnp.where(left, 0.0, near_par),
        jnp.where(left, barred(near_flag), 0.0),
        jnp.where(left, barred(far_flag), far_par_bias),
    )
    for j in range(pairs):
        cols = slice(j * HD, (j + 1) * HD)
        qo, qp = q_own[:, cols], q_par[:tokens, cols]
        q = jnp.concatenate([qo, qp], axis=0)
        k = jnp.concatenate([own[:tokens, cols], par[:tokens, cols]], axis=0)
        v = jnp.concatenate([own[tokens:, cols], par[tokens:, cols]], axis=0)
        near = dot(k, q, 1, 1)
        far = jnp.concatenate(
            [dot(far_own[:tokens, cols], qo, 1, 1), dot(far_par[:tokens, cols], qp, 1, 1)], axis=1
        )
        s = [near[:tokens] + bias[0], near[tokens:] + bias[1], far + bias[2]]
        top = jnp.max(jnp.maximum(jnp.maximum(s[0], s[1]), s[2]), axis=0, keepdims=True)
        e = [jnp.exp2((x - top) * rate) for x in s]
        inv = 1.0 / jnp.sum(e[0] + e[1] + e[2], axis=0, keepdims=True)
        low = [(x * inv).astype(BF16) for x in e]
        for i in range(3):
            probs[j, i * tokens : (i + 1) * tokens, :] = low[i]
        vfo, vfp = far_own[tokens:, cols], far_par[tokens:, cols]
        o_t = dot(v, jnp.concatenate(low[:2], axis=0), 0, 0)
        o_t += jnp.concatenate(
            [dot(vfo, low[2][:, :tokens], 0, 0), dot(vfp, low[2][:, tokens:], 0, 0)], axis=1
        )
        o = o_t.T.astype(BF16)
        att_own[:, cols] = o[:tokens]
        att_back[:, cols] = o[tokens:]
        o_low = o_t.astype(BF16)
        if direct:
            rows = HD // n_dp
            place = bit_reversed(j ^ (me >> 1), (pairs - 1).bit_length())
            for d in range(n_dp):
                block = bit_reversed((d ^ who[1]) >> 1, (n_dp // 2 - 1).bit_length())
                start = pl.multiple_of((block * pairs + place) * rows, rows)
                att_t[(d ^ who[1]) & 1, pl.ds(start, rows), :] = o_low[d * rows : (d + 1) * rows, :]
        else:
            att_t[cols, :] = o_low


def forward(who, listed, live, inputs, after, n_seq, n_dp):
    tokens, half = inputs[0].shape
    features = 2 * half
    heads, pairs = features // HD, half // HD
    direct = n_seq == heads and HD % n_dp == 0 and (HD // n_dp) % 16 == 0
    one = shape_of(tokens, half)
    turned = shape_of(2, half // 2, 2 * tokens) if direct else shape_of(half, 2 * tokens)
    probs, att_own, att_back, turned = call(
        functools.partial(forward_kernel, direct, n_dp),
        (shape_of(pairs, 3 * tokens, 2 * tokens), one, one, turned),
        [SMEM] * 3 + [VMEM] * 6 + [ANY],
        "patch_forward",
    )(who, listed, live, *inputs, after)
    if not direct:
        here = who[0]
        bits, d_bits = (n_seq - 1).bit_length(), (n_dp // 2 - 1).bit_length()
        order = jnp.array([bit_reversed(i, bits) for i in range(n_seq)], jnp.int32) ^ here
        d_order = [bit_reversed(i, d_bits) * 2 + c for c in range(2) for i in range(n_dp // 2)]
        full = jnp.zeros((heads // 2, 2, HD, 2 * tokens), BF16)
        full = lax.dynamic_update_slice(
            full, turned.reshape(heads // 2, 1, HD, 2 * tokens), (0, here & 1, 0, 0)
        )
        full = full.reshape(n_seq, n_dp, features // (n_seq * n_dp), 2 * tokens)
        full = jnp.take(full, order, axis=0)
        full = jnp.take(full, jnp.array(d_order, jnp.int32) ^ who[1], axis=1).transpose(1, 0, 2, 3)
        turned = full.reshape(2, features // 2, 2 * tokens)
    return probs, att_own, att_back, turned, 2 if direct else 1


def backward_kernel(
    who, q_own, q_par, own, par, far_own, far_par, ga_full, cot_par, w, probs,
    grads, ga, edge_a, edge_b,
):
    scale = 1.0 / math.sqrt(HD)
    tokens, half = q_own.shape
    slot = far_slot(who[0])
    last = slice(2 * tokens, 3 * tokens)
    for j in range(half // HD):
        cols = slice(j * HD, (j + 1) * HD)
        mine = head_cols(j, who[0] & 1)
        go = ga_full[:, mine]
        gp = dot(cot_par[...], w[mine, :], 1, 1).astype(BF16)
        g_both = jnp.concatenate([go, gp], axis=0)
        ga[:, cols] = g_both
        qo, qp = q_own[:, cols], q_par[:tokens, cols]
        v = jnp.concatenate([own[tokens:, cols], par[tokens:, cols]], axis=0)
        vfo, vfp = far_own[tokens:, cols], far_par[tokens:, cols]
        gn = dot(v, g_both, 1, 1)
        g = [
            gn[:tokens],
            gn[tokens:],
            jnp.concatenate([dot(vfo, go, 1, 1), dot(vfp, gp, 1, 1)], axis=1),
        ]
        p = [probs[j, i * tokens : (i + 1) * tokens, :].astype(F32) for i in range(3)]
        delta = jnp.sum(p[0] * g[0] + p[1] * g[1] + p[2] * g[2], axis=0, keepdims=True)
        ds = [(p[i] * (g[i] - delta)).astype(BF16) for i in range(3)]
        for i in range(3):
            grads[j, i * tokens : (i + 1) * tokens, :] = ds[i]
        dfo, dfp = ds[2][:, :tokens], ds[2][:, tokens:]
        own_far = jnp.concatenate(
            [dot(dfo, qo, 1, 0) * scale, dot(probs[j, last, :tokens], go, 1, 0)], axis=0
        ).astype(BF16)
        par_far = jnp.concatenate(
            [dot(dfp, qp, 1, 0) * scale, dot(probs[j, last, tokens:], gp, 1, 0)], axis=0
        ).astype(BF16)
        edge_a[:, cols] = jnp.where(slot == 0, own_far, par_far)
        edge_b[:, cols] = jnp.where(slot == 0, par_far, own_far)


def backward(who, inputs, ga_full, cot_par, w, probs):
    tokens, half = inputs[0].shape
    return call(
        backward_kernel,
        (shape_of(*probs.shape),) + (shape_of(2 * tokens, half),) * 3,
        [SMEM] + [VMEM] * 10,
        "patch_backward",
    )(who, *inputs, ga_full, cot_par, w, probs)


def gradient_kernel(
    q_own, q_par, own, par, far_own, far_par, ga, probs, grads, dq_own, dq_back, d_own, d_par
):
    scale = 1.0 / math.sqrt(HD)
    tokens, half = q_own.shape
    near, last = slice(0, 2 * tokens), slice(2 * tokens, 3 * tokens)
    for j in range(half // HD):
        cols = slice(j * HD, (j + 1) * HD)
        q = jnp.concatenate([q_own[:, cols], q_par[:tokens, cols]], axis=0)
        k = jnp.concatenate([own[:tokens, cols], par[:tokens, cols]], axis=0)
        kfo, kfp = far_own[:tokens, cols], far_par[:tokens, cols]
        low, dsn = probs[j, near, :], grads[j, near, :]
        dfo, dfp = grads[j, last, :tokens], grads[j, last, tokens:]
        dq = dot(dsn, k, 0, 0) + jnp.concatenate([dot(dfo, kfo, 0, 0), dot(dfp, kfp, 0, 0)], axis=0)
        dq = (dq * scale).astype(BF16)
        dq_own[:, cols] = dq[:tokens]
        dq_back[:, cols] = dq[tokens:]
        dk = (dot(dsn, q, 1, 0) * scale).astype(BF16)
        dv = dot(low, ga[:, cols], 1, 0).astype(BF16)
        d_own[:tokens, cols] = dk[:tokens]
        d_par[:tokens, cols] = dk[tokens:]
        d_own[tokens:, cols] = dv[:tokens]
        d_par[tokens:, cols] = dv[tokens:]


def gradients(inputs, ga, probs, grads):
    tokens, half = inputs[0].shape
    one, kv = shape_of(tokens, half), shape_of(2 * tokens, half)
    return call(
        gradient_kernel, (one, one, kv, kv), [VMEM] * 9, "patch_gradients"
    )(*inputs, ga, probs, grads)


def weight_kernel(att_keep, att_core, own, par, core_own, core_par, keep, send):
    size = keep.shape[0]
    tokens = own.shape[0]
    for target, start in ((send, size), (keep, 0)):
        rows = slice(start, start + size)
        total = dot(att_keep[rows, :tokens], own[...], 1, 0)
        total += dot(att_keep[rows, tokens:], par[...], 1, 0)
        total += dot(att_core[rows, :tokens], core_own[...], 1, 0)
        total += dot(att_core[rows, tokens:], core_par[...], 1, 0)
        target[...] = total.astype(target.dtype)


def weight_terms(*operands):
    rows = operands[0].shape[0]
    tokens, width = operands[2].shape
    return call(
        weight_kernel,
        (shape_of(rows // 2, width, dtype=F32), shape_of(rows // 2, width)),
        [VMEM] * 6,
        "weight_terms",
    )(*operands)


def output_kernel(who, att_own, att_back, w, out, att):
    mine = who[0] & 1
    for j in range(att_own.shape[1] // HD):
        cols = slice(j * HD, (j + 1) * HD)
        att[:, head_cols(j, mine)] = att_own[:, cols]
        att[:, head_cols(j, 1 - mine)] = att_back[:, cols]
    out[...] = dot(att[...], w[...], 1, 0).astype(BF16)


def finish_output(who, att_own, att_back, w):
    tokens = att_own.shape[0]
    return call(
        output_kernel,
        (shape_of(tokens, w.shape[1]),),
        [SMEM] + [VMEM] * 3,
        "finish_output",
        scratch=[pltpu.VMEM((tokens, w.shape[0]), BF16)],
    )(who, att_own, att_back, w)[0]


def returned_kernel(who, d_par, far_a, far_b, total):
    slot = far_slot(who[0])
    returned = jnp.where(slot == 0, far_b[...].astype(F32), far_a[...].astype(F32))
    total[...] = (d_par[...].astype(F32) + returned).astype(BF16)


def add_returned(who, d_par, far):
    return call(
        returned_kernel, (shape_of(*d_par.shape),), [SMEM] + [VMEM] * 3, "add_returned"
    )(who, d_par, *far)[0]


def final_kernel(who, dq_own, dq_back, own, far_a, far_b, home, dq, dk, dv):
    mine = who[0] & 1
    slot = far_slot(who[0])
    tokens = dk.shape[0]
    for j in range(own.shape[1] // HD):
        cols = slice(j * HD, (j + 1) * HD)
        dq[:, head_cols(j, mine)] = dq_own[:, cols]
        dq[:, head_cols(j, 1 - mine)] = dq_back[:, cols]
        for i, target in ((0, dk), (1, dv)):
            rows = slice(i * tokens, (i + 1) * tokens)
            far = jnp.where(slot == 0, far_a[rows, cols].astype(F32), far_b[rows, cols].astype(F32))
            target[:, head_cols(j, mine)] = (own[rows, cols].astype(F32) + far).astype(BF16)
            target[:, head_cols(j, 1 - mine)] = home[rows, cols]


def finish_gradients(who, dq_own, dq_back, own, far, home):
    tokens, half = dq_own.shape
    return call(
        final_kernel,
        (shape_of(tokens, 2 * half),) * 3,
        [SMEM] + [VMEM] * 6,
        "finish_gradients",
    )(who, dq_own, dq_back, own, *far, home)


def on_device(queries, key_states, values, w_out, cotangent, neighbours, counts):
    n_seq, n_dp = lax.axis_size("seq"), lax.axis_size("dp")
    me, my_dp = lax.axis_index("seq").astype(jnp.int32), lax.axis_index("dp").astype(jnp.int32)
    who = jnp.stack([me, my_dp])
    cot = cotangent[0]

    swap = [(i, i ^ 1) for i in range(n_seq)]
    relay = [(i, i + 2) for i in range(0, n_seq, 2) if i + 2 < n_seq]
    relay += [(i, i - 2) for i in range(1, n_seq, 2) if i - 2 >= 0]
    outer = [(b, a) for a, b in relay]
    edges = [[], []]
    for i in range(n_seq):
        edges[0].append((i, i ^ 2))
        other = i + 2 if (i >> 1) & 1 else i - 2
        if 0 <= other < n_seq:
            edges[1].append((i, other))
    send = lambda x, pairs: lax.ppermute(x, "seq", pairs)
    across = lambda x, k: lax.ppermute(x, "dp", [(i, i ^ k) for i in range(n_dp)])

    kv_send, own = pack_kv(who, key_states[0], values[0])
    q_send, q_own = pack_q(who, neighbours[0], counts, queries[0])
    par = send(kv_send, swap)
    far_par = send(own, outer)
    core_own = across(cot, 1)
    ga_full = dot(cot, w_out, 1, 1).astype(BF16)
    cot_par = send(cot, swap)
    q_par = send(q_send, swap)
    far_own = send(par, relay)
    core_par = across(cot_par, 1)

    inputs = (q_own, q_par, own, par, far_own, far_par)
    probs, att_own, att_back, att_t, step = forward(
        who, neighbours[0], counts, inputs, ga_full, n_seq, n_dp
    )
    att_core = across(att_t[1], 1)
    att_back = send(att_back, swap)
    grads, ga, *leaving = backward(who, inputs, ga_full, cot_par, w_out, probs)
    far = [send(leaving[i], edges[i]) for i in range(2)]
    keep, out = weight_terms(att_t[0], att_core, cot, cot_par, core_own, core_par)
    dq_own, dq_back, d_own, d_par = gradients(inputs, ga, probs, grads)
    dq_back = send(dq_back, swap)
    home = send(add_returned(who, d_par, far), swap)

    hops = []
    bit = 2
    while bit < n_dp:
        hops.append(("dp", n_dp, bit))
        bit *= 2
    while step < n_seq:
        hops.append(("seq", n_seq, step))
        step *= 2
    for place, (axis, count, bit) in enumerate(hops):
        total = keep + lax.ppermute(out, axis, [(i, i ^ bit) for i in range(count)]).astype(F32)
        rows = total.shape[0] // 2
        if place + 1 < len(hops):
            keep, out = total[:rows], total[rows:].astype(BF16)

    output = finish_output(who, att_own, att_back, w_out)
    dq, dk, dv = finish_gradients(who, dq_own, dq_back, d_own, far, home)
    return (output[None], dq[None], dk[None], dv[None], total)


def solution(mesh):
    placed = (
        P("dp", "seq", None),
        P("dp", "seq", None),
        P("dp", "seq", None),
        P(),
        P("dp", "seq", None),
        P("dp", "seq", None),
        P("dp", "seq"),
    )
    return jax.shard_map(
        on_device,
        mesh=mesh,
        in_specs=placed,
        out_specs=(
            P("dp", "seq", None),
            P("dp", "seq", None),
            P("dp", "seq", None),
            P("dp", "seq", None),
            P(("seq", "dp"), None),
        ),
        check_vma=False,
    )
```

```python
import functools
import math

import jax
import jax.numpy as jnp
from jax import lax
from jax.experimental import pallas as pl
from jax.experimental.pallas import tpu as pltpu
from jax.sharding import PartitionSpec as P

HD = 128
VMEM_LIMIT = 12 * 1024 * 1024
F32 = jnp.float32
BF16 = jnp.bfloat16
VMEM = pl.BlockSpec(memory_space=pltpu.VMEM)
SMEM = pl.BlockSpec(memory_space=pltpu.SMEM)
HBM = pl.BlockSpec(memory_space=pltpu.HBM)
ANY = pl.BlockSpec(memory_space=pl.ANY)
FLAG_ROWS = 16


def dot(a, b, ca, cb):
    return lax.dot_general(a, b, (((ca,), (cb,)), ((), ())), preferred_element_type=F32)


def bit_reversed(index, bits):
    out = 0
    for b in range(bits):
        out = out * 2 + ((index >> b) & 1)
    return out


def shape_of(*dims, dtype=BF16):
    return jax.ShapeDtypeStruct(dims, dtype)


def call(body, out_shape, in_specs, name, scratch=()):
    return pl.pallas_call(
        body,
        out_shape=out_shape,
        in_specs=in_specs,
        out_specs=(VMEM,) * len(out_shape),
        scratch_shapes=list(scratch),
        compiler_params=pltpu.CompilerParams(vmem_limit_bytes=VMEM_LIMIT),
        cost_estimate=pl.CostEstimate(flops=0, bytes_accessed=0, transcendentals=0),
        name=name,
    )


def head_cols(pair, parity):
    return pl.ds(pl.multiple_of((2 * pair + parity) * HD, HD), HD)


def listed_flags(me, listed, live):
    far_patch = jnp.where(me % 2 == 0, me - 1, me + 1)
    near, far = jnp.int32(0), jnp.int32(0)
    for slot in range(listed.shape[1]):
        used = slot < live[0, 0]
        near = jnp.where(used & (listed[0, slot] == (me ^ 1)), 1, near)
        far = jnp.where(used & (listed[0, slot] == far_patch), 1, far)
    return near, far


def in_hbm(x):
    return pltpu.with_memory_space_constraint(x, pltpu.HBM)


def pack_kernel(who, listed, live, q, k, v, kv_send, kv_keep, q_send, q_keep, listed_in, sems):
    mine = who[0] & 1
    tokens, half = q_keep.shape
    copies = []

    def copy(source, target):
        copies.append(pltpu.make_async_copy(source, target, sems.at[len(copies)]))
        copies[-1].start()

    copy(listed, listed_in)
    for kv, q_to, parity in ((kv_send, q_send, 1 - mine), (kv_keep, q_keep, mine)):
        for source, target, row in ((k, kv, 0), (v, kv, tokens), (q, q_to, 0)):
            for j in range(half // HD):
                copy(
                    source.at[:, head_cols(j, parity)],
                    target.at[row : row + tokens, j * HD : (j + 1) * HD],
                )
    copies[0].wait()
    near, far = listed_flags(who[0], listed_in, live)
    left = lax.broadcasted_iota(jnp.int32, (FLAG_ROWS, half), 1) < half // 2
    q_send[tokens : tokens + FLAG_ROWS, :] = jnp.where(left, near, far).astype(F32).astype(BF16)
    for item in copies[1:]:
        item.wait()


def pack(who, listed, live, q, k, v):
    tokens, features = k.shape
    half = features // 2
    kv = shape_of(2 * tokens, half)
    return call(
        pack_kernel,
        (kv, kv, shape_of(tokens + FLAG_ROWS, half), shape_of(tokens, half)),
        [SMEM, HBM, SMEM] + [HBM] * 3,
        "pack_heads",
        scratch=[
            pltpu.SMEM(listed.shape, jnp.int32),
            pltpu.SemaphoreType.DMA((3 * features // HD + 1,)),
        ],
    )(who, in_hbm(listed), live, in_hbm(q), in_hbm(k), in_hbm(v))


def turn_kernel(who, cot, cot_par, w, ga, cot_in, w_in, sems):
    tokens = cot.shape[0]
    pairs = ga.shape[1] // HD
    copies = [pltpu.make_async_copy(cot, cot_in, sems.at[pairs])]
    for j in range(pairs):
        rows = w.at[head_cols(j, who[0] & 1), :]
        copies.append(pltpu.make_async_copy(rows, w_in.at[j], sems.at[j]))
    for item in copies:
        item.start()
    copies[0].wait()
    for j in range(pairs):
        cols = slice(j * HD, (j + 1) * HD)
        copies[j + 1].wait()
        ga[:tokens, cols] = dot(cot_in[...], w_in[j], 1, 1).astype(BF16)
        ga[tokens:, cols] = dot(cot_par[...], w_in[j], 1, 1).astype(BF16)


def grad_attended(who, cot, cot_par, w):
    tokens, width = cot.shape
    pairs = w.shape[0] // (2 * HD)
    return call(
        turn_kernel,
        (shape_of(2 * tokens, pairs * HD),),
        [SMEM, HBM, VMEM, HBM],
        "grad_attended",
        scratch=[
            pltpu.VMEM((tokens, width), BF16),
            pltpu.VMEM((pairs, HD, width), BF16),
            pltpu.SemaphoreType.DMA((pairs + 1,)),
        ],
    )(who, in_hbm(cot), cot_par, in_hbm(w))[0]


def far_slot(me):
    return 1 - ((me & 1) ^ ((me >> 1) & 1))


def forward_kernel(
    direct, n_dp, who, listed, live, q_own, q_par, own, par, far_own, far_par, after,
    probs, att_own, att_back, att_t,
):
    rate = math.log2(math.e) / math.sqrt(HD)
    tokens, half = q_own.shape
    pairs = half // HD
    me = who[0]
    near_flag, far_flag = listed_flags(me, listed, live)
    barred = lambda x: jnp.where(x > 0, 0.0, -jnp.inf)
    theirs = q_par[tokens : tokens + FLAG_ROWS, :].astype(F32)[:1]
    left = lax.broadcasted_iota(jnp.int32, (1, 2 * tokens), 1) < tokens
    near_par = barred(jnp.broadcast_to(theirs[:, :1], (1, 2 * tokens)))
    far_par_bias = barred(jnp.broadcast_to(theirs[:, half - 1 :], (1, 2 * tokens)))
    bias = (
        jnp.where(left, 0.0, near_par),
        jnp.where(left, barred(near_flag), 0.0),
        jnp.where(left, barred(far_flag), far_par_bias),
    )
    for j in range(pairs):
        cols = slice(j * HD, (j + 1) * HD)
        qo, qp = q_own[:, cols], q_par[:tokens, cols]
        q = jnp.concatenate([qo, qp], axis=0)
        k = jnp.concatenate([own[:tokens, cols], par[:tokens, cols]], axis=0)
        v = jnp.concatenate([own[tokens:, cols], par[tokens:, cols]], axis=0)
        near = dot(k, q, 1, 1)
        far = jnp.concatenate(
            [dot(far_own[:tokens, cols], qo, 1, 1), dot(far_par[:tokens, cols], qp, 1, 1)], axis=1
        )
        s = [near[:tokens] + bias[0], near[tokens:] + bias[1], far + bias[2]]
        top = jnp.max(jnp.maximum(jnp.maximum(s[0], s[1]), s[2]), axis=0, keepdims=True)
        e = [jnp.exp2((x - top) * rate) for x in s]
        inv = 1.0 / jnp.sum(e[0] + e[1] + e[2], axis=0, keepdims=True)
        low = [(x * inv).astype(BF16) for x in e]
        for i in range(3):
            probs[j, i * tokens : (i + 1) * tokens, :] = low[i]
        vfo, vfp = far_own[tokens:, cols], far_par[tokens:, cols]
        o_t = dot(v, jnp.concatenate(low[:2], axis=0), 0, 0)
        o_t += jnp.concatenate(
            [dot(vfo, low[2][:, :tokens], 0, 0), dot(vfp, low[2][:, tokens:], 0, 0)], axis=1
        )
        o = o_t.T.astype(BF16)
        att_own[:, cols] = o[:tokens]
        att_back[:, cols] = o[tokens:]
        o_low = o_t.astype(BF16)
        if direct:
            rows = HD // n_dp
            place = bit_reversed(j ^ (me >> 1), (pairs - 1).bit_length())
            for d in range(n_dp):
                block = bit_reversed((d ^ who[1]) >> 1, (n_dp // 2 - 1).bit_length())
                start = pl.multiple_of((block * pairs + place) * rows, rows)
                att_t[(d ^ who[1]) & 1, pl.ds(start, rows), :] = o_low[d * rows : (d + 1) * rows, :]
        else:
            att_t[cols, :] = o_low


def forward(who, listed, live, inputs, after, n_seq, n_dp):
    tokens, half = inputs[0].shape
    features = 2 * half
    heads, pairs = features // HD, half // HD
    direct = n_seq == heads and HD % n_dp == 0 and (HD // n_dp) % 16 == 0
    one = shape_of(tokens, half)
    turned = shape_of(2, half // 2, 2 * tokens) if direct else shape_of(half, 2 * tokens)
    probs, att_own, att_back, turned = call(
        functools.partial(forward_kernel, direct, n_dp),
        (shape_of(pairs, 3 * tokens, 2 * tokens), one, one, turned),
        [SMEM] * 3 + [VMEM] * 6 + [ANY],
        "patch_forward",
    )(who, listed, live, *inputs, after)
    if not direct:
        here = who[0]
        bits, d_bits = (n_seq - 1).bit_length(), (n_dp // 2 - 1).bit_length()
        order = jnp.array([bit_reversed(i, bits) for i in range(n_seq)], jnp.int32) ^ here
        d_order = [bit_reversed(i, d_bits) * 2 + c for c in range(2) for i in range(n_dp // 2)]
        full = jnp.zeros((heads // 2, 2, HD, 2 * tokens), BF16)
        full = lax.dynamic_update_slice(
            full, turned.reshape(heads // 2, 1, HD, 2 * tokens), (0, here & 1, 0, 0)
        )
        full = full.reshape(n_seq, n_dp, features // (n_seq * n_dp), 2 * tokens)
        full = jnp.take(full, order, axis=0)
        full = jnp.take(full, jnp.array(d_order, jnp.int32) ^ who[1], axis=1).transpose(1, 0, 2, 3)
        turned = full.reshape(2, features // 2, 2 * tokens)
    return probs, att_own, att_back, turned, 2 if direct else 1


def backward_kernel(
    who, q_own, q_par, own, par, far_own, far_par, ga, probs, grads, edge_a, edge_b
):
    scale = 1.0 / math.sqrt(HD)
    tokens, half = q_own.shape
    slot = far_slot(who[0])
    last = slice(2 * tokens, 3 * tokens)
    for j in range(half // HD):
        cols = slice(j * HD, (j + 1) * HD)
        g_both = ga[:, cols]
        go, gp = g_both[:tokens], g_both[tokens:]
        qo, qp = q_own[:, cols], q_par[:tokens, cols]
        v = jnp.concatenate([own[tokens:, cols], par[tokens:, cols]], axis=0)
        vfo, vfp = far_own[tokens:, cols], far_par[tokens:, cols]
        gn = dot(v, g_both, 1, 1)
        g = [
            gn[:tokens],
            gn[tokens:],
            jnp.concatenate([dot(vfo, go, 1, 1), dot(vfp, gp, 1, 1)], axis=1),
        ]
        p = [probs[j, i * tokens : (i + 1) * tokens, :].astype(F32) for i in range(3)]
        delta = jnp.sum(p[0] * g[0] + p[1] * g[1] + p[2] * g[2], axis=0, keepdims=True)
        ds = [(p[i] * (g[i] - delta)).astype(BF16) for i in range(3)]
        for i in range(3):
            grads[j, i * tokens : (i + 1) * tokens, :] = ds[i]
        dfo, dfp = ds[2][:, :tokens], ds[2][:, tokens:]
        own_far = jnp.concatenate(
            [dot(dfo, qo, 1, 0) * scale, dot(probs[j, last, :tokens], go, 1, 0)], axis=0
        ).astype(BF16)
        par_far = jnp.concatenate(
            [dot(dfp, qp, 1, 0) * scale, dot(probs[j, last, tokens:], gp, 1, 0)], axis=0
        ).astype(BF16)
        edge_a[:, cols] = jnp.where(slot == 0, own_far, par_far)
        edge_b[:, cols] = jnp.where(slot == 0, par_far, own_far)


def backward(who, inputs, ga, probs):
    tokens, half = inputs[0].shape
    return call(
        backward_kernel,
        (shape_of(*probs.shape),) + (shape_of(2 * tokens, half),) * 2,
        [SMEM] + [VMEM] * 8,
        "patch_backward",
    )(who, *inputs, ga, probs)


def gradient_kernel(
    q_own, q_par, own, par, far_own, far_par, ga, probs, grads, dq_own, dq_back, d_own, d_par
):
    scale = 1.0 / math.sqrt(HD)
    tokens, half = q_own.shape
    near, last = slice(0, 2 * tokens), slice(2 * tokens, 3 * tokens)
    for j in range(half // HD):
        cols = slice(j * HD, (j + 1) * HD)
        q = jnp.concatenate([q_own[:, cols], q_par[:tokens, cols]], axis=0)
        k = jnp.concatenate([own[:tokens, cols], par[:tokens, cols]], axis=0)
        kfo, kfp = far_own[:tokens, cols], far_par[:tokens, cols]
        low, dsn = probs[j, near, :], grads[j, near, :]
        dfo, dfp = grads[j, last, :tokens], grads[j, last, tokens:]
        dq = dot(dsn, k, 0, 0) + jnp.concatenate([dot(dfo, kfo, 0, 0), dot(dfp, kfp, 0, 0)], axis=0)
        dq = (dq * scale).astype(BF16)
        dq_own[:, cols] = dq[:tokens]
        dq_back[:, cols] = dq[tokens:]
        dk = (dot(dsn, q, 1, 0) * scale).astype(BF16)
        dv = dot(low, ga[:, cols], 1, 0).astype(BF16)
        d_own[:tokens, cols] = dk[:tokens]
        d_par[:tokens, cols] = dk[tokens:]
        d_own[tokens:, cols] = dv[:tokens]
        d_par[tokens:, cols] = dv[tokens:]


def gradients(inputs, ga, probs, grads):
    tokens, half = inputs[0].shape
    one, kv = shape_of(tokens, half), shape_of(2 * tokens, half)
    return call(
        gradient_kernel, (one, one, kv, kv), [VMEM] * 9, "patch_gradients"
    )(*inputs, ga, probs, grads)


def weight_kernel(att_keep, att_core, own, par, core_own, core_par, after, keep, send):
    size = keep.shape[0]
    tokens = own.shape[0]
    for target, start in ((send, size), (keep, 0)):
        rows = slice(start, start + size)
        total = dot(att_keep[rows, :tokens], own[...], 1, 0)
        total += dot(att_keep[rows, tokens:], par[...], 1, 0)
        total += dot(att_core[rows, :tokens], core_own[...], 1, 0)
        total += dot(att_core[rows, tokens:], core_par[...], 1, 0)
        target[...] = total.astype(target.dtype)


def weight_terms(*operands):
    rows = operands[0].shape[0]
    tokens, width = operands[2].shape
    return call(
        weight_kernel,
        (shape_of(rows // 2, width, dtype=F32), shape_of(rows // 2, width)),
        [VMEM] * 6 + [ANY],
        "weight_terms",
    )(*operands)


def query_kernel(who, att_own, att_back, dq_own, dq_back, w, out, dq, att):
    mine = who[0] & 1
    for j in range(att_own.shape[1] // HD):
        cols = slice(j * HD, (j + 1) * HD)
        att[:, head_cols(j, mine)] = att_own[:, cols]
        att[:, head_cols(j, 1 - mine)] = att_back[:, cols]
        dq[:, head_cols(j, mine)] = dq_own[:, cols]
        dq[:, head_cols(j, 1 - mine)] = dq_back[:, cols]
    out[...] = dot(att[...], w[...], 1, 0).astype(BF16)


def finish_queries(who, att_own, att_back, dq_own, dq_back, w):
    tokens = att_own.shape[0]
    return call(
        query_kernel,
        (shape_of(tokens, w.shape[1]), shape_of(tokens, w.shape[0])),
        [SMEM] + [VMEM] * 5,
        "finish_queries",
        scratch=[pltpu.VMEM((tokens, w.shape[0]), BF16)],
    )(who, att_own, att_back, dq_own, dq_back, w)


def returned_kernel(who, d_par, far_a, far_b, total):
    slot = far_slot(who[0])
    returned = jnp.where(slot == 0, far_b[...].astype(F32), far_a[...].astype(F32))
    total[...] = (d_par[...].astype(F32) + returned).astype(BF16)


def add_returned(who, d_par, far):
    return call(
        returned_kernel, (shape_of(*d_par.shape),), [SMEM] + [VMEM] * 3, "add_returned"
    )(who, d_par, *far)[0]


def key_kernel(who, own, far_a, far_b, home, keep, out, dk, dv, total):
    mine = who[0] & 1
    slot = far_slot(who[0])
    tokens = dk.shape[0]
    for i, target in ((0, dk), (1, dv)):
        rows = slice(i * tokens, (i + 1) * tokens)
        for j in range(own.shape[1] // HD):
            cols = slice(j * HD, (j + 1) * HD)
            far = jnp.where(slot == 0, far_a[rows, cols].astype(F32), far_b[rows, cols].astype(F32))
            target[:, head_cols(j, mine)] = (own[rows, cols].astype(F32) + far).astype(BF16)
            target[:, head_cols(j, 1 - mine)] = home[rows, cols]
    total[...] = keep[...] + out[...].astype(F32)


def finish_keys(who, own, far, home, keep, out):
    tokens, half = own.shape[0] // 2, own.shape[1]
    return call(
        key_kernel,
        (shape_of(tokens, 2 * half),) * 2 + (shape_of(*keep.shape, dtype=F32),),
        [SMEM] + [VMEM] * 6,
        "finish_keys",
    )(who, own, *far, home, keep, out)


def on_device(queries, key_states, values, w_out, cotangent, neighbours, counts):
    n_seq, n_dp = lax.axis_size("seq"), lax.axis_size("dp")
    me, my_dp = lax.axis_index("seq").astype(jnp.int32), lax.axis_index("dp").astype(jnp.int32)
    who = jnp.stack([me, my_dp])
    cot = cotangent[0]

    swap = [(i, i ^ 1) for i in range(n_seq)]
    relay = [(i, i + 2) for i in range(0, n_seq, 2) if i + 2 < n_seq]
    relay += [(i, i - 2) for i in range(1, n_seq, 2) if i - 2 >= 0]
    outer = [(b, a) for a, b in relay]
    edges = [[], []]
    for i in range(n_seq):
        edges[0].append((i, i ^ 2))
        other = i + 2 if (i >> 1) & 1 else i - 2
        if 0 <= other < n_seq:
            edges[1].append((i, other))
    send = lambda x, pairs: lax.ppermute(x, "seq", pairs)
    across = lambda x, k: lax.ppermute(x, "dp", [(i, i ^ k) for i in range(n_dp)])

    kv_send, own, q_send, q_own = pack(
        who, neighbours[0], counts, queries[0], key_states[0], values[0]
    )
    par = send(kv_send, swap)
    q_par = send(q_send, swap)
    far_par = send(own, outer)
    cot_par = send(cot, swap)
    far_own = send(par, relay)
    core_own, core_par = across(cot, 1), across(cot_par, 1)
    ga = grad_attended(who, cot, cot_par, w_out)

    inputs = (q_own, q_par, own, par, far_own, far_par)
    probs, att_own, att_back, att_t, step = forward(
        who, neighbours[0], counts, inputs, ga, n_seq, n_dp
    )
    att_core = across(att_t[1], 1)
    att_back = send(att_back, swap)
    grads, *leaving = backward(who, inputs, ga, probs)
    far = [send(leaving[i], edges[i]) for i in range(2)]
    keep, out = weight_terms(att_t[0], att_core, cot, cot_par, core_own, core_par, leaving[0])
    dq_own, dq_back, d_own, d_par = gradients(inputs, ga, probs, grads)
    dq_back = send(dq_back, swap)
    home = send(add_returned(who, d_par, far), swap)

    hops = []
    bit = 2
    while bit < n_dp:
        hops.append(("dp", n_dp, bit))
        bit *= 2
    while step < n_seq:
        hops.append(("seq", n_seq, step))
        step *= 2
    for place, (axis, count, bit) in enumerate(hops):
        out = lax.ppermute(out, axis, [(i, i ^ bit) for i in range(count)])
        if place + 1 < len(hops):
            total = keep + out.astype(F32)
            rows = total.shape[0] // 2
            keep, out = total[:rows], total[rows:].astype(BF16)

    output, dq = finish_queries(who, att_own, att_back, dq_own, dq_back, w_out)
    dk, dv, total = finish_keys(who, d_own, far, home, keep, out)
    return (output[None], dq[None], dk[None], dv[None], total)


def solution(mesh):
    placed = (
        P("dp", "seq", None),
        P("dp", "seq", None),
        P("dp", "seq", None),
        P(),
        P("dp", "seq", None),
        P("dp", "seq", None),
        P("dp", "seq"),
    )
    return jax.shard_map(
        on_device,
        mesh=mesh,
        in_specs=placed,
        out_specs=(
            P("dp", "seq", None),
            P("dp", "seq", None),
            P("dp", "seq", None),
            P("dp", "seq", None),
            P(("seq", "dp"), None),
        ),
        check_vma=False,
    )
```

```python
import functools
import math

import jax
import jax.numpy as jnp
from jax import lax
from jax.experimental import pallas as pl
from jax.experimental.pallas import tpu as pltpu
from jax.sharding import PartitionSpec as P

HD = 128
VMEM_LIMIT = 12 * 1024 * 1024
F32 = jnp.float32
BF16 = jnp.bfloat16
VMEM = pl.BlockSpec(memory_space=pltpu.VMEM)
SMEM = pl.BlockSpec(memory_space=pltpu.SMEM)
HBM = pl.BlockSpec(memory_space=pltpu.HBM)
ANY = pl.BlockSpec(memory_space=pl.ANY)
FLAG_ROWS = 16


def dot(a, b, ca, cb):
    return lax.dot_general(a, b, (((ca,), (cb,)), ((), ())), preferred_element_type=F32)


def bit_reversed(index, bits):
    out = 0
    for b in range(bits):
        out = out * 2 + ((index >> b) & 1)
    return out


def shape_of(*dims, dtype=BF16):
    return jax.ShapeDtypeStruct(dims, dtype)


def call(body, out_shape, in_specs, name, scratch=()):
    return pl.pallas_call(
        body,
        out_shape=out_shape,
        in_specs=in_specs,
        out_specs=(VMEM,) * len(out_shape),
        scratch_shapes=list(scratch),
        compiler_params=pltpu.CompilerParams(vmem_limit_bytes=VMEM_LIMIT),
        cost_estimate=pl.CostEstimate(flops=0, bytes_accessed=0, transcendentals=0),
        name=name,
    )


def head_cols(pair, parity):
    return pl.ds(pl.multiple_of((2 * pair + parity) * HD, HD), HD)


def listed_flags(me, listed):
    far_patch = jnp.where(me % 2 == 0, me - 1, me + 1)
    near, far = jnp.int32(0), jnp.int32(0)
    for slot in range(listed.shape[1]):
        near = jnp.where(listed[0, slot] == (me ^ 1), 1, near)
        far = jnp.where(listed[0, slot] == far_patch, 1, far)
    return near, far


def in_hbm(x):
    return pltpu.with_memory_space_constraint(x, pltpu.HBM)


def pack_kernel(who, listed, q, k, v, kv_send, kv_keep, q_send, q_keep, listed_in, sems):
    mine = who[0] & 1
    tokens, half = q_keep.shape
    copies = []

    def copy(source, target):
        copies.append(pltpu.make_async_copy(source, target, sems.at[len(copies)]))
        copies[-1].start()

    copy(listed, listed_in)
    for kv, q_to, parity in ((kv_send, q_send, 1 - mine), (kv_keep, q_keep, mine)):
        for source, target, row in ((k, kv, 0), (v, kv, tokens), (q, q_to, 0)):
            for j in range(half // HD):
                copy(
                    source.at[:, head_cols(j, parity)],
                    target.at[row : row + tokens, j * HD : (j + 1) * HD],
                )
    copies[0].wait()
    near, far = listed_flags(who[0], listed_in)
    left = lax.broadcasted_iota(jnp.int32, (FLAG_ROWS, half), 1) < half // 2
    q_send[tokens : tokens + FLAG_ROWS, :] = jnp.where(left, near, far).astype(F32).astype(BF16)
    for item in copies[1:]:
        item.wait()


def pack(who, listed, q, k, v):
    tokens, features = k.shape
    half = features // 2
    kv = shape_of(2 * tokens, half)
    return call(
        pack_kernel,
        (kv, kv, shape_of(tokens + FLAG_ROWS, half), shape_of(tokens, half)),
        [SMEM] + [HBM] * 4,
        "pack_heads",
        scratch=[
            pltpu.SMEM(listed.shape, jnp.int32),
            pltpu.SemaphoreType.DMA((3 * features // HD + 1,)),
        ],
    )(who, *[in_hbm(x) for x in (listed, q, k, v)])


def turn_kernel(who, cot, cot_par, w, ga, cot_in, w_in, sems):
    tokens = cot.shape[0]
    pairs = ga.shape[1] // HD
    copies = [pltpu.make_async_copy(cot, cot_in, sems.at[pairs])]
    for j in range(pairs):
        rows = w.at[head_cols(j, who[0] & 1), :]
        copies.append(pltpu.make_async_copy(rows, w_in.at[j], sems.at[j]))
    for item in copies:
        item.start()
    copies[0].wait()
    for j in range(pairs):
        cols = slice(j * HD, (j + 1) * HD)
        copies[j + 1].wait()
        ga[:tokens, cols] = dot(cot_in[...], w_in[j], 1, 1).astype(BF16)
        ga[tokens:, cols] = dot(cot_par[...], w_in[j], 1, 1).astype(BF16)


def grad_attended(who, cot, cot_par, w):
    tokens, width = cot.shape
    pairs = w.shape[0] // (2 * HD)
    return call(
        turn_kernel,
        (shape_of(2 * tokens, pairs * HD),),
        [SMEM, HBM, VMEM, HBM],
        "grad_attended",
        scratch=[
            pltpu.VMEM((tokens, width), BF16),
            pltpu.VMEM((pairs, HD, width), BF16),
            pltpu.SemaphoreType.DMA((pairs + 1,)),
        ],
    )(who, in_hbm(cot), cot_par, in_hbm(w))[0]


def far_slot(me):
    return (me & 1) ^ ((me >> 1) & 1)


def forward_kernel(
    direct, n_dp, who, listed, q_own, q_par, own, par, far_own, far_par, after,
    probs, att_own, att_back, att_t,
):
    rate = math.log2(math.e) / math.sqrt(HD)
    tokens, half = q_own.shape
    pairs = half // HD
    me = who[0]
    near_flag, far_flag = listed_flags(me, listed)
    barred = lambda x: jnp.where(x > 0, 0.0, -jnp.inf)
    theirs = q_par[tokens : tokens + FLAG_ROWS, :].astype(F32)[:1]
    left = lax.broadcasted_iota(jnp.int32, (1, 2 * tokens), 1) < tokens
    near_par = barred(jnp.broadcast_to(theirs[:, :1], (1, 2 * tokens)))
    far_par_bias = barred(jnp.broadcast_to(theirs[:, half - 1 :], (1, 2 * tokens)))
    bias = (
        jnp.where(left, 0.0, near_par),
        jnp.where(left, barred(near_flag), 0.0),
        jnp.where(left, barred(far_flag), far_par_bias),
    )
    for j in range(pairs):
        cols = slice(j * HD, (j + 1) * HD)
        qo, qp = q_own[:, cols], q_par[:tokens, cols]
        q = jnp.concatenate([qo, qp], axis=0)
        k = jnp.concatenate([own[:tokens, cols], par[:tokens, cols]], axis=0)
        v = jnp.concatenate([own[tokens:, cols], par[tokens:, cols]], axis=0)
        near = dot(k, q, 1, 1)
        far = jnp.concatenate(
            [dot(far_own[:tokens, cols], qo, 1, 1), dot(far_par[:tokens, cols], qp, 1, 1)], axis=1
        )
        s = [near[:tokens] + bias[0], near[tokens:] + bias[1], far + bias[2]]
        top = jnp.max(jnp.maximum(jnp.maximum(s[0], s[1]), s[2]), axis=0, keepdims=True)
        e = [jnp.exp2((x - top) * rate) for x in s]
        inv = 1.0 / jnp.sum(e[0] + e[1] + e[2], axis=0, keepdims=True)
        low = [(x * inv).astype(BF16) for x in e]
        for i in range(3):
            probs[j, i * tokens : (i + 1) * tokens, :] = low[i]
        vfo, vfp = far_own[tokens:, cols], far_par[tokens:, cols]
        o_t = dot(v, jnp.concatenate(low[:2], axis=0), 0, 0)
        o_t += jnp.concatenate(
            [dot(vfo, low[2][:, :tokens], 0, 0), dot(vfp, low[2][:, tokens:], 0, 0)], axis=1
        )
        o = o_t.T.astype(BF16)
        att_own[:, cols] = o[:tokens]
        att_back[:, cols] = o[tokens:]
        o_low = o_t.astype(BF16)
        if direct:
            rows = HD // n_dp
            place = bit_reversed(j ^ (me >> 1), (pairs - 1).bit_length())
            for d in range(n_dp):
                block = bit_reversed((d ^ who[1]) >> 1, (n_dp // 2 - 1).bit_length())
                start = pl.multiple_of((block * pairs + place) * rows, rows)
                att_t[(d ^ who[1]) & 1, pl.ds(start, rows), :] = o_low[d * rows : (d + 1) * rows, :]
        else:
            att_t[cols, :] = o_low


def forward(who, listed, inputs, after, n_seq, n_dp):
    tokens, half = inputs[0].shape
    features = 2 * half
    heads, pairs = features // HD, half // HD
    direct = n_seq == heads and HD % n_dp == 0 and (HD // n_dp) % 16 == 0
    one = shape_of(tokens, half)
    turned = shape_of(2, half // 2, 2 * tokens) if direct else shape_of(half, 2 * tokens)
    probs, att_own, att_back, turned = call(
        functools.partial(forward_kernel, direct, n_dp),
        (shape_of(pairs, 3 * tokens, 2 * tokens), one, one, turned),
        [SMEM] * 2 + [VMEM] * 6 + [ANY],
        "patch_forward",
    )(who, listed, *inputs, after)
    if not direct:
        here = who[0]
        bits, d_bits = (n_seq - 1).bit_length(), (n_dp // 2 - 1).bit_length()
        order = jnp.array([bit_reversed(i, bits) for i in range(n_seq)], jnp.int32) ^ here
        d_order = [bit_reversed(i, d_bits) * 2 + c for c in range(2) for i in range(n_dp // 2)]
        full = jnp.zeros((heads // 2, 2, HD, 2 * tokens), BF16)
        full = lax.dynamic_update_slice(
            full, turned.reshape(heads // 2, 1, HD, 2 * tokens), (0, here & 1, 0, 0)
        )
        full = full.reshape(n_seq, n_dp, features // (n_seq * n_dp), 2 * tokens)
        full = jnp.take(full, order, axis=0)
        full = jnp.take(full, jnp.array(d_order, jnp.int32) ^ who[1], axis=1).transpose(1, 0, 2, 3)
        turned = full.reshape(2, features // 2, 2 * tokens)
    return probs, att_own, att_back, turned, 2 if direct else 1


def backward_kernel(
    who, q_own, q_par, own, par, far_own, far_par, ga, probs, grads, edge_a, edge_b
):
    scale = 1.0 / math.sqrt(HD)
    tokens, half = q_own.shape
    slot = far_slot(who[0])
    last = slice(2 * tokens, 3 * tokens)
    for j in range(half // HD):
        cols = slice(j * HD, (j + 1) * HD)
        g_both = ga[:, cols]
        go, gp = g_both[:tokens], g_both[tokens:]
        qo, qp = q_own[:, cols], q_par[:tokens, cols]
        v = jnp.concatenate([own[tokens:, cols], par[tokens:, cols]], axis=0)
        vfo, vfp = far_own[tokens:, cols], far_par[tokens:, cols]
        gn = dot(v, g_both, 1, 1)
        g = [
            gn[:tokens],
            gn[tokens:],
            jnp.concatenate([dot(vfo, go, 1, 1), dot(vfp, gp, 1, 1)], axis=1),
        ]
        p = [probs[j, i * tokens : (i + 1) * tokens, :].astype(F32) for i in range(3)]
        delta = jnp.sum(p[0] * g[0] + p[1] * g[1] + p[2] * g[2], axis=0, keepdims=True)
        ds = [(p[i] * (g[i] - delta)).astype(BF16) for i in range(3)]
        for i in range(3):
            grads[j, i * tokens : (i + 1) * tokens, :] = ds[i]
        dfo, dfp = ds[2][:, :tokens], ds[2][:, tokens:]
        own_far = jnp.concatenate(
            [dot(dfo, qo, 1, 0) * scale, dot(probs[j, last, :tokens], go, 1, 0)], axis=0
        ).astype(BF16)
        par_far = jnp.concatenate(
            [dot(dfp, qp, 1, 0) * scale, dot(probs[j, last, tokens:], gp, 1, 0)], axis=0
        ).astype(BF16)
        edge_a[:, cols] = jnp.where(slot == 0, own_far, par_far)
        edge_b[:, cols] = jnp.where(slot == 0, par_far, own_far)


def backward(who, inputs, ga, probs):
    tokens, half = inputs[0].shape
    return call(
        backward_kernel,
        (shape_of(*probs.shape),) + (shape_of(2 * tokens, half),) * 2,
        [SMEM] + [VMEM] * 8,
        "patch_backward",
    )(who, *inputs, ga, probs)


def gradient_kernel(
    q_own, q_par, own, par, far_own, far_par, ga, probs, grads, dq_own, dq_back, d_own, d_par
):
    scale = 1.0 / math.sqrt(HD)
    tokens, half = q_own.shape
    near, last = slice(0, 2 * tokens), slice(2 * tokens, 3 * tokens)
    for j in range(half // HD):
        cols = slice(j * HD, (j + 1) * HD)
        q = jnp.concatenate([q_own[:, cols], q_par[:tokens, cols]], axis=0)
        k = jnp.concatenate([own[:tokens, cols], par[:tokens, cols]], axis=0)
        kfo, kfp = far_own[:tokens, cols], far_par[:tokens, cols]
        low, dsn = probs[j, near, :], grads[j, near, :]
        dfo, dfp = grads[j, last, :tokens], grads[j, last, tokens:]
        dq = dot(dsn, k, 0, 0) + jnp.concatenate([dot(dfo, kfo, 0, 0), dot(dfp, kfp, 0, 0)], axis=0)
        dq = (dq * scale).astype(BF16)
        dq_own[:, cols] = dq[:tokens]
        dq_back[:, cols] = dq[tokens:]
        dk = (dot(dsn, q, 1, 0) * scale).astype(BF16)
        dv = dot(low, ga[:, cols], 1, 0).astype(BF16)
        d_own[:tokens, cols] = dk[:tokens]
        d_par[:tokens, cols] = dk[tokens:]
        d_own[tokens:, cols] = dv[:tokens]
        d_par[tokens:, cols] = dv[tokens:]


def gradients(inputs, ga, probs, grads):
    tokens, half = inputs[0].shape
    one, kv = shape_of(tokens, half), shape_of(2 * tokens, half)
    return call(
        gradient_kernel, (one, one, kv, kv), [VMEM] * 9, "patch_gradients"
    )(*inputs, ga, probs, grads)


def weight_kernel(att_keep, att_core, own, par, core_own, core_par, _after, _also, keep, send):
    size = keep.shape[0]
    tokens = own.shape[0]
    for target, start in ((send, size), (keep, 0)):
        rows = slice(start, start + size)
        total = dot(att_keep[rows, :tokens], own[...], 1, 0)
        total += dot(att_keep[rows, tokens:], par[...], 1, 0)
        total += dot(att_core[rows, :tokens], core_own[...], 1, 0)
        total += dot(att_core[rows, tokens:], core_par[...], 1, 0)
        target[...] = total.astype(target.dtype)


def weight_terms(*operands):
    rows = operands[0].shape[0]
    tokens, width = operands[2].shape
    return call(
        weight_kernel,
        (shape_of(rows // 2, width, dtype=F32), shape_of(rows // 2, width)),
        [VMEM] * 6 + [ANY] * 2,
        "weight_terms",
    )(*operands)


def halve_kernel(keep, arrived, after, next_keep, next_out):
    rows = next_keep.shape[0]
    next_out[...] = (keep[rows:, :] + arrived[rows:, :].astype(F32)).astype(BF16)
    next_keep[...] = keep[:rows, :] + arrived[:rows, :].astype(F32)


def halve(keep, arrived, after):
    rows, width = keep.shape[0] // 2, keep.shape[1]
    return call(
        halve_kernel,
        (shape_of(rows, width, dtype=F32), shape_of(rows, width)),
        [VMEM, VMEM, ANY],
        "halve_weight_sum",
    )(keep, arrived, after)


def query_kernel(who, att_own, att_back, dq_own, dq_back, w, out, dq, att):
    mine = who[0] & 1
    for j in range(att_own.shape[1] // HD):
        cols = slice(j * HD, (j + 1) * HD)
        att[:, head_cols(j, mine)] = att_own[:, cols]
        att[:, head_cols(j, 1 - mine)] = att_back[:, cols]
        dq[:, head_cols(j, mine)] = dq_own[:, cols]
        dq[:, head_cols(j, 1 - mine)] = dq_back[:, cols]
    out[...] = dot(att[...], w[...], 1, 0).astype(BF16)


def finish_queries(who, att_own, att_back, dq_own, dq_back, w):
    tokens = att_own.shape[0]
    return call(
        query_kernel,
        (shape_of(tokens, w.shape[1]), shape_of(tokens, w.shape[0])),
        [SMEM] + [VMEM] * 5,
        "finish_queries",
        scratch=[pltpu.VMEM((tokens, w.shape[0]), BF16)],
    )(who, att_own, att_back, dq_own, dq_back, w)


def returned_kernel(who, d_par, far_a, far_b, total):
    slot = far_slot(who[0])
    returned = jnp.where(slot == 0, far_b[...].astype(F32), far_a[...].astype(F32))
    total[...] = (d_par[...].astype(F32) + returned).astype(BF16)


def add_returned(who, d_par, far):
    return call(
        returned_kernel, (shape_of(*d_par.shape),), [SMEM] + [VMEM] * 3, "add_returned"
    )(who, d_par, *far)[0]


def key_kernel(who, own, far_a, far_b, home, keep, out, dk, dv, total):
    mine = who[0] & 1
    slot = far_slot(who[0])
    tokens = dk.shape[0]
    for i, target in ((0, dk), (1, dv)):
        rows = slice(i * tokens, (i + 1) * tokens)
        for j in range(own.shape[1] // HD):
            cols = slice(j * HD, (j + 1) * HD)
            far = jnp.where(slot == 0, far_a[rows, cols].astype(F32), far_b[rows, cols].astype(F32))
            target[:, head_cols(j, mine)] = (own[rows, cols].astype(F32) + far).astype(BF16)
            target[:, head_cols(j, 1 - mine)] = home[rows, cols]
    total[...] = keep[...] + out[...].astype(F32)


def finish_keys(who, own, far, home, keep, out):
    tokens, half = own.shape[0] // 2, own.shape[1]
    return call(
        key_kernel,
        (shape_of(tokens, 2 * half),) * 2 + (shape_of(*keep.shape, dtype=F32),),
        [SMEM] + [VMEM] * 6,
        "finish_keys",
    )(who, own, *far, home, keep, out)


def on_device(queries, key_states, values, w_out, cotangent, neighbours, counts):
    n_seq, n_dp = lax.axis_size("seq"), lax.axis_size("dp")
    me, my_dp = lax.axis_index("seq").astype(jnp.int32), lax.axis_index("dp").astype(jnp.int32)
    who = jnp.stack([me, my_dp])
    cot = cotangent[0]

    swap = [(i, i ^ 1) for i in range(n_seq)]
    relay = [(i, i + 2) for i in range(0, n_seq, 2) if i + 2 < n_seq]
    relay += [(i, i - 2) for i in range(1, n_seq, 2) if i - 2 >= 0]
    outer = [(b, a) for a, b in relay]
    edges = [[], []]
    for i in range(n_seq):
        edges[1].append((i, i ^ 2))
        other = i + 2 if (i >> 1) & 1 else i - 2
        if 0 <= other < n_seq:
            edges[0].append((i, other))
    send = lambda x, pairs: lax.ppermute(x, "seq", pairs)
    across = lambda x, k: lax.ppermute(x, "dp", [(i, i ^ k) for i in range(n_dp)])

    kv_send, own, q_send, q_own = pack(
        who, neighbours[0], queries[0], key_states[0], values[0]
    )
    par = send(kv_send, swap)
    q_par = send(q_send, swap)
    far_par = send(own, outer)
    cot_par = send(cot, swap)
    far_own = send(par, relay)
    core_own, core_par = across(cot, 1), across(cot_par, 1)
    ga = grad_attended(who, cot, cot_par, w_out)

    inputs = (q_own, q_par, own, par, far_own, far_par)
    probs, att_own, att_back, att_t, step = forward(
        who, neighbours[0], inputs, ga, n_seq, n_dp
    )
    att_core = across(att_t[1], 1)
    att_back = send(att_back, swap)
    grads, *leaving = backward(who, inputs, ga, probs)
    far = [send(leaving[i], edges[i]) for i in range(2)]
    keep, out = weight_terms(att_t[0], att_core, cot, cot_par, core_own, core_par, leaving[0], att_back)
    dq_own, dq_back, d_own, d_par = gradients(inputs, ga, probs, grads)
    dq_back = send(dq_back, swap)
    home = send(add_returned(who, d_par, far), swap)

    hops = []
    bit = 2
    while bit < n_dp:
        hops.append(("dp", n_dp, bit))
        bit *= 2
    while step < n_seq:
        hops.append(("seq", n_seq, step))
        step *= 2
    for place, (axis, count, bit) in enumerate(hops):
        out = lax.ppermute(out, axis, [(i, i ^ bit) for i in range(count)])
        if place + 1 < len(hops):
            keep, out = halve(keep, out, dq_back)

    output, dq = finish_queries(who, att_own, att_back, dq_own, dq_back, w_out)
    dk, dv, total = finish_keys(who, d_own, far, home, keep, out)
    return (output[None], dq[None], dk[None], dv[None], total)


def solution(mesh):
    placed = (
        P("dp", "seq", None),
        P("dp", "seq", None),
        P("dp", "seq", None),
        P(),
        P("dp", "seq", None),
        P("dp", "seq", None),
        P("dp", "seq"),
    )
    return jax.shard_map(
        on_device,
        mesh=mesh,
        in_specs=placed,
        out_specs=(
            P("dp", "seq", None),
            P("dp", "seq", None),
            P("dp", "seq", None),
            P("dp", "seq", None),
            P(("seq", "dp"), None),
        ),
        check_vma=False,
    )
```

```python
import functools
import math

import jax
import jax.numpy as jnp
from jax import lax
from jax.experimental import pallas as pl
from jax.experimental.pallas import tpu as pltpu
from jax.sharding import PartitionSpec as P

HD = 128
VMEM_LIMIT = 12 * 1024 * 1024
F32 = jnp.float32
BF16 = jnp.bfloat16
VMEM = pl.BlockSpec(memory_space=pltpu.VMEM)
SMEM = pl.BlockSpec(memory_space=pltpu.SMEM)
HBM = pl.BlockSpec(memory_space=pltpu.HBM)
ANY = pl.BlockSpec(memory_space=pl.ANY)
FLAG_ROWS = 16


def dot(a, b, ca, cb):
    return lax.dot_general(a, b, (((ca,), (cb,)), ((), ())), preferred_element_type=F32)


def bit_reversed(index, bits):
    out = 0
    for b in range(bits):
        out = out * 2 + ((index >> b) & 1)
    return out


def shape_of(*dims, dtype=BF16):
    return jax.ShapeDtypeStruct(dims, dtype)


def call(body, out_shape, in_specs, name, scratch=(), moved=0):
    return pl.pallas_call(
        body,
        out_shape=out_shape,
        in_specs=in_specs,
        out_specs=(VMEM,) * len(out_shape),
        scratch_shapes=list(scratch),
        compiler_params=pltpu.CompilerParams(vmem_limit_bytes=VMEM_LIMIT),
        cost_estimate=pl.CostEstimate(flops=0, bytes_accessed=moved, transcendentals=0),
        name=name,
    )


def head_cols(pair, parity):
    return pl.ds(pl.multiple_of((2 * pair + parity) * HD, HD), HD)


def listed_flags(me, listed):
    far_patch = jnp.where(me % 2 == 0, me - 1, me + 1)
    near, far = jnp.int32(0), jnp.int32(0)
    for slot in range(listed.shape[1]):
        near = jnp.where(listed[0, slot] == (me ^ 1), 1, near)
        far = jnp.where(listed[0, slot] == far_patch, 1, far)
    return near, far


def in_hbm(x):
    return pltpu.with_memory_space_constraint(x, pltpu.HBM)


def pack_kernel(who, listed, q, k, v, kv_send, kv_keep, q_send, q_keep, listed_in, sems):
    mine = who[0] & 1
    tokens, half = q_keep.shape
    copies = []

    def copy(source, target):
        copies.append(pltpu.make_async_copy(source, target, sems.at[len(copies)]))
        copies[-1].start()

    copy(listed, listed_in)
    for kv, q_to, parity in ((kv_send, q_send, 1 - mine), (kv_keep, q_keep, mine)):
        for source, target, row in ((k, kv, 0), (v, kv, tokens), (q, q_to, 0)):
            for j in range(half // HD):
                copy(
                    source.at[:, head_cols(j, parity)],
                    target.at[row : row + tokens, j * HD : (j + 1) * HD],
                )
    copies[0].wait()
    near, far = listed_flags(who[0], listed_in)
    left = lax.broadcasted_iota(jnp.int32, (FLAG_ROWS, half), 1) < half // 2
    q_send[tokens : tokens + FLAG_ROWS, :] = jnp.where(left, near, far).astype(F32).astype(BF16)
    for item in copies[1:]:
        item.wait()


def pack(who, listed, q, k, v):
    tokens, features = k.shape
    half = features // 2
    kv = shape_of(2 * tokens, half)
    return call(
        pack_kernel,
        (kv, kv, shape_of(tokens + FLAG_ROWS, half), shape_of(tokens, half)),
        [SMEM] + [HBM] * 4,
        "pack_heads",
        scratch=[
            pltpu.SMEM(listed.shape, jnp.int32),
            pltpu.SemaphoreType.DMA((3 * features // HD + 1,)),
        ],
    )(who, *[in_hbm(x) for x in (listed, q, k, v)])


def turn_kernel(who, cot, cot_par, w, ga, cot_in, w_in, sems):
    tokens = cot.shape[0]
    pairs = ga.shape[1] // HD
    copies = [pltpu.make_async_copy(cot, cot_in, sems.at[pairs])]
    for j in range(pairs):
        rows = w.at[head_cols(j, who[0] & 1), :]
        copies.append(pltpu.make_async_copy(rows, w_in.at[j], sems.at[j]))
    for item in copies:
        item.start()
    copies[0].wait()
    for j in range(pairs):
        cols = slice(j * HD, (j + 1) * HD)
        copies[j + 1].wait()
        ga[:tokens, cols] = dot(cot_in[...], w_in[j], 1, 1).astype(BF16)
        ga[tokens:, cols] = dot(cot_par[...], w_in[j], 1, 1).astype(BF16)


def grad_attended(who, cot, cot_par, w):
    tokens, width = cot.shape
    pairs = w.shape[0] // (2 * HD)
    return call(
        turn_kernel,
        (shape_of(2 * tokens, pairs * HD),),
        [SMEM, HBM, VMEM, HBM],
        "grad_attended",
        scratch=[
            pltpu.VMEM((tokens, width), BF16),
            pltpu.VMEM((pairs, HD, width), BF16),
            pltpu.SemaphoreType.DMA((pairs + 1,)),
        ],
    )(who, in_hbm(cot), cot_par, in_hbm(w))[0]


def far_slot(me):
    return (me & 1) ^ ((me >> 1) & 1)


def forward_kernel(
    direct, n_dp, who, listed, q_own, q_par, own, par, far_own, far_par, after,
    probs, att_own, att_back, att_t,
):
    rate = math.log2(math.e) / math.sqrt(HD)
    tokens, half = q_own.shape
    pairs = half // HD
    me = who[0]
    near_flag, far_flag = listed_flags(me, listed)
    barred = lambda x: jnp.where(x > 0, 0.0, -jnp.inf)
    theirs = q_par[tokens : tokens + FLAG_ROWS, :].astype(F32)[:1]
    left = lax.broadcasted_iota(jnp.int32, (1, 2 * tokens), 1) < tokens
    near_par = barred(jnp.broadcast_to(theirs[:, :1], (1, 2 * tokens)))
    far_par_bias = barred(jnp.broadcast_to(theirs[:, half - 1 :], (1, 2 * tokens)))
    bias = (
        jnp.where(left, 0.0, near_par),
        jnp.where(left, barred(near_flag), 0.0),
        jnp.where(left, barred(far_flag), far_par_bias),
    )
    for j in range(pairs):
        cols = slice(j * HD, (j + 1) * HD)
        qo, qp = q_own[:, cols], q_par[:tokens, cols]
        q = jnp.concatenate([qo, qp], axis=0)
        k = jnp.concatenate([own[:tokens, cols], par[:tokens, cols]], axis=0)
        v = jnp.concatenate([own[tokens:, cols], par[tokens:, cols]], axis=0)
        near = dot(k, q, 1, 1)
        far = jnp.concatenate(
            [dot(far_own[:tokens, cols], qo, 1, 1), dot(far_par[:tokens, cols], qp, 1, 1)], axis=1
        )
        s = [near[:tokens] + bias[0], near[tokens:] + bias[1], far + bias[2]]
        top = jnp.max(jnp.maximum(jnp.maximum(s[0], s[1]), s[2]), axis=0, keepdims=True)
        e = [jnp.exp2((x - top) * rate) for x in s]
        inv = 1.0 / jnp.sum(e[0] + e[1] + e[2], axis=0, keepdims=True)
        low = [(x * inv).astype(BF16) for x in e]
        for i in range(3):
            probs[j, i * tokens : (i + 1) * tokens, :] = low[i]
        vfo, vfp = far_own[tokens:, cols], far_par[tokens:, cols]
        o_t = dot(v, jnp.concatenate(low[:2], axis=0), 0, 0)
        o_t += jnp.concatenate(
            [dot(vfo, low[2][:, :tokens], 0, 0), dot(vfp, low[2][:, tokens:], 0, 0)], axis=1
        )
        o = o_t.T.astype(BF16)
        att_own[:, cols] = o[:tokens]
        att_back[:, cols] = o[tokens:]
        o_low = o_t.astype(BF16)
        if direct:
            rows = HD // n_dp
            place = bit_reversed(j ^ (me >> 1), (pairs - 1).bit_length())
            for d in range(n_dp):
                block = bit_reversed((d ^ who[1]) >> 1, (n_dp // 2 - 1).bit_length())
                start = pl.multiple_of((block * pairs + place) * rows, rows)
                att_t[(d ^ who[1]) & 1, pl.ds(start, rows), :] = o_low[d * rows : (d + 1) * rows, :]
        else:
            att_t[cols, :] = o_low


def forward(who, listed, inputs, after, n_seq, n_dp):
    tokens, half = inputs[0].shape
    features = 2 * half
    heads, pairs = features // HD, half // HD
    direct = n_seq == heads and HD % n_dp == 0 and (HD // n_dp) % 16 == 0
    one = shape_of(tokens, half)
    turned = shape_of(2, half // 2, 2 * tokens) if direct else shape_of(half, 2 * tokens)
    probs, att_own, att_back, turned = call(
        functools.partial(forward_kernel, direct, n_dp),
        (shape_of(pairs, 3 * tokens, 2 * tokens), one, one, turned),
        [SMEM] * 2 + [VMEM] * 6 + [ANY],
        "patch_forward",
    )(who, listed, *inputs, after)
    if not direct:
        here = who[0]
        bits, d_bits = (n_seq - 1).bit_length(), (n_dp // 2 - 1).bit_length()
        order = jnp.array([bit_reversed(i, bits) for i in range(n_seq)], jnp.int32) ^ here
        d_order = [bit_reversed(i, d_bits) * 2 + c for c in range(2) for i in range(n_dp // 2)]
        full = jnp.zeros((heads // 2, 2, HD, 2 * tokens), BF16)
        full = lax.dynamic_update_slice(
            full, turned.reshape(heads // 2, 1, HD, 2 * tokens), (0, here & 1, 0, 0)
        )
        full = full.reshape(n_seq, n_dp, features // (n_seq * n_dp), 2 * tokens)
        full = jnp.take(full, order, axis=0)
        full = jnp.take(full, jnp.array(d_order, jnp.int32) ^ who[1], axis=1).transpose(1, 0, 2, 3)
        turned = full.reshape(2, features // 2, 2 * tokens)
    return probs, att_own, att_back, turned, 2 if direct else 1


def backward_kernel(
    who, q_own, q_par, own, par, far_own, far_par, ga, probs, _after, _also, grads, edge_a, edge_b
):
    scale = 1.0 / math.sqrt(HD)
    tokens, half = q_own.shape
    slot = far_slot(who[0])
    last = slice(2 * tokens, 3 * tokens)
    for j in range(half // HD):
        cols = slice(j * HD, (j + 1) * HD)
        g_both = ga[:, cols]
        go, gp = g_both[:tokens], g_both[tokens:]
        qo, qp = q_own[:, cols], q_par[:tokens, cols]
        v = jnp.concatenate([own[tokens:, cols], par[tokens:, cols]], axis=0)
        vfo, vfp = far_own[tokens:, cols], far_par[tokens:, cols]
        gn = dot(v, g_both, 1, 1)
        g = [
            gn[:tokens],
            gn[tokens:],
            jnp.concatenate([dot(vfo, go, 1, 1), dot(vfp, gp, 1, 1)], axis=1),
        ]
        p = [probs[j, i * tokens : (i + 1) * tokens, :].astype(F32) for i in range(3)]
        delta = jnp.sum(p[0] * g[0] + p[1] * g[1] + p[2] * g[2], axis=0, keepdims=True)
        ds = [(p[i] * (g[i] - delta)).astype(BF16) for i in range(3)]
        for i in range(3):
            grads[j, i * tokens : (i + 1) * tokens, :] = ds[i]
        dfo, dfp = ds[2][:, :tokens], ds[2][:, tokens:]
        own_far = jnp.concatenate(
            [dot(dfo, qo, 1, 0) * scale, dot(probs[j, last, :tokens], go, 1, 0)], axis=0
        ).astype(BF16)
        par_far = jnp.concatenate(
            [dot(dfp, qp, 1, 0) * scale, dot(probs[j, last, tokens:], gp, 1, 0)], axis=0
        ).astype(BF16)
        edge_a[:, cols] = jnp.where(slot == 0, own_far, par_far)
        edge_b[:, cols] = jnp.where(slot == 0, par_far, own_far)


def backward(who, inputs, ga, probs, *after):
    tokens, half = inputs[0].shape
    return call(
        backward_kernel,
        (shape_of(*probs.shape),) + (shape_of(2 * tokens, half),) * 2,
        [SMEM] + [VMEM] * 8 + [ANY] * 2,
        "patch_backward",
    )(who, *inputs, ga, probs, *after)


def gradient_kernel(
    q_own, q_par, own, par, far_own, far_par, ga, probs, grads, _after, dq_own, dq_back, d_own, d_par
):
    scale = 1.0 / math.sqrt(HD)
    tokens, half = q_own.shape
    near, last = slice(0, 2 * tokens), slice(2 * tokens, 3 * tokens)
    for j in range(half // HD):
        cols = slice(j * HD, (j + 1) * HD)
        q = jnp.concatenate([q_own[:, cols], q_par[:tokens, cols]], axis=0)
        k = jnp.concatenate([own[:tokens, cols], par[:tokens, cols]], axis=0)
        kfo, kfp = far_own[:tokens, cols], far_par[:tokens, cols]
        low, dsn = probs[j, near, :], grads[j, near, :]
        dfo, dfp = grads[j, last, :tokens], grads[j, last, tokens:]
        dq = dot(dsn, k, 0, 0) + jnp.concatenate([dot(dfo, kfo, 0, 0), dot(dfp, kfp, 0, 0)], axis=0)
        dq = (dq * scale).astype(BF16)
        dq_own[:, cols] = dq[:tokens]
        dq_back[:, cols] = dq[tokens:]
        dk = (dot(dsn, q, 1, 0) * scale).astype(BF16)
        dv = dot(low, ga[:, cols], 1, 0).astype(BF16)
        d_own[:tokens, cols] = dk[:tokens]
        d_par[:tokens, cols] = dk[tokens:]
        d_own[tokens:, cols] = dv[:tokens]
        d_par[tokens:, cols] = dv[tokens:]


def gradients(inputs, ga, probs, grads, after):
    tokens, half = inputs[0].shape
    one, kv = shape_of(tokens, half), shape_of(2 * tokens, half)
    return call(
        gradient_kernel, (one, one, kv, kv), [VMEM] * 9 + [ANY], "patch_gradients"
    )(*inputs, ga, probs, grads, after)


def weight_kernel(att_keep, att_core, own, par, core_own, core_par, keep, send):
    size = keep.shape[0]
    tokens = own.shape[0]
    for target, start in ((send, size), (keep, 0)):
        rows = slice(start, start + size)
        total = dot(att_keep[rows, :tokens], own[...], 1, 0)
        total += dot(att_keep[rows, tokens:], par[...], 1, 0)
        total += dot(att_core[rows, :tokens], core_own[...], 1, 0)
        total += dot(att_core[rows, tokens:], core_par[...], 1, 0)
        target[...] = total.astype(target.dtype)


def weight_terms(*operands):
    rows = operands[0].shape[0]
    tokens, width = operands[2].shape
    return call(
        weight_kernel,
        (shape_of(rows // 2, width, dtype=F32), shape_of(rows // 2, width)),
        [VMEM] * 6,
        "weight_terms",
    )(*operands)


def halve_kernel(keep, arrived, next_keep, next_out):
    rows = next_keep.shape[0]
    next_out[...] = (keep[rows:, :] + arrived[rows:, :].astype(F32)).astype(BF16)
    next_keep[...] = keep[:rows, :] + arrived[:rows, :].astype(F32)


def halve(keep, arrived):
    rows, width = keep.shape[0] // 2, keep.shape[1]
    return call(
        halve_kernel,
        (shape_of(rows, width, dtype=F32), shape_of(rows, width)),
        [VMEM, VMEM],
        "halve_weight_sum",
        moved=18 * rows * width,
    )(keep, arrived)


def query_kernel(who, att_own, att_back, dq_own, dq_back, w, out, dq, att):
    mine = who[0] & 1
    for j in range(att_own.shape[1] // HD):
        cols = slice(j * HD, (j + 1) * HD)
        att[:, head_cols(j, mine)] = att_own[:, cols]
        att[:, head_cols(j, 1 - mine)] = att_back[:, cols]
        dq[:, head_cols(j, mine)] = dq_own[:, cols]
        dq[:, head_cols(j, 1 - mine)] = dq_back[:, cols]
    out[...] = dot(att[...], w[...], 1, 0).astype(BF16)


def finish_queries(who, att_own, att_back, dq_own, dq_back, w):
    tokens = att_own.shape[0]
    return call(
        query_kernel,
        (shape_of(tokens, w.shape[1]), shape_of(tokens, w.shape[0])),
        [SMEM] + [VMEM] * 5,
        "finish_queries",
        scratch=[pltpu.VMEM((tokens, w.shape[0]), BF16)],
    )(who, att_own, att_back, dq_own, dq_back, w)


def returned_kernel(who, d_par, far_a, far_b, _after, _also, total):
    slot = far_slot(who[0])
    returned = jnp.where(slot == 0, far_b[...].astype(F32), far_a[...].astype(F32))
    total[...] = (d_par[...].astype(F32) + returned).astype(BF16)


def add_returned(who, d_par, far, *after):
    return call(
        returned_kernel, (shape_of(*d_par.shape),), [SMEM] + [VMEM] * 3 + [ANY] * 2, "add_returned"
    )(who, d_par, *far, *after)[0]


def key_kernel(who, own, far_a, far_b, home, keep, out, dk, dv, total):
    mine = who[0] & 1
    slot = far_slot(who[0])
    tokens = dk.shape[0]
    for i, target in ((0, dk), (1, dv)):
        rows = slice(i * tokens, (i + 1) * tokens)
        for j in range(own.shape[1] // HD):
            cols = slice(j * HD, (j + 1) * HD)
            far = jnp.where(slot == 0, far_a[rows, cols].astype(F32), far_b[rows, cols].astype(F32))
            target[:, head_cols(j, mine)] = (own[rows, cols].astype(F32) + far).astype(BF16)
            target[:, head_cols(j, 1 - mine)] = home[rows, cols]
    total[...] = keep[...] + out[...].astype(F32)


def finish_keys(who, own, far, home, keep, out):
    tokens, half = own.shape[0] // 2, own.shape[1]
    return call(
        key_kernel,
        (shape_of(tokens, 2 * half),) * 2 + (shape_of(*keep.shape, dtype=F32),),
        [SMEM] + [VMEM] * 6,
        "finish_keys",
    )(who, own, *far, home, keep, out)


def exchange(x, hop):
    axis, count, bit = hop
    return lax.ppermute(x, axis, [(i, i ^ bit) for i in range(count)])


def on_device(queries, key_states, values, w_out, cotangent, neighbours, counts):
    n_seq, n_dp = lax.axis_size("seq"), lax.axis_size("dp")
    me, my_dp = lax.axis_index("seq").astype(jnp.int32), lax.axis_index("dp").astype(jnp.int32)
    who = jnp.stack([me, my_dp])
    cot = cotangent[0]

    swap = [(i, i ^ 1) for i in range(n_seq)]
    relay = [(i, i + 2) for i in range(0, n_seq, 2) if i + 2 < n_seq]
    relay += [(i, i - 2) for i in range(1, n_seq, 2) if i - 2 >= 0]
    outer = [(b, a) for a, b in relay]
    edges = [[], []]
    for i in range(n_seq):
        edges[1].append((i, i ^ 2))
        other = i + 2 if (i >> 1) & 1 else i - 2
        if 0 <= other < n_seq:
            edges[0].append((i, other))
    send = lambda x, pairs: lax.ppermute(x, "seq", pairs)
    across = lambda x, k: lax.ppermute(x, "dp", [(i, i ^ k) for i in range(n_dp)])

    kv_send, own, q_send, q_own = pack(
        who, neighbours[0], queries[0], key_states[0], values[0]
    )
    par = send(kv_send, swap)
    q_par = send(q_send, swap)
    far_par = send(own, outer)
    cot_par = send(cot, swap)
    far_own = send(par, relay)
    core_own, core_par = across(cot, 1), across(cot_par, 1)
    ga = grad_attended(who, cot, cot_par, w_out)

    inputs = (q_own, q_par, own, par, far_own, far_par)
    probs, att_own, att_back, att_t, step = forward(
        who, neighbours[0], inputs, ga, n_seq, n_dp
    )
    att_core = across(att_t[1], 1)
    att_back = send(att_back, swap)
    keep, out = weight_terms(att_t[0], att_core, cot, cot_par, core_own, core_par)
    grads, *leaving = backward(who, inputs, ga, probs, keep, att_back)
    far = [send(leaving[i], edges[i]) for i in range(2)]
    hops = []
    bit = 2
    while bit < n_dp:
        hops.append(("dp", n_dp, bit))
        bit *= 2
    while step < n_seq:
        hops.append(("seq", n_seq, step))
        step *= 2
    arrived = exchange(out, hops[0])
    keep, out = halve(keep, arrived)
    dq_own, dq_back, d_own, d_par = gradients(inputs, ga, probs, grads, keep)
    dq_back = send(dq_back, swap)
    for hop in hops[1:-1]:
        keep, out = halve(keep, exchange(out, hop))
    home = send(add_returned(who, d_par, far, dq_back, keep), swap)
    arrived = exchange(out, hops[-1])

    output, dq = finish_queries(who, att_own, att_back, dq_own, dq_back, w_out)
    dk, dv, total = finish_keys(who, d_own, far, home, keep, arrived)
    return (output[None], dq[None], dk[None], dv[None], total)


def solution(mesh):
    placed = (
        P("dp", "seq", None),
        P("dp", "seq", None),
        P("dp", "seq", None),
        P(),
        P("dp", "seq", None),
        P("dp", "seq", None),
        P("dp", "seq"),
    )
    return jax.shard_map(
        on_device,
        mesh=mesh,
        in_specs=placed,
        out_specs=(
            P("dp", "seq", None),
            P("dp", "seq", None),
            P("dp", "seq", None),
            P("dp", "seq", None),
            P(("seq", "dp"), None),
        ),
        check_vma=False,
    )
```

```python
import functools
import math

import jax
import jax.numpy as jnp
from jax import lax
from jax.experimental import pallas as pl
from jax.experimental.pallas import tpu as pltpu
from jax.sharding import PartitionSpec as P

HD = 128
VMEM_LIMIT = 12 * 1024 * 1024
F32 = jnp.float32
BF16 = jnp.bfloat16
VMEM = pl.BlockSpec(memory_space=pltpu.VMEM)
SMEM = pl.BlockSpec(memory_space=pltpu.SMEM)
HBM = pl.BlockSpec(memory_space=pltpu.HBM)
ANY = pl.BlockSpec(memory_space=pl.ANY)
FLAG_ROWS = 16


def dot(a, b, ca, cb):
    return lax.dot_general(a, b, (((ca,), (cb,)), ((), ())), preferred_element_type=F32)


def bit_reversed(index, bits):
    out = 0
    for b in range(bits):
        out = out * 2 + ((index >> b) & 1)
    return out


def shape_of(*dims, dtype=BF16):
    return jax.ShapeDtypeStruct(dims, dtype)


def call(body, out_shape, in_specs, name, scratch=()):
    return pl.pallas_call(
        body,
        out_shape=out_shape,
        in_specs=in_specs,
        out_specs=(VMEM,) * len(out_shape),
        scratch_shapes=list(scratch),
        compiler_params=pltpu.CompilerParams(vmem_limit_bytes=VMEM_LIMIT),
        cost_estimate=pl.CostEstimate(flops=0, bytes_accessed=0, transcendentals=0),
        name=name,
    )


def head_cols(pair, parity):
    return pl.ds(pl.multiple_of((2 * pair + parity) * HD, HD), HD)


def listed_flags(me, listed):
    far_patch = jnp.where(me % 2 == 0, me - 1, me + 1)
    near, far = jnp.int32(0), jnp.int32(0)
    for slot in range(listed.shape[1]):
        near = jnp.where(listed[0, slot] == (me ^ 1), 1, near)
        far = jnp.where(listed[0, slot] == far_patch, 1, far)
    return near, far


def in_hbm(x):
    return pltpu.with_memory_space_constraint(x, pltpu.HBM)


def pack_kernel(who, listed, q, k, v, kv_send, kv_keep, q_send, q_keep, listed_in, sems):
    mine = who[0] & 1
    tokens, half = q_keep.shape
    copies = []

    def copy(source, target):
        copies.append(pltpu.make_async_copy(source, target, sems.at[len(copies)]))
        copies[-1].start()

    copy(listed, listed_in)
    for kv, q_to, parity in ((kv_send, q_send, 1 - mine), (kv_keep, q_keep, mine)):
        for source, target, row in ((k, kv, 0), (v, kv, tokens), (q, q_to, 0)):
            for j in range(half // HD):
                copy(
                    source.at[:, head_cols(j, parity)],
                    target.at[row : row + tokens, j * HD : (j + 1) * HD],
                )
    copies[0].wait()
    near, far = listed_flags(who[0], listed_in)
    left = lax.broadcasted_iota(jnp.int32, (FLAG_ROWS, half), 1) < half // 2
    q_send[tokens : tokens + FLAG_ROWS, :] = jnp.where(left, near, far).astype(F32).astype(BF16)
    for item in copies[1:]:
        item.wait()


def pack(who, listed, q, k, v):
    tokens, features = k.shape
    half = features // 2
    kv = shape_of(2 * tokens, half)
    return call(
        pack_kernel,
        (kv, kv, shape_of(tokens + FLAG_ROWS, half), shape_of(tokens, half)),
        [SMEM] + [HBM] * 4,
        "pack_heads",
        scratch=[
            pltpu.SMEM(listed.shape, jnp.int32),
            pltpu.SemaphoreType.DMA((3 * features // HD + 1,)),
        ],
    )(who, *[in_hbm(x) for x in (listed, q, k, v)])


def turn_kernel(who, cot, cot_par, w, ga, cot_in, w_in, sems):
    tokens = cot.shape[0]
    pairs = ga.shape[1] // HD
    copies = [pltpu.make_async_copy(cot, cot_in, sems.at[pairs])]
    for j in range(pairs):
        rows = w.at[head_cols(j, who[0] & 1), :]
        copies.append(pltpu.make_async_copy(rows, w_in.at[j], sems.at[j]))
    for item in copies:
        item.start()
    copies[0].wait()
    for j in range(pairs):
        cols = slice(j * HD, (j + 1) * HD)
        copies[j + 1].wait()
        ga[:tokens, cols] = dot(cot_in[...], w_in[j], 1, 1).astype(BF16)
        ga[tokens:, cols] = dot(cot_par[...], w_in[j], 1, 1).astype(BF16)


def grad_attended(who, cot, cot_par, w):
    tokens, width = cot.shape
    pairs = w.shape[0] // (2 * HD)
    return call(
        turn_kernel,
        (shape_of(2 * tokens, pairs * HD),),
        [SMEM, HBM, VMEM, HBM],
        "grad_attended",
        scratch=[
            pltpu.VMEM((tokens, width), BF16),
            pltpu.VMEM((pairs, HD, width), BF16),
            pltpu.SemaphoreType.DMA((pairs + 1,)),
        ],
    )(who, in_hbm(cot), cot_par, in_hbm(w))[0]


def far_slot(me):
    return (me & 1) ^ ((me >> 1) & 1)


def forward_kernel(
    direct, n_dp, who, listed, q_own, q_par, own, par, far_own, far_par, after,
    probs, att_own, att_back, att_t,
):
    rate = math.log2(math.e) / math.sqrt(HD)
    tokens, half = q_own.shape
    pairs = half // HD
    me = who[0]
    near_flag, far_flag = listed_flags(me, listed)
    barred = lambda x: jnp.where(x > 0, 0.0, -jnp.inf)
    theirs = q_par[tokens : tokens + FLAG_ROWS, :].astype(F32)[:1]
    left = lax.broadcasted_iota(jnp.int32, (1, 2 * tokens), 1) < tokens
    near_par = barred(jnp.broadcast_to(theirs[:, :1], (1, 2 * tokens)))
    far_par_bias = barred(jnp.broadcast_to(theirs[:, half - 1 :], (1, 2 * tokens)))
    bias = (
        jnp.where(left, 0.0, near_par),
        jnp.where(left, barred(near_flag), 0.0),
        jnp.where(left, barred(far_flag), far_par_bias),
    )
    for j in range(pairs):
        cols = slice(j * HD, (j + 1) * HD)
        qo, qp = q_own[:, cols], q_par[:tokens, cols]
        q = jnp.concatenate([qo, qp], axis=0)
        k = jnp.concatenate([own[:tokens, cols], par[:tokens, cols]], axis=0)
        v = jnp.concatenate([own[tokens:, cols], par[tokens:, cols]], axis=0)
        near = dot(k, q, 1, 1)
        far = jnp.concatenate(
            [dot(far_own[:tokens, cols], qo, 1, 1), dot(far_par[:tokens, cols], qp, 1, 1)], axis=1
        )
        s = [near[:tokens] + bias[0], near[tokens:] + bias[1], far + bias[2]]
        top = jnp.max(jnp.maximum(jnp.maximum(s[0], s[1]), s[2]), axis=0, keepdims=True)
        e = [jnp.exp2((x - top) * rate) for x in s]
        inv = 1.0 / jnp.sum(e[0] + e[1] + e[2], axis=0, keepdims=True)
        low = [(x * inv).astype(BF16) for x in e]
        for i in range(3):
            probs[j, i * tokens : (i + 1) * tokens, :] = low[i]
        vfo, vfp = far_own[tokens:, cols], far_par[tokens:, cols]
        o_t = dot(v, jnp.concatenate(low[:2], axis=0), 0, 0)
        o_t += jnp.concatenate(
            [dot(vfo, low[2][:, :tokens], 0, 0), dot(vfp, low[2][:, tokens:], 0, 0)], axis=1
        )
        o = o_t.T.astype(BF16)
        att_own[:, cols] = o[:tokens]
        att_back[:, cols] = o[tokens:]
        o_low = o_t.astype(BF16)
        if direct:
            rows = HD // n_dp
            place = bit_reversed(j ^ (me >> 1), (pairs - 1).bit_length())
            for d in range(n_dp):
                block = bit_reversed((d ^ who[1]) >> 1, (n_dp // 2 - 1).bit_length())
                start = pl.multiple_of((block * pairs + place) * rows, rows)
                att_t[(d ^ who[1]) & 1, pl.ds(start, rows), :] = o_low[d * rows : (d + 1) * rows, :]
        else:
            att_t[cols, :] = o_low


def forward(who, listed, inputs, after, n_seq, n_dp):
    tokens, half = inputs[0].shape
    features = 2 * half
    heads, pairs = features // HD, half // HD
    direct = n_seq == heads and HD % n_dp == 0 and (HD // n_dp) % 16 == 0
    one = shape_of(tokens, half)
    turned = shape_of(2, half // 2, 2 * tokens) if direct else shape_of(half, 2 * tokens)
    probs, att_own, att_back, turned = call(
        functools.partial(forward_kernel, direct, n_dp),
        (shape_of(pairs, 3 * tokens, 2 * tokens), one, one, turned),
        [SMEM] * 2 + [VMEM] * 6 + [ANY],
        "patch_forward",
    )(who, listed, *inputs, after)
    if not direct:
        here = who[0]
        bits, d_bits = (n_seq - 1).bit_length(), (n_dp // 2 - 1).bit_length()
        order = jnp.array([bit_reversed(i, bits) for i in range(n_seq)], jnp.int32) ^ here
        d_order = [bit_reversed(i, d_bits) * 2 + c for c in range(2) for i in range(n_dp // 2)]
        full = jnp.zeros((heads // 2, 2, HD, 2 * tokens), BF16)
        full = lax.dynamic_update_slice(
            full, turned.reshape(heads // 2, 1, HD, 2 * tokens), (0, here & 1, 0, 0)
        )
        full = full.reshape(n_seq, n_dp, features // (n_seq * n_dp), 2 * tokens)
        full = jnp.take(full, order, axis=0)
        full = jnp.take(full, jnp.array(d_order, jnp.int32) ^ who[1], axis=1).transpose(1, 0, 2, 3)
        turned = full.reshape(2, features // 2, 2 * tokens)
    return probs, att_own, att_back, turned, 2 if direct else 1


def backward_kernel(
    who, q_own, q_par, own, par, far_own, far_par, ga, probs, _after, grads, edge_a, edge_b
):
    scale = 1.0 / math.sqrt(HD)
    tokens, half = q_own.shape
    slot = far_slot(who[0])
    last = slice(2 * tokens, 3 * tokens)
    for j in range(half // HD):
        cols = slice(j * HD, (j + 1) * HD)
        g_both = ga[:, cols]
        go, gp = g_both[:tokens], g_both[tokens:]
        qo, qp = q_own[:, cols], q_par[:tokens, cols]
        v = jnp.concatenate([own[tokens:, cols], par[tokens:, cols]], axis=0)
        vfo, vfp = far_own[tokens:, cols], far_par[tokens:, cols]
        gn = dot(v, g_both, 1, 1)
        g = [
            gn[:tokens],
            gn[tokens:],
            jnp.concatenate([dot(vfo, go, 1, 1), dot(vfp, gp, 1, 1)], axis=1),
        ]
        p = [probs[j, i * tokens : (i + 1) * tokens, :].astype(F32) for i in range(3)]
        delta = jnp.sum(p[0] * g[0] + p[1] * g[1] + p[2] * g[2], axis=0, keepdims=True)
        ds = [(p[i] * (g[i] - delta)).astype(BF16) for i in range(3)]
        for i in range(3):
            grads[j, i * tokens : (i + 1) * tokens, :] = ds[i]
        dfo, dfp = ds[2][:, :tokens], ds[2][:, tokens:]
        own_far = jnp.concatenate(
            [dot(dfo, qo, 1, 0) * scale, dot(probs[j, last, :tokens], go, 1, 0)], axis=0
        ).astype(BF16)
        par_far = jnp.concatenate(
            [dot(dfp, qp, 1, 0) * scale, dot(probs[j, last, tokens:], gp, 1, 0)], axis=0
        ).astype(BF16)
        edge_a[:, cols] = jnp.where(slot == 0, own_far, par_far)
        edge_b[:, cols] = jnp.where(slot == 0, par_far, own_far)


def backward(who, inputs, ga, probs, after):
    tokens, half = inputs[0].shape
    return call(
        backward_kernel,
        (shape_of(*probs.shape),) + (shape_of(2 * tokens, half),) * 2,
        [SMEM] + [VMEM] * 8 + [ANY],
        "patch_backward",
    )(who, *inputs, ga, probs, after)


def gradient_kernel(
    q_own, q_par, own, par, far_own, far_par, ga, probs, grads, dq_own, dq_back, d_own, d_par
):
    scale = 1.0 / math.sqrt(HD)
    tokens, half = q_own.shape
    near, last = slice(0, 2 * tokens), slice(2 * tokens, 3 * tokens)
    for j in range(half // HD):
        cols = slice(j * HD, (j + 1) * HD)
        q = jnp.concatenate([q_own[:, cols], q_par[:tokens, cols]], axis=0)
        k = jnp.concatenate([own[:tokens, cols], par[:tokens, cols]], axis=0)
        kfo, kfp = far_own[:tokens, cols], far_par[:tokens, cols]
        low, dsn = probs[j, near, :], grads[j, near, :]
        dfo, dfp = grads[j, last, :tokens], grads[j, last, tokens:]
        dq = dot(dsn, k, 0, 0) + jnp.concatenate([dot(dfo, kfo, 0, 0), dot(dfp, kfp, 0, 0)], axis=0)
        dq = (dq * scale).astype(BF16)
        dq_own[:, cols] = dq[:tokens]
        dq_back[:, cols] = dq[tokens:]
        dk = (dot(dsn, q, 1, 0) * scale).astype(BF16)
        dv = dot(low, ga[:, cols], 1, 0).astype(BF16)
        d_own[:tokens, cols] = dk[:tokens]
        d_par[:tokens, cols] = dk[tokens:]
        d_own[tokens:, cols] = dv[:tokens]
        d_par[tokens:, cols] = dv[tokens:]


def gradients(inputs, ga, probs, grads):
    tokens, half = inputs[0].shape
    one, kv = shape_of(tokens, half), shape_of(2 * tokens, half)
    return call(
        gradient_kernel, (one, one, kv, kv), [VMEM] * 9, "patch_gradients"
    )(*inputs, ga, probs, grads)


def weight_kernel(att_keep, att_core, own, par, core_own, core_par, keep, send):
    size = keep.shape[0]
    tokens = own.shape[0]
    for target, start in ((send, size), (keep, 0)):
        rows = slice(start, start + size)
        total = dot(att_keep[rows, :tokens], own[...], 1, 0)
        total += dot(att_keep[rows, tokens:], par[...], 1, 0)
        total += dot(att_core[rows, :tokens], core_own[...], 1, 0)
        total += dot(att_core[rows, tokens:], core_par[...], 1, 0)
        target[...] = total.astype(target.dtype)


def weight_terms(*operands):
    rows = operands[0].shape[0]
    tokens, width = operands[2].shape
    return call(
        weight_kernel,
        (shape_of(rows // 2, width, dtype=F32), shape_of(rows // 2, width)),
        [VMEM] * 6,
        "weight_terms",
    )(*operands)


def query_kernel(who, att_own, att_back, dq_own, dq_back, w, out, dq, att):
    mine = who[0] & 1
    for j in range(att_own.shape[1] // HD):
        cols = slice(j * HD, (j + 1) * HD)
        att[:, head_cols(j, mine)] = att_own[:, cols]
        att[:, head_cols(j, 1 - mine)] = att_back[:, cols]
        dq[:, head_cols(j, mine)] = dq_own[:, cols]
        dq[:, head_cols(j, 1 - mine)] = dq_back[:, cols]
    out[...] = dot(att[...], w[...], 1, 0).astype(BF16)


def finish_queries(who, att_own, att_back, dq_own, dq_back, w):
    tokens = att_own.shape[0]
    return call(
        query_kernel,
        (shape_of(tokens, w.shape[1]), shape_of(tokens, w.shape[0])),
        [SMEM] + [VMEM] * 5,
        "finish_queries",
        scratch=[pltpu.VMEM((tokens, w.shape[0]), BF16)],
    )(who, att_own, att_back, dq_own, dq_back, w)


def returned_kernel(who, d_par, far_a, far_b, total):
    slot = far_slot(who[0])
    returned = jnp.where(slot == 0, far_b[...].astype(F32), far_a[...].astype(F32))
    total[...] = (d_par[...].astype(F32) + returned).astype(BF16)


def add_returned(who, d_par, far):
    return call(
        returned_kernel, (shape_of(*d_par.shape),), [SMEM] + [VMEM] * 3, "add_returned"
    )(who, d_par, *far)[0]


def key_kernel(who, own, far_a, far_b, home, keep, out, dk, dv, total):
    mine = who[0] & 1
    slot = far_slot(who[0])
    tokens = dk.shape[0]
    for i, target in ((0, dk), (1, dv)):
        rows = slice(i * tokens, (i + 1) * tokens)
        for j in range(own.shape[1] // HD):
            cols = slice(j * HD, (j + 1) * HD)
            far = jnp.where(slot == 0, far_a[rows, cols].astype(F32), far_b[rows, cols].astype(F32))
            target[:, head_cols(j, mine)] = (own[rows, cols].astype(F32) + far).astype(BF16)
            target[:, head_cols(j, 1 - mine)] = home[rows, cols]
    total[...] = keep[...] + out[...].astype(F32)


def finish_keys(who, own, far, home, keep, out):
    tokens, half = own.shape[0] // 2, own.shape[1]
    return call(
        key_kernel,
        (shape_of(tokens, 2 * half),) * 2 + (shape_of(*keep.shape, dtype=F32),),
        [SMEM] + [VMEM] * 6,
        "finish_keys",
    )(who, own, *far, home, keep, out)


def on_device(queries, key_states, values, w_out, cotangent, neighbours, counts):
    n_seq, n_dp = lax.axis_size("seq"), lax.axis_size("dp")
    me, my_dp = lax.axis_index("seq").astype(jnp.int32), lax.axis_index("dp").astype(jnp.int32)
    who = jnp.stack([me, my_dp])
    cot = cotangent[0]

    swap = [(i, i ^ 1) for i in range(n_seq)]
    relay = [(i, i + 2) for i in range(0, n_seq, 2) if i + 2 < n_seq]
    relay += [(i, i - 2) for i in range(1, n_seq, 2) if i - 2 >= 0]
    outer = [(b, a) for a, b in relay]
    edges = [[], []]
    for i in range(n_seq):
        edges[1].append((i, i ^ 2))
        other = i + 2 if (i >> 1) & 1 else i - 2
        if 0 <= other < n_seq:
            edges[0].append((i, other))
    send = lambda x, pairs: lax.ppermute(x, "seq", pairs)
    across = lambda x, k: lax.ppermute(x, "dp", [(i, i ^ k) for i in range(n_dp)])

    kv_send, own, q_send, q_own = pack(
        who, neighbours[0], queries[0], key_states[0], values[0]
    )
    par = send(kv_send, swap)
    q_par = send(q_send, swap)
    far_par = send(own, outer)
    cot_par = send(cot, swap)
    far_own = send(par, relay)
    core_own, core_par = across(cot, 1), across(cot_par, 1)
    ga = grad_attended(who, cot, cot_par, w_out)

    inputs = (q_own, q_par, own, par, far_own, far_par)
    probs, att_own, att_back, att_t, step = forward(
        who, neighbours[0], inputs, ga, n_seq, n_dp
    )
    att_core = across(att_t[1], 1)
    att_back = send(att_back, swap)
    keep, out = weight_terms(att_t[0], att_core, cot, cot_par, core_own, core_par)
    grads, *leaving = backward(who, inputs, ga, probs, keep)
    far = [send(leaving[i], edges[i]) for i in range(2)]
    dq_own, dq_back, d_own, d_par = gradients(inputs, ga, probs, grads)
    dq_back = send(dq_back, swap)
    home = send(add_returned(who, d_par, far), swap)

    hops = []
    bit = 2
    while bit < n_dp:
        hops.append(("dp", n_dp, bit))
        bit *= 2
    while step < n_seq:
        hops.append(("seq", n_seq, step))
        step *= 2
    for place, (axis, count, bit) in enumerate(hops):
        out = lax.ppermute(out, axis, [(i, i ^ bit) for i in range(count)])
        if place + 1 < len(hops):
            total = keep + out.astype(F32)
            rows = total.shape[0] // 2
            keep, out = total[:rows], total[rows:].astype(BF16)

    output, dq = finish_queries(who, att_own, att_back, dq_own, dq_back, w_out)
    dk, dv, total = finish_keys(who, d_own, far, home, keep, out)
    return (output[None], dq[None], dk[None], dv[None], total)


def solution(mesh):
    placed = (
        P("dp", "seq", None),
        P("dp", "seq", None),
        P("dp", "seq", None),
        P(),
        P("dp", "seq", None),
        P("dp", "seq", None),
        P("dp", "seq"),
    )
    return jax.shard_map(
        on_device,
        mesh=mesh,
        in_specs=placed,
        out_specs=(
            P("dp", "seq", None),
            P("dp", "seq", None),
            P("dp", "seq", None),
            P("dp", "seq", None),
            P(("seq", "dp"), None),
        ),
        check_vma=False,
    )
```

```python
import functools
import math

import jax
import jax.numpy as jnp
from jax import lax
from jax.experimental import pallas as pl
from jax.experimental.pallas import tpu as pltpu
from jax.sharding import PartitionSpec as P

HD = 128
VMEM_LIMIT = 12 * 1024 * 1024
F32 = jnp.float32
BF16 = jnp.bfloat16
VMEM = pl.BlockSpec(memory_space=pltpu.VMEM)
HBM = pl.BlockSpec(memory_space=pltpu.HBM)
ANY = pl.BlockSpec(memory_space=pl.ANY)
FLAG_ROWS = 16


def dot(a, b, ca, cb):
    return lax.dot_general(a, b, (((ca,), (cb,)), ((), ())), preferred_element_type=F32)


def bit_reversed(index, bits):
    out = 0
    for b in range(bits):
        out = out * 2 + ((index >> b) & 1)
    return out


def shape_of(*dims, dtype=BF16):
    return jax.ShapeDtypeStruct(dims, dtype)


def call(body, out_shape, in_specs, name, scratch=()):
    return pl.pallas_call(
        body,
        out_shape=out_shape,
        in_specs=in_specs,
        out_specs=(VMEM,) * len(out_shape),
        scratch_shapes=list(scratch),
        compiler_params=pltpu.CompilerParams(vmem_limit_bytes=VMEM_LIMIT),
        cost_estimate=pl.CostEstimate(flops=0, bytes_accessed=0, transcendentals=0),
        name=name,
    )


def head_cols(pair, parity):
    return pl.ds(pl.multiple_of((2 * pair + parity) * HD, HD), HD)


def listed_flags(me, listed):
    far_patch = jnp.where(me % 2 == 0, me - 1, me + 1)
    near, far = jnp.int32(0), jnp.int32(0)
    for slot in range(listed.shape[1]):
        near = jnp.where(listed[0, slot] == (me ^ 1), 1, near)
        far = jnp.where(listed[0, slot] == far_patch, 1, far)
    return near, far


def in_hbm(x):
    return pltpu.with_memory_space_constraint(x, pltpu.HBM)


def pack_kernel(listed, q, k, v, kv_send, kv_keep, q_send, q_keep, listed_in, sems):
    mine = lax.axis_index("seq") & 1
    tokens, half = q_keep.shape[0] - FLAG_ROWS, q_keep.shape[1]
    copies = []

    def copy(source, target):
        copies.append(pltpu.make_async_copy(source, target, sems.at[len(copies)]))
        copies[-1].start()

    copy(listed, listed_in)
    for kv, q_to, parity in ((kv_send, q_send, 1 - mine), (kv_keep, q_keep, mine)):
        for source, target, row in ((k, kv, 0), (v, kv, tokens), (q, q_to, 0)):
            for j in range(half // HD):
                copy(
                    source.at[:, head_cols(j, parity)],
                    target.at[row : row + tokens, j * HD : (j + 1) * HD],
                )
    copies[0].wait()
    near, far = listed_flags(lax.axis_index("seq"), listed_in)
    left = lax.broadcasted_iota(jnp.int32, (FLAG_ROWS, half), 1) < half // 2
    flags = jnp.where(left, near, far).astype(F32).astype(BF16)
    q_send[tokens : tokens + FLAG_ROWS, :] = flags
    q_keep[tokens : tokens + FLAG_ROWS, :] = flags
    for item in copies[1:]:
        item.wait()


def pack(listed, q, k, v):
    tokens, features = k.shape
    half = features // 2
    kv = shape_of(2 * tokens, half)
    return call(
        pack_kernel,
        (kv, kv) + (shape_of(tokens + FLAG_ROWS, half),) * 2,
        [HBM] * 4,
        "pack_heads",
        scratch=[
            pltpu.SMEM(listed.shape, jnp.int32),
            pltpu.SemaphoreType.DMA((3 * features // HD + 1,)),
        ],
    )(*[in_hbm(x) for x in (listed, q, k, v)])


def turn_kernel(cot, cot_par, w, ga, cot_in, w_in, sems):
    tokens = cot.shape[0]
    pairs = ga.shape[1] // HD
    copies = [pltpu.make_async_copy(cot, cot_in, sems.at[pairs])]
    for j in range(pairs):
        rows = w.at[head_cols(j, lax.axis_index("seq") & 1), :]
        copies.append(pltpu.make_async_copy(rows, w_in.at[j], sems.at[j]))
    for item in copies:
        item.start()
    copies[0].wait()
    for j in range(pairs):
        cols = slice(j * HD, (j + 1) * HD)
        copies[j + 1].wait()
        ga[:tokens, cols] = dot(cot_in[...], w_in[j], 1, 1).astype(BF16)
        ga[tokens:, cols] = dot(cot_par[...], w_in[j], 1, 1).astype(BF16)


def grad_attended(cot, cot_par, w):
    tokens, width = cot.shape
    pairs = w.shape[0] // (2 * HD)
    return call(
        turn_kernel,
        (shape_of(2 * tokens, pairs * HD),),
        [HBM, VMEM, HBM],
        "grad_attended",
        scratch=[
            pltpu.VMEM((tokens, width), BF16),
            pltpu.VMEM((pairs, HD, width), BF16),
            pltpu.SemaphoreType.DMA((pairs + 1,)),
        ],
    )(in_hbm(cot), cot_par, in_hbm(w))[0]


def far_slot(me):
    return (me & 1) ^ ((me >> 1) & 1)


def forward_kernel(
    direct, n_dp, q_own, q_par, own, par, far_own, far_par, after,
    probs, att_own, att_back, att_t,
):
    rate = math.log2(math.e) / math.sqrt(HD)
    tokens, half = q_own.shape[0] - FLAG_ROWS, q_own.shape[1]
    pairs = half // HD
    me = lax.axis_index("seq")
    left = lax.broadcasted_iota(jnp.int32, (1, 2 * tokens), 1) < tokens

    def barred(x, place):
        flag = x[tokens : tokens + FLAG_ROWS, :].astype(F32)[:1, place : place + 1]
        return jnp.where(jnp.broadcast_to(flag, (1, 2 * tokens)) > 0, 0.0, -jnp.inf)

    bias = (
        jnp.where(left, 0.0, barred(q_par, 0)),
        jnp.where(left, barred(q_own, 0), 0.0),
        jnp.where(left, barred(q_own, half - 1), barred(q_par, half - 1)),
    )
    for j in range(pairs):
        cols = slice(j * HD, (j + 1) * HD)
        qo, qp = q_own[:tokens, cols], q_par[:tokens, cols]
        q = jnp.concatenate([qo, qp], axis=0)
        k = jnp.concatenate([own[:tokens, cols], par[:tokens, cols]], axis=0)
        v = jnp.concatenate([own[tokens:, cols], par[tokens:, cols]], axis=0)
        near = dot(k, q, 1, 1)
        far = jnp.concatenate(
            [dot(far_own[:tokens, cols], qo, 1, 1), dot(far_par[:tokens, cols], qp, 1, 1)], axis=1
        )
        s = [near[:tokens] + bias[0], near[tokens:] + bias[1], far + bias[2]]
        top = jnp.max(jnp.maximum(jnp.maximum(s[0], s[1]), s[2]), axis=0, keepdims=True)
        e = [jnp.exp2((x - top) * rate) for x in s]
        inv = 1.0 / jnp.sum(e[0] + e[1] + e[2], axis=0, keepdims=True)
        low = [(x * inv).astype(BF16) for x in e]
        for i in range(3):
            probs[j, i * tokens : (i + 1) * tokens, :] = low[i]
        vfo, vfp = far_own[tokens:, cols], far_par[tokens:, cols]
        o_t = dot(v, jnp.concatenate(low[:2], axis=0), 0, 0)
        o_t += jnp.concatenate(
            [dot(vfo, low[2][:, :tokens], 0, 0), dot(vfp, low[2][:, tokens:], 0, 0)], axis=1
        )
        o = o_t.T.astype(BF16)
        att_own[:, cols] = o[:tokens]
        att_back[:, cols] = o[tokens:]
        o_low = o_t.astype(BF16)
        if direct:
            rows = HD // n_dp
            place = bit_reversed(j ^ (me >> 1), (pairs - 1).bit_length())
            for d in range(n_dp):
                block = bit_reversed((d ^ lax.axis_index("dp")) >> 1, (n_dp // 2 - 1).bit_length())
                start = pl.multiple_of((block * pairs + place) * rows, rows)
                att_t[(d ^ lax.axis_index("dp")) & 1, pl.ds(start, rows), :] = o_low[d * rows : (d + 1) * rows, :]
        else:
            att_t[cols, :] = o_low


def forward(inputs, after, n_seq, n_dp):
    tokens, half = inputs[0].shape[0] - FLAG_ROWS, inputs[0].shape[1]
    features = 2 * half
    heads, pairs = features // HD, half // HD
    direct = n_seq == heads and HD % n_dp == 0 and (HD // n_dp) % 16 == 0
    one = shape_of(tokens, half)
    turned = shape_of(2, half // 2, 2 * tokens) if direct else shape_of(half, 2 * tokens)
    probs, att_own, att_back, turned = call(
        functools.partial(forward_kernel, direct, n_dp),
        (shape_of(pairs, 3 * tokens, 2 * tokens), one, one, turned),
        [VMEM] * 6 + [ANY],
        "patch_forward",
    )(*inputs, after)
    if not direct:
        here = lax.axis_index("seq")
        bits, d_bits = (n_seq - 1).bit_length(), (n_dp // 2 - 1).bit_length()
        order = jnp.array([bit_reversed(i, bits) for i in range(n_seq)], jnp.int32) ^ here
        d_order = [bit_reversed(i, d_bits) * 2 + c for c in range(2) for i in range(n_dp // 2)]
        full = jnp.zeros((heads // 2, 2, HD, 2 * tokens), BF16)
        full = lax.dynamic_update_slice(
            full, turned.reshape(heads // 2, 1, HD, 2 * tokens), (0, here & 1, 0, 0)
        )
        full = full.reshape(n_seq, n_dp, features // (n_seq * n_dp), 2 * tokens)
        full = jnp.take(full, order, axis=0)
        full = jnp.take(full, jnp.array(d_order, jnp.int32) ^ lax.axis_index("dp"), axis=1).transpose(1, 0, 2, 3)
        turned = full.reshape(2, features // 2, 2 * tokens)
    return probs, att_own, att_back, turned, 2 if direct else 1


def backward_kernel(
    q_own, q_par, own, par, far_own, far_par, ga, probs, _after, grads, edge_a, edge_b
):
    scale = 1.0 / math.sqrt(HD)
    tokens, half = q_own.shape[0] - FLAG_ROWS, q_own.shape[1]
    slot = far_slot(lax.axis_index("seq"))
    last = slice(2 * tokens, 3 * tokens)
    for j in range(half // HD):
        cols = slice(j * HD, (j + 1) * HD)
        g_both = ga[:, cols]
        go, gp = g_both[:tokens], g_both[tokens:]
        qo, qp = q_own[:tokens, cols], q_par[:tokens, cols]
        v = jnp.concatenate([own[tokens:, cols], par[tokens:, cols]], axis=0)
        vfo, vfp = far_own[tokens:, cols], far_par[tokens:, cols]
        gn = dot(v, g_both, 1, 1)
        g = [
            gn[:tokens],
            gn[tokens:],
            jnp.concatenate([dot(vfo, go, 1, 1), dot(vfp, gp, 1, 1)], axis=1),
        ]
        p = [probs[j, i * tokens : (i + 1) * tokens, :].astype(F32) for i in range(3)]
        delta = jnp.sum(p[0] * g[0] + p[1] * g[1] + p[2] * g[2], axis=0, keepdims=True)
        ds = [(p[i] * (g[i] - delta)).astype(BF16) for i in range(3)]
        for i in range(3):
            grads[j, i * tokens : (i + 1) * tokens, :] = ds[i]
        dfo, dfp = ds[2][:, :tokens], ds[2][:, tokens:]
        own_far = jnp.concatenate(
            [dot(dfo, qo, 1, 0) * scale, dot(probs[j, last, :tokens], go, 1, 0)], axis=0
        ).astype(BF16)
        par_far = jnp.concatenate(
            [dot(dfp, qp, 1, 0) * scale, dot(probs[j, last, tokens:], gp, 1, 0)], axis=0
        ).astype(BF16)
        edge_a[:, cols] = jnp.where(slot == 0, own_far, par_far)
        edge_b[:, cols] = jnp.where(slot == 0, par_far, own_far)


def backward(inputs, ga, probs, after):
    tokens, half = inputs[0].shape[0] - FLAG_ROWS, inputs[0].shape[1]
    return call(
        backward_kernel,
        (shape_of(*probs.shape),) + (shape_of(2 * tokens, half),) * 2,
        [VMEM] * 8 + [ANY],
        "patch_backward",
    )(*inputs, ga, probs, after)


def gradient_kernel(
    q_own, q_par, own, par, far_own, far_par, ga, probs, grads, dq_own, dq_back, d_own, d_par
):
    scale = 1.0 / math.sqrt(HD)
    tokens, half = q_own.shape[0] - FLAG_ROWS, q_own.shape[1]
    near, last = slice(0, 2 * tokens), slice(2 * tokens, 3 * tokens)
    for j in range(half // HD):
        cols = slice(j * HD, (j + 1) * HD)
        q = jnp.concatenate([q_own[:tokens, cols], q_par[:tokens, cols]], axis=0)
        k = jnp.concatenate([own[:tokens, cols], par[:tokens, cols]], axis=0)
        kfo, kfp = far_own[:tokens, cols], far_par[:tokens, cols]
        low, dsn = probs[j, near, :], grads[j, near, :]
        dfo, dfp = grads[j, last, :tokens], grads[j, last, tokens:]
        dq = dot(dsn, k, 0, 0) + jnp.concatenate([dot(dfo, kfo, 0, 0), dot(dfp, kfp, 0, 0)], axis=0)
        dq = (dq * scale).astype(BF16)
        dq_own[:, cols] = dq[:tokens]
        dq_back[:, cols] = dq[tokens:]
        dk = (dot(dsn, q, 1, 0) * scale).astype(BF16)
        dv = dot(low, ga[:, cols], 1, 0).astype(BF16)
        d_own[:tokens, cols] = dk[:tokens]
        d_par[:tokens, cols] = dk[tokens:]
        d_own[tokens:, cols] = dv[:tokens]
        d_par[tokens:, cols] = dv[tokens:]


def gradients(inputs, ga, probs, grads):
    tokens, half = inputs[0].shape[0] - FLAG_ROWS, inputs[0].shape[1]
    one, kv = shape_of(tokens, half), shape_of(2 * tokens, half)
    return call(
        gradient_kernel, (one, one, kv, kv), [VMEM] * 9, "patch_gradients"
    )(*inputs, ga, probs, grads)


def weight_kernel(att_keep, att_core, own, par, core_own, core_par, keep, send):
    size = keep.shape[0]
    tokens = own.shape[0]
    for target, start in ((send, size), (keep, 0)):
        rows = slice(start, start + size)
        total = dot(att_keep[rows, :tokens], own[...], 1, 0)
        total += dot(att_keep[rows, tokens:], par[...], 1, 0)
        total += dot(att_core[rows, :tokens], core_own[...], 1, 0)
        total += dot(att_core[rows, tokens:], core_par[...], 1, 0)
        target[...] = total.astype(target.dtype)


def weight_terms(*operands):
    rows = operands[0].shape[0]
    tokens, width = operands[2].shape
    return call(
        weight_kernel,
        (shape_of(rows // 2, width, dtype=F32), shape_of(rows // 2, width)),
        [VMEM] * 6,
        "weight_terms",
    )(*operands)


def query_kernel(att_own, att_back, dq_own, dq_back, w, out, dq, att):
    mine = lax.axis_index("seq") & 1
    for j in range(att_own.shape[1] // HD):
        cols = slice(j * HD, (j + 1) * HD)
        att[:, head_cols(j, mine)] = att_own[:, cols]
        att[:, head_cols(j, 1 - mine)] = att_back[:, cols]
        dq[:, head_cols(j, mine)] = dq_own[:, cols]
        dq[:, head_cols(j, 1 - mine)] = dq_back[:, cols]
    out[...] = dot(att[...], w[...], 1, 0).astype(BF16)


def finish_queries(att_own, att_back, dq_own, dq_back, w):
    tokens = att_own.shape[0]
    return call(
        query_kernel,
        (shape_of(tokens, w.shape[1]), shape_of(tokens, w.shape[0])),
        [VMEM] * 5,
        "finish_queries",
        scratch=[pltpu.VMEM((tokens, w.shape[0]), BF16)],
    )(att_own, att_back, dq_own, dq_back, w)


def returned_kernel(d_par, far_a, far_b, total):
    slot = far_slot(lax.axis_index("seq"))
    returned = jnp.where(slot == 0, far_b[...].astype(F32), far_a[...].astype(F32))
    total[...] = (d_par[...].astype(F32) + returned).astype(BF16)


def add_returned(d_par, far):
    return call(
        returned_kernel, (shape_of(*d_par.shape),), [VMEM] * 3, "add_returned"
    )(d_par, *far)[0]


def key_kernel(own, far_a, far_b, home, keep, out, dk, dv, total):
    mine = lax.axis_index("seq") & 1
    slot = far_slot(lax.axis_index("seq"))
    tokens = dk.shape[0]
    for i, target in ((0, dk), (1, dv)):
        rows = slice(i * tokens, (i + 1) * tokens)
        for j in range(own.shape[1] // HD):
            cols = slice(j * HD, (j + 1) * HD)
            far = jnp.where(slot == 0, far_a[rows, cols].astype(F32), far_b[rows, cols].astype(F32))
            target[:, head_cols(j, mine)] = (own[rows, cols].astype(F32) + far).astype(BF16)
            target[:, head_cols(j, 1 - mine)] = home[rows, cols]
    total[...] = keep[...] + out[...].astype(F32)


def finish_keys(own, far, home, keep, out):
    tokens, half = own.shape[0] // 2, own.shape[1]
    return call(
        key_kernel,
        (shape_of(tokens, 2 * half),) * 2 + (shape_of(*keep.shape, dtype=F32),),
        [VMEM] * 6,
        "finish_keys",
    )(own, *far, home, keep, out)


def on_device(queries, key_states, values, w_out, cotangent, neighbours, counts):
    n_seq, n_dp = lax.axis_size("seq"), lax.axis_size("dp")
    cot = cotangent[0]

    swap = [(i, i ^ 1) for i in range(n_seq)]
    relay = [(i, i + 2) for i in range(0, n_seq, 2) if i + 2 < n_seq]
    relay += [(i, i - 2) for i in range(1, n_seq, 2) if i - 2 >= 0]
    outer = [(b, a) for a, b in relay]
    edges = [[], []]
    for i in range(n_seq):
        edges[1].append((i, i ^ 2))
        other = i + 2 if (i >> 1) & 1 else i - 2
        if 0 <= other < n_seq:
            edges[0].append((i, other))
    send = lambda x, pairs: lax.ppermute(x, "seq", pairs)
    across = lambda x, k: lax.ppermute(x, "dp", [(i, i ^ k) for i in range(n_dp)])

    kv_send, own, q_send, q_own = pack(
        neighbours[0], queries[0], key_states[0], values[0]
    )
    par = send(kv_send, swap)
    q_par = send(q_send, swap)
    far_par = send(own, outer)
    cot_par = send(cot, swap)
    far_own = send(par, relay)
    core_own, core_par = across(cot, 1), across(cot_par, 1)
    ga = grad_attended(cot, cot_par, w_out)

    inputs = (q_own, q_par, own, par, far_own, far_par)
    probs, att_own, att_back, att_t, step = forward(
        inputs, ga, n_seq, n_dp
    )
    att_core = across(att_t[1], 1)
    att_back = send(att_back, swap)
    keep, out = weight_terms(att_t[0], att_core, cot, cot_par, core_own, core_par)
    grads, *leaving = backward(inputs, ga, probs, keep)
    far = [send(leaving[i], edges[i]) for i in range(2)]
    dq_own, dq_back, d_own, d_par = gradients(inputs, ga, probs, grads)
    dq_back = send(dq_back, swap)
    home = send(add_returned(d_par, far), swap)

    hops = []
    bit = 2
    while bit < n_dp:
        hops.append(("dp", n_dp, bit))
        bit *= 2
    while step < n_seq:
        hops.append(("seq", n_seq, step))
        step *= 2
    for place, (axis, count, bit) in enumerate(hops):
        out = lax.ppermute(out, axis, [(i, i ^ bit) for i in range(count)])
        if place + 1 < len(hops):
            total = keep + out.astype(F32)
            rows = total.shape[0] // 2
            keep, out = total[:rows], total[rows:].astype(BF16)

    output, dq = finish_queries(att_own, att_back, dq_own, dq_back, w_out)
    dk, dv, total = finish_keys(d_own, far, home, keep, out)
    return (output[None], dq[None], dk[None], dv[None], total)


def solution(mesh):
    placed = (
        P("dp", "seq", None),
        P("dp", "seq", None),
        P("dp", "seq", None),
        P(),
        P("dp", "seq", None),
        P("dp", "seq", None),
        P("dp", "seq"),
    )
    return jax.shard_map(
        on_device,
        mesh=mesh,
        in_specs=placed,
        out_specs=(
            P("dp", "seq", None),
            P("dp", "seq", None),
            P("dp", "seq", None),
            P("dp", "seq", None),
            P(("seq", "dp"), None),
        ),
        check_vma=False,
    )
```

```python
import functools
import math

import jax
import jax.numpy as jnp
from jax import lax
from jax.experimental import pallas as pl
from jax.experimental.pallas import tpu as pltpu
from jax.sharding import PartitionSpec as P

HD = 128
VMEM_LIMIT = 12 * 1024 * 1024
F32 = jnp.float32
BF16 = jnp.bfloat16
VMEM = pl.BlockSpec(memory_space=pltpu.VMEM)
HBM = pl.BlockSpec(memory_space=pltpu.HBM)
ANY = pl.BlockSpec(memory_space=pl.ANY)
FLAG_ROWS = 16


def dot(a, b, ca, cb):
    return lax.dot_general(a, b, (((ca,), (cb,)), ((), ())), preferred_element_type=F32)


def bit_reversed(index, bits):
    out = 0
    for b in range(bits):
        out = out * 2 + ((index >> b) & 1)
    return out


def shape_of(*dims, dtype=BF16):
    return jax.ShapeDtypeStruct(dims, dtype)


def call(body, out_shape, in_specs, name, scratch=()):
    return pl.pallas_call(
        body,
        out_shape=out_shape,
        in_specs=in_specs,
        out_specs=(VMEM,) * len(out_shape),
        scratch_shapes=list(scratch),
        compiler_params=pltpu.CompilerParams(vmem_limit_bytes=VMEM_LIMIT),
        cost_estimate=pl.CostEstimate(flops=0, bytes_accessed=0, transcendentals=0),
        name=name,
    )


def head_cols(pair, parity):
    return pl.ds(pl.multiple_of((2 * pair + parity) * HD, HD), HD)


def listed_flags(me, listed):
    far_patch = jnp.where(me % 2 == 0, me - 1, me + 1)
    near, far = jnp.int32(0), jnp.int32(0)
    for slot in range(listed.shape[1]):
        near = jnp.where(listed[0, slot] == (me ^ 1), 1, near)
        far = jnp.where(listed[0, slot] == far_patch, 1, far)
    return near, far


def in_hbm(x):
    return pltpu.with_memory_space_constraint(x, pltpu.HBM)


def pack_kernel(listed, q, k, v, kv_send, kv_keep, q_send, q_keep, listed_in, sems):
    mine = lax.axis_index("seq") & 1
    tokens, half = q_keep.shape[0] - FLAG_ROWS, q_keep.shape[1]
    copies = []

    def copy(source, target):
        copies.append(pltpu.make_async_copy(source, target, sems.at[len(copies)]))
        copies[-1].start()

    copy(listed, listed_in)
    for kv, q_to, parity in ((kv_send, q_send, 1 - mine), (kv_keep, q_keep, mine)):
        for source, target, row in ((k, kv, 0), (v, kv, tokens), (q, q_to, 0)):
            for j in range(half // HD):
                copy(
                    source.at[:, head_cols(j, parity)],
                    target.at[row : row + tokens, j * HD : (j + 1) * HD],
                )
    copies[0].wait()
    near, far = listed_flags(lax.axis_index("seq"), listed_in)
    left = lax.broadcasted_iota(jnp.int32, (FLAG_ROWS, half), 1) < half // 2
    flags = jnp.where(left, near, far).astype(F32).astype(BF16)
    q_send[tokens : tokens + FLAG_ROWS, :] = flags
    q_keep[tokens : tokens + FLAG_ROWS, :] = flags
    for item in copies[1:]:
        item.wait()


def pack(listed, q, k, v):
    tokens, features = k.shape
    half = features // 2
    kv = shape_of(2 * tokens, half)
    return call(
        pack_kernel,
        (kv, kv) + (shape_of(tokens + FLAG_ROWS, half),) * 2,
        [HBM] * 4,
        "pack_heads",
        scratch=[
            pltpu.SMEM(listed.shape, jnp.int32),
            pltpu.SemaphoreType.DMA((3 * features // HD + 1,)),
        ],
    )(*[in_hbm(x) for x in (listed, q, k, v)])


def turn_kernel(cot, cot_par, w, ga, cot_in, w_in, sems):
    tokens = cot.shape[0]
    pairs = ga.shape[1] // HD
    copies = [pltpu.make_async_copy(cot, cot_in, sems.at[pairs])]
    for j in range(pairs):
        rows = w.at[head_cols(j, lax.axis_index("seq") & 1), :]
        copies.append(pltpu.make_async_copy(rows, w_in.at[j], sems.at[j]))
    for item in copies:
        item.start()
    copies[0].wait()
    for j in range(pairs):
        cols = slice(j * HD, (j + 1) * HD)
        copies[j + 1].wait()
        ga[:tokens, cols] = dot(cot_in[...], w_in[j], 1, 1).astype(BF16)
        ga[tokens:, cols] = dot(cot_par[...], w_in[j], 1, 1).astype(BF16)


def grad_attended(cot, cot_par, w):
    tokens, width = cot.shape
    pairs = w.shape[0] // (2 * HD)
    return call(
        turn_kernel,
        (shape_of(2 * tokens, pairs * HD),),
        [HBM, VMEM, HBM],
        "grad_attended",
        scratch=[
            pltpu.VMEM((tokens, width), BF16),
            pltpu.VMEM((pairs, HD, width), BF16),
            pltpu.SemaphoreType.DMA((pairs + 1,)),
        ],
    )(in_hbm(cot), cot_par, in_hbm(w))[0]


def far_slot(me):
    return (me & 1) ^ ((me >> 1) & 1)


def forward_kernel(
    direct, n_dp, q_own, q_par, own, par, far_own, far_par, after,
    probs, att_own, att_back, att_t,
):
    rate = math.log2(math.e) / math.sqrt(HD)
    tokens, half = q_own.shape[0] - FLAG_ROWS, q_own.shape[1]
    pairs = half // HD
    me = lax.axis_index("seq")
    left = lax.broadcasted_iota(jnp.int32, (1, 2 * tokens), 1) < tokens

    def barred(x, place):
        flag = x[tokens : tokens + FLAG_ROWS, :].astype(F32)[:1, place : place + 1]
        return jnp.where(jnp.broadcast_to(flag, (1, 2 * tokens)) > 0, 0.0, -jnp.inf)

    bias = (
        jnp.where(left, 0.0, barred(q_par, 0)),
        jnp.where(left, barred(q_own, 0), 0.0),
        jnp.where(left, barred(q_own, half - 1), barred(q_par, half - 1)),
    )
    for j in range(pairs):
        cols = slice(j * HD, (j + 1) * HD)
        qo, qp = q_own[:tokens, cols], q_par[:tokens, cols]
        q = jnp.concatenate([qo, qp], axis=0)
        k = jnp.concatenate([own[:tokens, cols], par[:tokens, cols]], axis=0)
        v = jnp.concatenate([own[tokens:, cols], par[tokens:, cols]], axis=0)
        near = dot(k, q, 1, 1)
        far = jnp.concatenate(
            [dot(far_own[:tokens, cols], qo, 1, 1), dot(far_par[:tokens, cols], qp, 1, 1)], axis=1
        )
        s = [near[:tokens] + bias[0], near[tokens:] + bias[1], far + bias[2]]
        top = jnp.max(jnp.maximum(jnp.maximum(s[0], s[1]), s[2]), axis=0, keepdims=True)
        e = [jnp.exp2((x - top) * rate) for x in s]
        inv = 1.0 / jnp.sum(e[0] + e[1] + e[2], axis=0, keepdims=True)
        low = [(x * inv).astype(BF16) for x in e]
        for i in range(3):
            probs[j, i * tokens : (i + 1) * tokens, :] = low[i]
        vfo, vfp = far_own[tokens:, cols], far_par[tokens:, cols]
        o_t = dot(v, jnp.concatenate(low[:2], axis=0), 0, 0)
        o_t += jnp.concatenate(
            [dot(vfo, low[2][:, :tokens], 0, 0), dot(vfp, low[2][:, tokens:], 0, 0)], axis=1
        )
        o = o_t.T.astype(BF16)
        att_own[:, cols] = o[:tokens]
        att_back[:, cols] = o[tokens:]
        o_low = o_t.astype(BF16)
        if direct:
            rows = HD // n_dp
            place = bit_reversed(j ^ (me >> 1), (pairs - 1).bit_length())
            for d in range(n_dp):
                block = bit_reversed((d ^ lax.axis_index("dp")) >> 1, (n_dp // 2 - 1).bit_length())
                start = pl.multiple_of((block * pairs + place) * rows, rows)
                att_t[(d ^ lax.axis_index("dp")) & 1, pl.ds(start, rows), :] = o_low[d * rows : (d + 1) * rows, :]
        else:
            att_t[cols, :] = o_low


def forward(inputs, after, n_seq, n_dp):
    tokens, half = inputs[0].shape[0] - FLAG_ROWS, inputs[0].shape[1]
    features = 2 * half
    heads, pairs = features // HD, half // HD
    direct = n_seq == heads and HD % n_dp == 0 and (HD // n_dp) % 16 == 0
    one = shape_of(tokens, half)
    turned = shape_of(2, half // 2, 2 * tokens) if direct else shape_of(half, 2 * tokens)
    probs, att_own, att_back, turned = call(
        functools.partial(forward_kernel, direct, n_dp),
        (shape_of(pairs, 3 * tokens, 2 * tokens), one, one, turned),
        [VMEM] * 6 + [ANY],
        "patch_forward",
    )(*inputs, after)
    if not direct:
        here = lax.axis_index("seq")
        bits, d_bits = (n_seq - 1).bit_length(), (n_dp // 2 - 1).bit_length()
        order = jnp.array([bit_reversed(i, bits) for i in range(n_seq)], jnp.int32) ^ here
        d_order = [bit_reversed(i, d_bits) * 2 + c for c in range(2) for i in range(n_dp // 2)]
        full = jnp.zeros((heads // 2, 2, HD, 2 * tokens), BF16)
        full = lax.dynamic_update_slice(
            full, turned.reshape(heads // 2, 1, HD, 2 * tokens), (0, here & 1, 0, 0)
        )
        full = full.reshape(n_seq, n_dp, features // (n_seq * n_dp), 2 * tokens)
        full = jnp.take(full, order, axis=0)
        full = jnp.take(full, jnp.array(d_order, jnp.int32) ^ lax.axis_index("dp"), axis=1).transpose(1, 0, 2, 3)
        turned = full.reshape(2, features // 2, 2 * tokens)
    return probs, att_own, att_back, turned, 2 if direct else 1


def backward_kernel(
    q_own, q_par, own, par, far_own, far_par, ga, probs, grads, edge_a, edge_b
):
    scale = 1.0 / math.sqrt(HD)
    tokens, half = q_own.shape[0] - FLAG_ROWS, q_own.shape[1]
    slot = far_slot(lax.axis_index("seq"))
    last = slice(2 * tokens, 3 * tokens)
    for j in range(half // HD):
        cols = slice(j * HD, (j + 1) * HD)
        g_both = ga[:, cols]
        go, gp = g_both[:tokens], g_both[tokens:]
        qo, qp = q_own[:tokens, cols], q_par[:tokens, cols]
        v = jnp.concatenate([own[tokens:, cols], par[tokens:, cols]], axis=0)
        vfo, vfp = far_own[tokens:, cols], far_par[tokens:, cols]
        gn = dot(v, g_both, 1, 1)
        g = [
            gn[:tokens],
            gn[tokens:],
            jnp.concatenate([dot(vfo, go, 1, 1), dot(vfp, gp, 1, 1)], axis=1),
        ]
        p = [probs[j, i * tokens : (i + 1) * tokens, :].astype(F32) for i in range(3)]
        delta = jnp.sum(p[0] * g[0] + p[1] * g[1] + p[2] * g[2], axis=0, keepdims=True)
        ds = [(p[i] * (g[i] - delta)).astype(BF16) for i in range(3)]
        for i in range(3):
            grads[j, i * tokens : (i + 1) * tokens, :] = ds[i]
        dfo, dfp = ds[2][:, :tokens], ds[2][:, tokens:]
        own_far = jnp.concatenate(
            [dot(dfo, qo, 1, 0) * scale, dot(probs[j, last, :tokens], go, 1, 0)], axis=0
        ).astype(BF16)
        par_far = jnp.concatenate(
            [dot(dfp, qp, 1, 0) * scale, dot(probs[j, last, tokens:], gp, 1, 0)], axis=0
        ).astype(BF16)
        edge_a[:, cols] = jnp.where(slot == 0, own_far, par_far)
        edge_b[:, cols] = jnp.where(slot == 0, par_far, own_far)


def backward(inputs, ga, probs):
    tokens, half = inputs[0].shape[0] - FLAG_ROWS, inputs[0].shape[1]
    return call(
        backward_kernel,
        (shape_of(*probs.shape),) + (shape_of(2 * tokens, half),) * 2,
        [VMEM] * 8,
        "patch_backward",
    )(*inputs, ga, probs)


def gradient_kernel(
    q_own, q_par, own, par, far_own, far_par, ga, probs, grads, dq_own, dq_back, d_own, d_par
):
    scale = 1.0 / math.sqrt(HD)
    tokens, half = q_own.shape[0] - FLAG_ROWS, q_own.shape[1]
    near, last = slice(0, 2 * tokens), slice(2 * tokens, 3 * tokens)
    for j in range(half // HD):
        cols = slice(j * HD, (j + 1) * HD)
        q = jnp.concatenate([q_own[:tokens, cols], q_par[:tokens, cols]], axis=0)
        k = jnp.concatenate([own[:tokens, cols], par[:tokens, cols]], axis=0)
        kfo, kfp = far_own[:tokens, cols], far_par[:tokens, cols]
        low, dsn = probs[j, near, :], grads[j, near, :]
        dfo, dfp = grads[j, last, :tokens], grads[j, last, tokens:]
        dq = dot(dsn, k, 0, 0) + jnp.concatenate([dot(dfo, kfo, 0, 0), dot(dfp, kfp, 0, 0)], axis=0)
        dq = (dq * scale).astype(BF16)
        dq_own[:, cols] = dq[:tokens]
        dq_back[:, cols] = dq[tokens:]
        dk = (dot(dsn, q, 1, 0) * scale).astype(BF16)
        dv = dot(low, ga[:, cols], 1, 0).astype(BF16)
        d_own[:tokens, cols] = dk[:tokens]
        d_par[:tokens, cols] = dk[tokens:]
        d_own[tokens:, cols] = dv[:tokens]
        d_par[tokens:, cols] = dv[tokens:]


def gradients(inputs, ga, probs, grads):
    tokens, half = inputs[0].shape[0] - FLAG_ROWS, inputs[0].shape[1]
    one, kv = shape_of(tokens, half), shape_of(2 * tokens, half)
    return call(
        gradient_kernel, (one, one, kv, kv), [VMEM] * 9, "patch_gradients"
    )(*inputs, ga, probs, grads)


def weight_kernel(kept, att_keep, att_core, own, par, core_own, core_par, _after, target):
    size = target.shape[0]
    tokens = own.shape[0]
    rows = slice(0, size) if kept else slice(size, 2 * size)
    total = dot(att_keep[rows, :tokens], own[...], 1, 0)
    total += dot(att_keep[rows, tokens:], par[...], 1, 0)
    total += dot(att_core[rows, :tokens], core_own[...], 1, 0)
    total += dot(att_core[rows, tokens:], core_par[...], 1, 0)
    target[...] = total.astype(target.dtype)


def weight_terms(kept, operands, after):
    rows, width = operands[0].shape[0] // 2, operands[2].shape[1]
    return call(
        functools.partial(weight_kernel, kept),
        (shape_of(rows, width, dtype=F32 if kept else BF16),),
        [VMEM] * 6 + [ANY],
        "weight_terms_kept" if kept else "weight_terms_sent",
    )(*operands, after)[0]


def query_kernel(att_own, att_back, dq_own, dq_back, w, out, dq, att):
    mine = lax.axis_index("seq") & 1
    for j in range(att_own.shape[1] // HD):
        cols = slice(j * HD, (j + 1) * HD)
        att[:, head_cols(j, mine)] = att_own[:, cols]
        att[:, head_cols(j, 1 - mine)] = att_back[:, cols]
        dq[:, head_cols(j, mine)] = dq_own[:, cols]
        dq[:, head_cols(j, 1 - mine)] = dq_back[:, cols]
    out[...] = dot(att[...], w[...], 1, 0).astype(BF16)


def finish_queries(att_own, att_back, dq_own, dq_back, w):
    tokens = att_own.shape[0]
    return call(
        query_kernel,
        (shape_of(tokens, w.shape[1]), shape_of(tokens, w.shape[0])),
        [VMEM] * 5,
        "finish_queries",
        scratch=[pltpu.VMEM((tokens, w.shape[0]), BF16)],
    )(att_own, att_back, dq_own, dq_back, w)


def returned_kernel(d_par, far_a, far_b, total):
    slot = far_slot(lax.axis_index("seq"))
    returned = jnp.where(slot == 0, far_b[...].astype(F32), far_a[...].astype(F32))
    total[...] = (d_par[...].astype(F32) + returned).astype(BF16)


def add_returned(d_par, far):
    return call(
        returned_kernel, (shape_of(*d_par.shape),), [VMEM] * 3, "add_returned"
    )(d_par, *far)[0]


def key_kernel(own, far_a, far_b, home, keep, out, dk, dv, total):
    mine = lax.axis_index("seq") & 1
    slot = far_slot(lax.axis_index("seq"))
    tokens = dk.shape[0]
    for i, target in ((0, dk), (1, dv)):
        rows = slice(i * tokens, (i + 1) * tokens)
        for j in range(own.shape[1] // HD):
            cols = slice(j * HD, (j + 1) * HD)
            far = jnp.where(slot == 0, far_a[rows, cols].astype(F32), far_b[rows, cols].astype(F32))
            target[:, head_cols(j, mine)] = (own[rows, cols].astype(F32) + far).astype(BF16)
            target[:, head_cols(j, 1 - mine)] = home[rows, cols]
    total[...] = keep[...] + out[...].astype(F32)


def finish_keys(own, far, home, keep, out):
    tokens, half = own.shape[0] // 2, own.shape[1]
    return call(
        key_kernel,
        (shape_of(tokens, 2 * half),) * 2 + (shape_of(*keep.shape, dtype=F32),),
        [VMEM] * 6,
        "finish_keys",
    )(own, *far, home, keep, out)


def on_device(queries, key_states, values, w_out, cotangent, neighbours, counts):
    n_seq, n_dp = lax.axis_size("seq"), lax.axis_size("dp")
    cot = cotangent[0]

    swap = [(i, i ^ 1) for i in range(n_seq)]
    relay = [(i, i + 2) for i in range(0, n_seq, 2) if i + 2 < n_seq]
    relay += [(i, i - 2) for i in range(1, n_seq, 2) if i - 2 >= 0]
    outer = [(b, a) for a, b in relay]
    edges = [[], []]
    for i in range(n_seq):
        edges[1].append((i, i ^ 2))
        other = i + 2 if (i >> 1) & 1 else i - 2
        if 0 <= other < n_seq:
            edges[0].append((i, other))
    send = lambda x, pairs: lax.ppermute(x, "seq", pairs)
    across = lambda x, k: lax.ppermute(x, "dp", [(i, i ^ k) for i in range(n_dp)])

    kv_send, own, q_send, q_own = pack(
        neighbours[0], queries[0], key_states[0], values[0]
    )
    par = send(kv_send, swap)
    q_par = send(q_send, swap)
    far_par = send(own, outer)
    cot_par = send(cot, swap)
    far_own = send(par, relay)
    core_own, core_par = across(cot, 1), across(cot_par, 1)
    ga = grad_attended(cot, cot_par, w_out)

    inputs = (q_own, q_par, own, par, far_own, far_par)
    probs, att_own, att_back, att_t, step = forward(
        inputs, ga, n_seq, n_dp
    )
    att_core = across(att_t[1], 1)
    att_back = send(att_back, swap)
    grads, *leaving = backward(inputs, ga, probs)
    operands = (att_t[0], att_core, cot, cot_par, core_own, core_par)
    out = weight_terms(False, operands, leaving[0])
    keep = weight_terms(True, operands, out)
    far = [send(leaving[i], edges[i]) for i in range(2)]
    dq_own, dq_back, d_own, d_par = gradients(inputs, ga, probs, grads)
    dq_back = send(dq_back, swap)
    home = send(add_returned(d_par, far), swap)

    hops = []
    bit = 2
    while bit < n_dp:
        hops.append(("dp", n_dp, bit))
        bit *= 2
    while step < n_seq:
        hops.append(("seq", n_seq, step))
        step *= 2
    for place, (axis, count, bit) in enumerate(hops):
        out = lax.ppermute(out, axis, [(i, i ^ bit) for i in range(count)])
        if place + 1 < len(hops):
            total = keep + out.astype(F32)
            rows = total.shape[0] // 2
            keep, out = total[:rows], total[rows:].astype(BF16)

    output, dq = finish_queries(att_own, att_back, dq_own, dq_back, w_out)
    dk, dv, total = finish_keys(d_own, far, home, keep, out)
    return (output[None], dq[None], dk[None], dv[None], total)


def solution(mesh):
    placed = (
        P("dp", "seq", None),
        P("dp", "seq", None),
        P("dp", "seq", None),
        P(),
        P("dp", "seq", None),
        P("dp", "seq", None),
        P("dp", "seq"),
    )
    return jax.shard_map(
        on_device,
        mesh=mesh,
        in_specs=placed,
        out_specs=(
            P("dp", "seq", None),
            P("dp", "seq", None),
            P("dp", "seq", None),
            P("dp", "seq", None),
            P(("seq", "dp"), None),
        ),
        check_vma=False,
    )
```

```python
import functools
import math

import jax
import jax.numpy as jnp
from jax import lax
from jax.experimental import pallas as pl
from jax.experimental.pallas import tpu as pltpu
from jax.sharding import PartitionSpec as P

HD = 128
VMEM_LIMIT = 12 * 1024 * 1024
F32 = jnp.float32
BF16 = jnp.bfloat16
VMEM = pl.BlockSpec(memory_space=pltpu.VMEM)
HBM = pl.BlockSpec(memory_space=pltpu.HBM)
ANY = pl.BlockSpec(memory_space=pl.ANY)
FLAG_ROWS = 16


def dot(a, b, ca, cb):
    return lax.dot_general(a, b, (((ca,), (cb,)), ((), ())), preferred_element_type=F32)


def bit_reversed(index, bits):
    out = 0
    for b in range(bits):
        out = out * 2 + ((index >> b) & 1)
    return out


def shape_of(*dims, dtype=BF16):
    return jax.ShapeDtypeStruct(dims, dtype)


def call(body, out_shape, in_specs, name, scratch=()):
    return pl.pallas_call(
        body,
        out_shape=out_shape,
        in_specs=in_specs,
        out_specs=(VMEM,) * len(out_shape),
        scratch_shapes=list(scratch),
        compiler_params=pltpu.CompilerParams(vmem_limit_bytes=VMEM_LIMIT),
        cost_estimate=pl.CostEstimate(flops=0, bytes_accessed=0, transcendentals=0),
        name=name,
    )


def head_cols(pair, parity):
    return pl.ds(pl.multiple_of((2 * pair + parity) * HD, HD), HD)


def listed_flags(me, listed):
    far_patch = jnp.where(me % 2 == 0, me - 1, me + 1)
    near, far = jnp.int32(0), jnp.int32(0)
    for slot in range(listed.shape[1]):
        near = jnp.where(listed[0, slot] == (me ^ 1), 1, near)
        far = jnp.where(listed[0, slot] == far_patch, 1, far)
    return near, far


def in_hbm(x):
    return pltpu.with_memory_space_constraint(x, pltpu.HBM)


def pack_kernel(listed, q, k, v, kv_send, kv_keep, q_send, q_keep, listed_in, sems):
    mine = lax.axis_index("seq") & 1
    tokens, half = q_keep.shape[0] - FLAG_ROWS, q_keep.shape[1]
    copies = []

    def copy(source, target):
        copies.append(pltpu.make_async_copy(source, target, sems.at[len(copies)]))
        copies[-1].start()

    copy(listed, listed_in)
    for kv, q_to, parity in ((kv_send, q_send, 1 - mine), (kv_keep, q_keep, mine)):
        for source, target, row in ((k, kv, 0), (v, kv, tokens), (q, q_to, 0)):
            for j in range(half // HD):
                copy(
                    source.at[:, head_cols(j, parity)],
                    target.at[row : row + tokens, j * HD : (j + 1) * HD],
                )
    copies[0].wait()
    near, far = listed_flags(lax.axis_index("seq"), listed_in)
    left = lax.broadcasted_iota(jnp.int32, (FLAG_ROWS, half), 1) < half // 2
    flags = jnp.where(left, near, far).astype(F32).astype(BF16)
    q_send[tokens : tokens + FLAG_ROWS, :] = flags
    q_keep[tokens : tokens + FLAG_ROWS, :] = flags
    for item in copies[1:]:
        item.wait()


def pack(listed, q, k, v):
    tokens, features = k.shape
    half = features // 2
    kv = shape_of(2 * tokens, half)
    return call(
        pack_kernel,
        (kv, kv) + (shape_of(tokens + FLAG_ROWS, half),) * 2,
        [HBM] * 4,
        "pack_heads",
        scratch=[
            pltpu.SMEM(listed.shape, jnp.int32),
            pltpu.SemaphoreType.DMA((3 * features // HD + 1,)),
        ],
    )(*[in_hbm(x) for x in (listed, q, k, v)])


def turn_kernel(cot, cot_par, w, ga, cot_in, w_in, sems):
    tokens = cot.shape[0]
    pairs = ga.shape[1] // HD
    copies = [pltpu.make_async_copy(cot, cot_in, sems.at[pairs])]
    for j in range(pairs):
        rows = w.at[head_cols(j, lax.axis_index("seq") & 1), :]
        copies.append(pltpu.make_async_copy(rows, w_in.at[j], sems.at[j]))
    for item in copies:
        item.start()
    copies[0].wait()
    for j in range(pairs):
        cols = slice(j * HD, (j + 1) * HD)
        copies[j + 1].wait()
        ga[:tokens, cols] = dot(cot_in[...], w_in[j], 1, 1).astype(BF16)
        ga[tokens:, cols] = dot(cot_par[...], w_in[j], 1, 1).astype(BF16)


def grad_attended(cot, cot_par, w):
    tokens, width = cot.shape
    pairs = w.shape[0] // (2 * HD)
    return call(
        turn_kernel,
        (shape_of(2 * tokens, pairs * HD),),
        [HBM, VMEM, HBM],
        "grad_attended",
        scratch=[
            pltpu.VMEM((tokens, width), BF16),
            pltpu.VMEM((pairs, HD, width), BF16),
            pltpu.SemaphoreType.DMA((pairs + 1,)),
        ],
    )(in_hbm(cot), cot_par, in_hbm(w))[0]


def far_slot(me):
    return (me & 1) ^ ((me >> 1) & 1)


def forward_kernel(
    direct, n_dp, q_own, q_par, own, par, far_own, far_par, after,
    probs, att_own, att_back, att_t,
):
    rate = math.log2(math.e) / math.sqrt(HD)
    tokens, half = q_own.shape[0] - FLAG_ROWS, q_own.shape[1]
    pairs = half // HD
    me = lax.axis_index("seq")
    left = lax.broadcasted_iota(jnp.int32, (1, 2 * tokens), 1) < tokens

    def barred(x, place):
        flag = x[tokens : tokens + FLAG_ROWS, :].astype(F32)[:1, place : place + 1]
        return jnp.where(jnp.broadcast_to(flag, (1, 2 * tokens)) > 0, 0.0, -jnp.inf)

    bias = (
        jnp.where(left, 0.0, barred(q_par, 0)),
        jnp.where(left, barred(q_own, 0), 0.0),
        jnp.where(left, barred(q_own, half - 1), barred(q_par, half - 1)),
    )
    for j in range(pairs):
        cols = slice(j * HD, (j + 1) * HD)
        qo, qp = q_own[:tokens, cols], q_par[:tokens, cols]
        q = jnp.concatenate([qo, qp], axis=0)
        k = jnp.concatenate([own[:tokens, cols], par[:tokens, cols]], axis=0)
        v = jnp.concatenate([own[tokens:, cols], par[tokens:, cols]], axis=0)
        near = dot(k, q, 1, 1)
        far = jnp.concatenate(
            [dot(far_own[:tokens, cols], qo, 1, 1), dot(far_par[:tokens, cols], qp, 1, 1)], axis=1
        )
        s = [near[:tokens] + bias[0], near[tokens:] + bias[1], far + bias[2]]
        top = jnp.max(jnp.maximum(jnp.maximum(s[0], s[1]), s[2]), axis=0, keepdims=True)
        e = [jnp.exp2((x - top) * rate) for x in s]
        inv = 1.0 / jnp.sum(e[0] + e[1] + e[2], axis=0, keepdims=True)
        low = [(x * inv).astype(BF16) for x in e]
        for i in range(3):
            probs[j, i * tokens : (i + 1) * tokens, :] = low[i]
        vfo, vfp = far_own[tokens:, cols], far_par[tokens:, cols]
        o_t = dot(v, jnp.concatenate(low[:2], axis=0), 0, 0)
        o_t += jnp.concatenate(
            [dot(vfo, low[2][:, :tokens], 0, 0), dot(vfp, low[2][:, tokens:], 0, 0)], axis=1
        )
        o = o_t.T.astype(BF16)
        att_own[:, cols] = o[:tokens]
        att_back[:, cols] = o[tokens:]
        o_low = o_t.astype(BF16)
        if direct:
            rows = HD // n_dp
            place = bit_reversed(j ^ (me >> 1), (pairs - 1).bit_length())
            for d in range(n_dp):
                block = bit_reversed((d ^ lax.axis_index("dp")) >> 1, (n_dp // 2 - 1).bit_length())
                start = pl.multiple_of((block * pairs + place) * rows, rows)
                att_t[(d ^ lax.axis_index("dp")) & 1, pl.ds(start, rows), :] = o_low[d * rows : (d + 1) * rows, :]
        else:
            att_t[cols, :] = o_low


def forward(inputs, after, n_seq, n_dp):
    tokens, half = inputs[0].shape[0] - FLAG_ROWS, inputs[0].shape[1]
    features = 2 * half
    heads, pairs = features // HD, half // HD
    direct = n_seq == heads and HD % n_dp == 0 and (HD // n_dp) % 16 == 0
    one = shape_of(tokens, half)
    turned = shape_of(2, half // 2, 2 * tokens) if direct else shape_of(half, 2 * tokens)
    probs, att_own, att_back, turned = call(
        functools.partial(forward_kernel, direct, n_dp),
        (shape_of(pairs, 3 * tokens, 2 * tokens), one, one, turned),
        [VMEM] * 6 + [ANY],
        "patch_forward",
    )(*inputs, after)
    if not direct:
        here = lax.axis_index("seq")
        bits, d_bits = (n_seq - 1).bit_length(), (n_dp // 2 - 1).bit_length()
        order = jnp.array([bit_reversed(i, bits) for i in range(n_seq)], jnp.int32) ^ here
        d_order = [bit_reversed(i, d_bits) * 2 + c for c in range(2) for i in range(n_dp // 2)]
        full = jnp.zeros((heads // 2, 2, HD, 2 * tokens), BF16)
        full = lax.dynamic_update_slice(
            full, turned.reshape(heads // 2, 1, HD, 2 * tokens), (0, here & 1, 0, 0)
        )
        full = full.reshape(n_seq, n_dp, features // (n_seq * n_dp), 2 * tokens)
        full = jnp.take(full, order, axis=0)
        full = jnp.take(full, jnp.array(d_order, jnp.int32) ^ lax.axis_index("dp"), axis=1).transpose(1, 0, 2, 3)
        turned = full.reshape(2, features // 2, 2 * tokens)
    return probs, att_own, att_back, turned, 2 if direct else 1


def backward_kernel(
    q_own, q_par, own, par, far_own, far_par, ga, probs, grads, edge_a, edge_b
):
    scale = 1.0 / math.sqrt(HD)
    tokens, half = q_own.shape[0] - FLAG_ROWS, q_own.shape[1]
    slot = far_slot(lax.axis_index("seq"))
    last = slice(2 * tokens, 3 * tokens)
    for j in range(half // HD):
        cols = slice(j * HD, (j + 1) * HD)
        g_both = ga[:, cols]
        go, gp = g_both[:tokens], g_both[tokens:]
        qo, qp = q_own[:tokens, cols], q_par[:tokens, cols]
        v = jnp.concatenate([own[tokens:, cols], par[tokens:, cols]], axis=0)
        vfo, vfp = far_own[tokens:, cols], far_par[tokens:, cols]
        gn = dot(v, g_both, 1, 1)
        g = [
            gn[:tokens],
            gn[tokens:],
            jnp.concatenate([dot(vfo, go, 1, 1), dot(vfp, gp, 1, 1)], axis=1),
        ]
        p = [probs[j, i * tokens : (i + 1) * tokens, :].astype(F32) for i in range(3)]
        delta = jnp.sum(p[0] * g[0] + p[1] * g[1] + p[2] * g[2], axis=0, keepdims=True)
        ds = [(p[i] * (g[i] - delta)).astype(BF16) for i in range(3)]
        for i in range(3):
            grads[j, i * tokens : (i + 1) * tokens, :] = ds[i]
        dfo, dfp = ds[2][:, :tokens], ds[2][:, tokens:]
        own_far = jnp.concatenate(
            [dot(dfo, qo, 1, 0) * scale, dot(probs[j, last, :tokens], go, 1, 0)], axis=0
        ).astype(BF16)
        par_far = jnp.concatenate(
            [dot(dfp, qp, 1, 0) * scale, dot(probs[j, last, tokens:], gp, 1, 0)], axis=0
        ).astype(BF16)
        edge_a[:, cols] = jnp.where(slot == 0, own_far, par_far)
        edge_b[:, cols] = jnp.where(slot == 0, par_far, own_far)


def backward(inputs, ga, probs):
    tokens, half = inputs[0].shape[0] - FLAG_ROWS, inputs[0].shape[1]
    return call(
        backward_kernel,
        (shape_of(*probs.shape),) + (shape_of(2 * tokens, half),) * 2,
        [VMEM] * 8,
        "patch_backward",
    )(*inputs, ga, probs)


def gradient_kernel(
    q_own, q_par, own, par, far_own, far_par, ga, probs, grads, dq_own, dq_back, d_own, d_par
):
    scale = 1.0 / math.sqrt(HD)
    tokens, half = q_own.shape[0] - FLAG_ROWS, q_own.shape[1]
    near, last = slice(0, 2 * tokens), slice(2 * tokens, 3 * tokens)
    for j in range(half // HD):
        cols = slice(j * HD, (j + 1) * HD)
        q = jnp.concatenate([q_own[:tokens, cols], q_par[:tokens, cols]], axis=0)
        k = jnp.concatenate([own[:tokens, cols], par[:tokens, cols]], axis=0)
        kfo, kfp = far_own[:tokens, cols], far_par[:tokens, cols]
        low, dsn = probs[j, near, :], grads[j, near, :]
        dfo, dfp = grads[j, last, :tokens], grads[j, last, tokens:]
        dq = dot(dsn, k, 0, 0) + jnp.concatenate([dot(dfo, kfo, 0, 0), dot(dfp, kfp, 0, 0)], axis=0)
        dq = (dq * scale).astype(BF16)
        dq_own[:, cols] = dq[:tokens]
        dq_back[:, cols] = dq[tokens:]
        dk = (dot(dsn, q, 1, 0) * scale).astype(BF16)
        dv = dot(low, ga[:, cols], 1, 0).astype(BF16)
        d_own[:tokens, cols] = dk[:tokens]
        d_par[:tokens, cols] = dk[tokens:]
        d_own[tokens:, cols] = dv[:tokens]
        d_par[tokens:, cols] = dv[tokens:]


def gradients(inputs, ga, probs, grads):
    tokens, half = inputs[0].shape[0] - FLAG_ROWS, inputs[0].shape[1]
    one, kv = shape_of(tokens, half), shape_of(2 * tokens, half)
    return call(
        gradient_kernel, (one, one, kv, kv), [VMEM] * 9, "patch_gradients"
    )(*inputs, ga, probs, grads)


def weight_kernel(kept, att_keep, att_core, own, par, core_own, core_par, _after, target):
    size = target.shape[0]
    tokens = own.shape[0]
    rows = slice(0, size) if kept else slice(size, 2 * size)
    total = dot(att_keep[rows, :tokens], own[...], 1, 0)
    total += dot(att_keep[rows, tokens:], par[...], 1, 0)
    total += dot(att_core[rows, :tokens], core_own[...], 1, 0)
    total += dot(att_core[rows, tokens:], core_par[...], 1, 0)
    target[...] = total.astype(target.dtype)


def weight_terms(kept, operands, after):
    rows, width = operands[0].shape[0] // 2, operands[2].shape[1]
    return call(
        functools.partial(weight_kernel, kept),
        (shape_of(rows, width, dtype=F32 if kept else BF16),),
        [VMEM] * 6 + [ANY],
        "weight_terms_kept" if kept else "weight_terms_sent",
    )(*operands, after)[0]


def query_kernel(att_own, att_back, dq_own, dq_back, w, out, dq, att):
    mine = lax.axis_index("seq") & 1
    for j in range(att_own.shape[1] // HD):
        cols = slice(j * HD, (j + 1) * HD)
        att[:, head_cols(j, mine)] = att_own[:, cols]
        att[:, head_cols(j, 1 - mine)] = att_back[:, cols]
        dq[:, head_cols(j, mine)] = dq_own[:, cols]
        dq[:, head_cols(j, 1 - mine)] = dq_back[:, cols]
    out[...] = dot(att[...], w[...], 1, 0).astype(BF16)


def finish_queries(att_own, att_back, dq_own, dq_back, w):
    tokens = att_own.shape[0]
    return call(
        query_kernel,
        (shape_of(tokens, w.shape[1]), shape_of(tokens, w.shape[0])),
        [VMEM] * 5,
        "finish_queries",
        scratch=[pltpu.VMEM((tokens, w.shape[0]), BF16)],
    )(att_own, att_back, dq_own, dq_back, w)


def returned_kernel(d_par, far_a, far_b, total):
    slot = far_slot(lax.axis_index("seq"))
    returned = jnp.where(slot == 0, far_b[...].astype(F32), far_a[...].astype(F32))
    total[...] = (d_par[...].astype(F32) + returned).astype(BF16)


def add_returned(d_par, far):
    return call(
        returned_kernel, (shape_of(*d_par.shape),), [VMEM] * 3, "add_returned"
    )(d_par, *far)[0]


def key_kernel(own, far_a, far_b, home, keep, out, dk, dv, total):
    mine = lax.axis_index("seq") & 1
    slot = far_slot(lax.axis_index("seq"))
    tokens = dk.shape[0]
    for i, target in ((0, dk), (1, dv)):
        rows = slice(i * tokens, (i + 1) * tokens)
        for j in range(own.shape[1] // HD):
            cols = slice(j * HD, (j + 1) * HD)
            far = jnp.where(slot == 0, far_a[rows, cols].astype(F32), far_b[rows, cols].astype(F32))
            target[:, head_cols(j, mine)] = (own[rows, cols].astype(F32) + far).astype(BF16)
            target[:, head_cols(j, 1 - mine)] = home[rows, cols]
    total[...] = keep[...] + out[...].astype(F32)


def finish_keys(own, far, home, keep, out):
    tokens, half = own.shape[0] // 2, own.shape[1]
    return call(
        key_kernel,
        (shape_of(tokens, 2 * half),) * 2 + (shape_of(*keep.shape, dtype=F32),),
        [VMEM] * 6,
        "finish_keys",
    )(own, *far, home, keep, out)


def on_device(queries, key_states, values, w_out, cotangent, neighbours, counts):
    n_seq, n_dp = lax.axis_size("seq"), lax.axis_size("dp")
    cot = cotangent[0]

    swap = [(i, i ^ 1) for i in range(n_seq)]
    relay = [(i, i + 2) for i in range(0, n_seq, 2) if i + 2 < n_seq]
    relay += [(i, i - 2) for i in range(1, n_seq, 2) if i - 2 >= 0]
    outer = [(b, a) for a, b in relay]
    edges = [[], []]
    for i in range(n_seq):
        edges[1].append((i, i ^ 2))
        other = i + 2 if (i >> 1) & 1 else i - 2
        if 0 <= other < n_seq:
            edges[0].append((i, other))
    send = lambda x, pairs: lax.ppermute(x, "seq", pairs)
    across = lambda x, k: lax.ppermute(x, "dp", [(i, i ^ k) for i in range(n_dp)])

    kv_send, own, q_send, q_own = pack(
        neighbours[0], queries[0], key_states[0], values[0]
    )
    par = send(kv_send, swap)
    q_par = send(q_send, swap)
    far_par = send(own, outer)
    cot_par = send(cot, swap)
    far_own = send(par, relay)
    core_own, core_par = across(cot, 1), across(cot_par, 1)
    ga = grad_attended(cot, cot_par, w_out)

    inputs = (q_own, q_par, own, par, far_own, far_par)
    probs, att_own, att_back, att_t, step = forward(
        inputs, ga, n_seq, n_dp
    )
    att_core = across(att_t[1], 1)
    att_back = send(att_back, swap)
    grads, *leaving = backward(inputs, ga, probs)
    operands = (att_t[0], att_core, cot, cot_par, core_own, core_par)
    out = weight_terms(False, operands, leaving[0])
    keep = weight_terms(True, operands, out)
    far = [send(leaving[i], edges[i]) for i in range(2)]
    dq_own, dq_back, d_own, d_par = gradients(inputs, ga, probs, grads)
    dq_back = send(dq_back, swap)
    home = send(add_returned(d_par, far), swap)

    hops = []
    bit = 2
    while bit < n_dp:
        hops.append(("dp", n_dp, bit))
        bit *= 2
    while step < n_seq:
        hops.append(("seq", n_seq, step))
        step *= 2
    for place, (axis, count, bit) in enumerate(hops):
        out = lax.ppermute(out, axis, [(i, i ^ bit) for i in range(count)])
        if place == 0:
            out, d_own, att_back = lax.optimization_barrier((out, d_own, att_back))
        if place + 1 < len(hops):
            total = keep + out.astype(F32)
            rows = total.shape[0] // 2
            keep, out = total[:rows], total[rows:].astype(BF16)

    output, dq = finish_queries(att_own, att_back, dq_own, dq_back, w_out)
    dk, dv, total = finish_keys(d_own, far, home, keep, out)
    return (output[None], dq[None], dk[None], dv[None], total)


def solution(mesh):
    placed = (
        P("dp", "seq", None),
        P("dp", "seq", None),
        P("dp", "seq", None),
        P(),
        P("dp", "seq", None),
        P("dp", "seq", None),
        P("dp", "seq"),
    )
    return jax.shard_map(
        on_device,
        mesh=mesh,
        in_specs=placed,
        out_specs=(
            P("dp", "seq", None),
            P("dp", "seq", None),
            P("dp", "seq", None),
            P("dp", "seq", None),
            P(("seq", "dp"), None),
        ),
        check_vma=False,
    )
```

```python
import functools
import math

import jax
import jax.numpy as jnp
from jax import lax
from jax.experimental import pallas as pl
from jax.experimental.pallas import tpu as pltpu
from jax.sharding import PartitionSpec as P

HD = 128
VMEM_LIMIT = 12 * 1024 * 1024
F32 = jnp.float32
BF16 = jnp.bfloat16
VMEM = pl.BlockSpec(memory_space=pltpu.VMEM)
HBM = pl.BlockSpec(memory_space=pltpu.HBM)
ANY = pl.BlockSpec(memory_space=pl.ANY)
FLAG_ROWS = 16


def dot(a, b, ca, cb):
    return lax.dot_general(a, b, (((ca,), (cb,)), ((), ())), preferred_element_type=F32)


def bit_reversed(index, bits):
    out = 0
    for b in range(bits):
        out = out * 2 + ((index >> b) & 1)
    return out


def shape_of(*dims, dtype=BF16):
    return jax.ShapeDtypeStruct(dims, dtype)


def call(body, out_shape, in_specs, name, scratch=()):
    return pl.pallas_call(
        body,
        out_shape=out_shape,
        in_specs=in_specs,
        out_specs=(VMEM,) * len(out_shape),
        scratch_shapes=list(scratch),
        compiler_params=pltpu.CompilerParams(vmem_limit_bytes=VMEM_LIMIT),
        cost_estimate=pl.CostEstimate(flops=0, bytes_accessed=0, transcendentals=0),
        name=name,
    )


def head_cols(pair, parity):
    return pl.ds(pl.multiple_of((2 * pair + parity) * HD, HD), HD)


def listed_flags(me, listed):
    far_patch = jnp.where(me % 2 == 0, me - 1, me + 1)
    near, far = jnp.int32(0), jnp.int32(0)
    for slot in range(listed.shape[1]):
        near = jnp.where(listed[0, slot] == (me ^ 1), 1, near)
        far = jnp.where(listed[0, slot] == far_patch, 1, far)
    return near, far


def in_hbm(x):
    return pltpu.with_memory_space_constraint(x, pltpu.HBM)


def pack_kernel(listed, q, k, v, kv_send, kv_keep, q_send, q_keep, listed_in, sems):
    mine = lax.axis_index("seq") & 1
    tokens, half = q_keep.shape[0] - FLAG_ROWS, q_keep.shape[1]
    copies = []

    def copy(source, target):
        copies.append(pltpu.make_async_copy(source, target, sems.at[len(copies)]))
        copies[-1].start()

    copy(listed, listed_in)
    for kv, q_to, parity in ((kv_send, q_send, 1 - mine), (kv_keep, q_keep, mine)):
        for source, target, row in ((k, kv, 0), (v, kv, tokens), (q, q_to, 0)):
            for j in range(half // HD):
                copy(
                    source.at[:, head_cols(j, parity)],
                    target.at[row : row + tokens, j * HD : (j + 1) * HD],
                )
    copies[0].wait()
    near, far = listed_flags(lax.axis_index("seq"), listed_in)
    left = lax.broadcasted_iota(jnp.int32, (FLAG_ROWS, half), 1) < half // 2
    flags = jnp.where(left, near, far).astype(F32).astype(BF16)
    q_send[tokens : tokens + FLAG_ROWS, :] = flags
    q_keep[tokens : tokens + FLAG_ROWS, :] = flags
    for item in copies[1:]:
        item.wait()


def pack(listed, q, k, v):
    tokens, features = k.shape
    half = features // 2
    kv = shape_of(2 * tokens, half)
    return call(
        pack_kernel,
        (kv, kv) + (shape_of(tokens + FLAG_ROWS, half),) * 2,
        [HBM] * 4,
        "pack_heads",
        scratch=[
            pltpu.SMEM(listed.shape, jnp.int32),
            pltpu.SemaphoreType.DMA((3 * features // HD + 1,)),
        ],
    )(*[in_hbm(x) for x in (listed, q, k, v)])


def turn_kernel(cot, cot_par, w, ga, cot_in, w_in, sems):
    tokens = cot.shape[0]
    pairs = ga.shape[1] // HD
    copies = [pltpu.make_async_copy(cot, cot_in, sems.at[pairs])]
    for j in range(pairs):
        rows = w.at[head_cols(j, lax.axis_index("seq") & 1), :]
        copies.append(pltpu.make_async_copy(rows, w_in.at[j], sems.at[j]))
    for item in copies:
        item.start()
    copies[0].wait()
    for j in range(pairs):
        cols = slice(j * HD, (j + 1) * HD)
        copies[j + 1].wait()
        ga[:tokens, cols] = dot(cot_in[...], w_in[j], 1, 1).astype(BF16)
        ga[tokens:, cols] = dot(cot_par[...], w_in[j], 1, 1).astype(BF16)


def grad_attended(cot, cot_par, w):
    tokens, width = cot.shape
    pairs = w.shape[0] // (2 * HD)
    return call(
        turn_kernel,
        (shape_of(2 * tokens, pairs * HD),),
        [HBM, VMEM, HBM],
        "grad_attended",
        scratch=[
            pltpu.VMEM((tokens, width), BF16),
            pltpu.VMEM((pairs, HD, width), BF16),
            pltpu.SemaphoreType.DMA((pairs + 1,)),
        ],
    )(in_hbm(cot), cot_par, in_hbm(w))[0]


def far_slot(me):
    return (me & 1) ^ ((me >> 1) & 1)


def forward_kernel(
    direct, n_dp, q_own, q_par, own, par, far_own, far_par, after,
    probs, att_own, att_back, att_t,
):
    rate = math.log2(math.e) / math.sqrt(HD)
    tokens, half = q_own.shape[0] - FLAG_ROWS, q_own.shape[1]
    pairs = half // HD
    me = lax.axis_index("seq")
    left = lax.broadcasted_iota(jnp.int32, (1, 2 * tokens), 1) < tokens

    def barred(x, place):
        flag = x[tokens : tokens + FLAG_ROWS, :].astype(F32)[:1, place : place + 1]
        return jnp.where(jnp.broadcast_to(flag, (1, 2 * tokens)) > 0, 0.0, -jnp.inf)

    bias = (
        jnp.where(left, 0.0, barred(q_par, 0)),
        jnp.where(left, barred(q_own, 0), 0.0),
        jnp.where(left, barred(q_own, half - 1), barred(q_par, half - 1)),
    )
    for j in range(pairs):
        cols = slice(j * HD, (j + 1) * HD)
        qo, qp = q_own[:tokens, cols], q_par[:tokens, cols]
        q = jnp.concatenate([qo, qp], axis=0)
        k = jnp.concatenate([own[:tokens, cols], par[:tokens, cols]], axis=0)
        v = jnp.concatenate([own[tokens:, cols], par[tokens:, cols]], axis=0)
        near = dot(k, q, 1, 1)
        far = jnp.concatenate(
            [dot(far_own[:tokens, cols], qo, 1, 1), dot(far_par[:tokens, cols], qp, 1, 1)], axis=1
        )
        s = [near[:tokens] + bias[0], near[tokens:] + bias[1], far + bias[2]]
        top = jnp.max(jnp.maximum(jnp.maximum(s[0], s[1]), s[2]), axis=0, keepdims=True)
        e = [jnp.exp2((x - top) * rate) for x in s]
        inv = 1.0 / jnp.sum(e[0] + e[1] + e[2], axis=0, keepdims=True)
        low = [(x * inv).astype(BF16) for x in e]
        for i in range(3):
            probs[j, i * tokens : (i + 1) * tokens, :] = low[i]
        vfo, vfp = far_own[tokens:, cols], far_par[tokens:, cols]
        o_t = dot(v, jnp.concatenate(low[:2], axis=0), 0, 0)
        o_t += jnp.concatenate(
            [dot(vfo, low[2][:, :tokens], 0, 0), dot(vfp, low[2][:, tokens:], 0, 0)], axis=1
        )
        o = o_t.T.astype(BF16)
        att_own[:, cols] = o[:tokens]
        att_back[:, cols] = o[tokens:]
        o_low = o_t.astype(BF16)
        if direct:
            rows = HD // n_dp
            place = bit_reversed(j ^ (me >> 1), (pairs - 1).bit_length())
            for d in range(n_dp):
                block = bit_reversed((d ^ lax.axis_index("dp")) >> 1, (n_dp // 2 - 1).bit_length())
                start = pl.multiple_of((block * pairs + place) * rows, rows)
                att_t[(d ^ lax.axis_index("dp")) & 1, pl.ds(start, rows), :] = o_low[d * rows : (d + 1) * rows, :]
        else:
            att_t[cols, :] = o_low


def forward(inputs, after, n_seq, n_dp):
    tokens, half = inputs[0].shape[0] - FLAG_ROWS, inputs[0].shape[1]
    features = 2 * half
    heads, pairs = features // HD, half // HD
    direct = n_seq == heads and HD % n_dp == 0 and (HD // n_dp) % 16 == 0
    one = shape_of(tokens, half)
    turned = shape_of(2, half // 2, 2 * tokens) if direct else shape_of(half, 2 * tokens)
    probs, att_own, att_back, turned = call(
        functools.partial(forward_kernel, direct, n_dp),
        (shape_of(pairs, 3 * tokens, 2 * tokens), one, one, turned),
        [VMEM] * 6 + [ANY],
        "patch_forward",
    )(*inputs, after)
    if not direct:
        here = lax.axis_index("seq")
        bits, d_bits = (n_seq - 1).bit_length(), (n_dp // 2 - 1).bit_length()
        order = jnp.array([bit_reversed(i, bits) for i in range(n_seq)], jnp.int32) ^ here
        d_order = [bit_reversed(i, d_bits) * 2 + c for c in range(2) for i in range(n_dp // 2)]
        full = jnp.zeros((heads // 2, 2, HD, 2 * tokens), BF16)
        full = lax.dynamic_update_slice(
            full, turned.reshape(heads // 2, 1, HD, 2 * tokens), (0, here & 1, 0, 0)
        )
        full = full.reshape(n_seq, n_dp, features // (n_seq * n_dp), 2 * tokens)
        full = jnp.take(full, order, axis=0)
        full = jnp.take(full, jnp.array(d_order, jnp.int32) ^ lax.axis_index("dp"), axis=1).transpose(1, 0, 2, 3)
        turned = full.reshape(2, features // 2, 2 * tokens)
    return probs, att_own, att_back, turned, 2 if direct else 1


def backward_kernel(
    q_own, q_par, own, par, far_own, far_par, ga, probs, grads, edge_a_v, edge_b_v, edge_a_k, edge_b_k
):
    scale = 1.0 / math.sqrt(HD)
    tokens, half = q_own.shape[0] - FLAG_ROWS, q_own.shape[1]
    slot = far_slot(lax.axis_index("seq"))
    last = slice(2 * tokens, 3 * tokens)
    for j in range(half // HD):
        cols = slice(j * HD, (j + 1) * HD)
        g_both = ga[:, cols]
        go, gp = g_both[:tokens], g_both[tokens:]
        qo, qp = q_own[:tokens, cols], q_par[:tokens, cols]
        v = jnp.concatenate([own[tokens:, cols], par[tokens:, cols]], axis=0)
        vfo, vfp = far_own[tokens:, cols], far_par[tokens:, cols]
        gn = dot(v, g_both, 1, 1)
        g = [
            gn[:tokens],
            gn[tokens:],
            jnp.concatenate([dot(vfo, go, 1, 1), dot(vfp, gp, 1, 1)], axis=1),
        ]
        p = [probs[j, i * tokens : (i + 1) * tokens, :].astype(F32) for i in range(3)]
        delta = jnp.sum(p[0] * g[0] + p[1] * g[1] + p[2] * g[2], axis=0, keepdims=True)
        ds = [(p[i] * (g[i] - delta)).astype(BF16) for i in range(3)]
        for i in range(3):
            grads[j, i * tokens : (i + 1) * tokens, :] = ds[i]
        dfo, dfp = ds[2][:, :tokens], ds[2][:, tokens:]
        far_v = (dot(probs[j, last, :tokens], go, 1, 0), dot(probs[j, last, tokens:], gp, 1, 0))
        far_k = (dot(dfo, qo, 1, 0) * scale, dot(dfp, qp, 1, 0) * scale)
        for (mine, theirs), edge_a, edge_b in ((far_v, edge_a_v, edge_b_v), (far_k, edge_a_k, edge_b_k)):
            mine, theirs = mine.astype(BF16), theirs.astype(BF16)
            edge_a[:, cols] = jnp.where(slot == 0, mine, theirs)
            edge_b[:, cols] = jnp.where(slot == 0, theirs, mine)


def backward(inputs, ga, probs):
    tokens, half = inputs[0].shape[0] - FLAG_ROWS, inputs[0].shape[1]
    return call(
        backward_kernel,
        (shape_of(*probs.shape),) + (shape_of(tokens, half),) * 4,
        [VMEM] * 8,
        "patch_backward",
    )(*inputs, ga, probs)


def gradient_kernel(
    q_own, q_par, own, par, far_own, far_par, ga, probs, grads, dq_own, dq_back, d_own, d_par_k, d_par_v
):
    scale = 1.0 / math.sqrt(HD)
    tokens, half = q_own.shape[0] - FLAG_ROWS, q_own.shape[1]
    near, last = slice(0, 2 * tokens), slice(2 * tokens, 3 * tokens)
    for j in range(half // HD):
        cols = slice(j * HD, (j + 1) * HD)
        q = jnp.concatenate([q_own[:tokens, cols], q_par[:tokens, cols]], axis=0)
        k = jnp.concatenate([own[:tokens, cols], par[:tokens, cols]], axis=0)
        kfo, kfp = far_own[:tokens, cols], far_par[:tokens, cols]
        low, dsn = probs[j, near, :], grads[j, near, :]
        dfo, dfp = grads[j, last, :tokens], grads[j, last, tokens:]
        dq = dot(dsn, k, 0, 0) + jnp.concatenate([dot(dfo, kfo, 0, 0), dot(dfp, kfp, 0, 0)], axis=0)
        dq = (dq * scale).astype(BF16)
        dq_own[:, cols] = dq[:tokens]
        dq_back[:, cols] = dq[tokens:]
        dk = (dot(dsn, q, 1, 0) * scale).astype(BF16)
        dv = dot(low, ga[:, cols], 1, 0).astype(BF16)
        d_own[:tokens, cols] = dk[:tokens]
        d_par_k[:, cols] = dk[tokens:]
        d_own[tokens:, cols] = dv[:tokens]
        d_par_v[:, cols] = dv[tokens:]


def gradients(inputs, ga, probs, grads):
    tokens, half = inputs[0].shape[0] - FLAG_ROWS, inputs[0].shape[1]
    one, kv = shape_of(tokens, half), shape_of(2 * tokens, half)
    return call(
        gradient_kernel, (one, one, kv, one, one), [VMEM] * 9, "patch_gradients"
    )(*inputs, ga, probs, grads)


def weight_kernel(kept, att_keep, att_core, own, par, core_own, core_par, _after, target):
    size = target.shape[0]
    tokens = own.shape[0]
    rows = slice(0, size) if kept else slice(size, 2 * size)
    total = dot(att_keep[rows, :tokens], own[...], 1, 0)
    total += dot(att_keep[rows, tokens:], par[...], 1, 0)
    total += dot(att_core[rows, :tokens], core_own[...], 1, 0)
    total += dot(att_core[rows, tokens:], core_par[...], 1, 0)
    target[...] = total.astype(target.dtype)


def weight_terms(kept, operands, after):
    rows, width = operands[0].shape[0] // 2, operands[2].shape[1]
    return call(
        functools.partial(weight_kernel, kept),
        (shape_of(rows, width, dtype=F32 if kept else BF16),),
        [VMEM] * 6 + [ANY],
        "weight_terms_kept" if kept else "weight_terms_sent",
    )(*operands, after)[0]


def query_kernel(att_own, att_back, dq_own, dq_back, w, out, dq, att):
    mine = lax.axis_index("seq") & 1
    for j in range(att_own.shape[1] // HD):
        cols = slice(j * HD, (j + 1) * HD)
        att[:, head_cols(j, mine)] = att_own[:, cols]
        att[:, head_cols(j, 1 - mine)] = att_back[:, cols]
        dq[:, head_cols(j, mine)] = dq_own[:, cols]
        dq[:, head_cols(j, 1 - mine)] = dq_back[:, cols]
    out[...] = dot(att[...], w[...], 1, 0).astype(BF16)


def finish_queries(att_own, att_back, dq_own, dq_back, w):
    tokens = att_own.shape[0]
    return call(
        query_kernel,
        (shape_of(tokens, w.shape[1]), shape_of(tokens, w.shape[0])),
        [VMEM] * 5,
        "finish_queries",
        scratch=[pltpu.VMEM((tokens, w.shape[0]), BF16)],
    )(att_own, att_back, dq_own, dq_back, w)


def returned_kernel(d_par, far_a, far_b, _after, total):
    slot = far_slot(lax.axis_index("seq"))
    returned = jnp.where(slot == 0, far_b[...].astype(F32), far_a[...].astype(F32))
    total[...] = (d_par[...].astype(F32) + returned).astype(BF16)


def add_returned(d_par, far, after):
    return call(
        returned_kernel, (shape_of(*d_par.shape),), [VMEM] * 3 + [ANY], "add_returned"
    )(d_par, *far, after)[0]


def key_kernel(own, a_v, b_v, a_k, b_k, home_k, home_v, keep, out, dk, dv, total):
    mine = lax.axis_index("seq") & 1
    slot = far_slot(lax.axis_index("seq"))
    tokens = dk.shape[0]
    for i, far_a, far_b, home, target in ((0, a_k, b_k, home_k, dk), (1, a_v, b_v, home_v, dv)):
        rows = slice(i * tokens, (i + 1) * tokens)
        for j in range(own.shape[1] // HD):
            cols = slice(j * HD, (j + 1) * HD)
            far = jnp.where(slot == 0, far_a[:, cols].astype(F32), far_b[:, cols].astype(F32))
            target[:, head_cols(j, mine)] = (own[rows, cols].astype(F32) + far).astype(BF16)
            target[:, head_cols(j, 1 - mine)] = home[:, cols]
    total[...] = keep[...] + out[...].astype(F32)


def finish_keys(own, far, home, keep, out):
    tokens, half = own.shape[0] // 2, own.shape[1]
    return call(
        key_kernel,
        (shape_of(tokens, 2 * half),) * 2 + (shape_of(*keep.shape, dtype=F32),),
        [VMEM] * 9,
        "finish_keys",
    )(own, *far, *home, keep, out)


def on_device(queries, key_states, values, w_out, cotangent, neighbours, counts):
    n_seq, n_dp = lax.axis_size("seq"), lax.axis_size("dp")
    cot = cotangent[0]

    swap = [(i, i ^ 1) for i in range(n_seq)]
    relay = [(i, i + 2) for i in range(0, n_seq, 2) if i + 2 < n_seq]
    relay += [(i, i - 2) for i in range(1, n_seq, 2) if i - 2 >= 0]
    outer = [(b, a) for a, b in relay]
    edges = [[], []]
    for i in range(n_seq):
        edges[1].append((i, i ^ 2))
        other = i + 2 if (i >> 1) & 1 else i - 2
        if 0 <= other < n_seq:
            edges[0].append((i, other))
    send = lambda x, pairs: lax.ppermute(x, "seq", pairs)
    across = lambda x, k: lax.ppermute(x, "dp", [(i, i ^ k) for i in range(n_dp)])

    kv_send, own, q_send, q_own = pack(
        neighbours[0], queries[0], key_states[0], values[0]
    )
    par = send(kv_send, swap)
    q_par = send(q_send, swap)
    far_par = send(own, outer)
    cot_par = send(cot, swap)
    far_own = send(par, relay)
    core_own, core_par = across(cot, 1), across(cot_par, 1)
    ga = grad_attended(cot, cot_par, w_out)

    inputs = (q_own, q_par, own, par, far_own, far_par)
    probs, att_own, att_back, att_t, step = forward(
        inputs, ga, n_seq, n_dp
    )
    att_core = across(att_t[1], 1)
    att_back = send(att_back, swap)
    grads, *leaving = backward(inputs, ga, probs)
    operands = (att_t[0], att_core, cot, cot_par, core_own, core_par)
    out = weight_terms(False, operands, leaving[0])
    keep = weight_terms(True, operands, out)
    far = [send(leaving[i], edges[i % 2]) for i in range(4)]
    dq_own, dq_back, d_own, d_par_k, d_par_v = gradients(inputs, ga, probs, grads)
    dq_back = send(dq_back, swap)
    sum_v = add_returned(d_par_v, far[:2], d_par_v)
    sum_k = add_returned(d_par_k, far[2:], sum_v)
    home_v, home_k = send(sum_v, swap), send(sum_k, swap)

    hops = []
    bit = 2
    while bit < n_dp:
        hops.append(("dp", n_dp, bit))
        bit *= 2
    while step < n_seq:
        hops.append(("seq", n_seq, step))
        step *= 2
    for place, (axis, count, bit) in enumerate(hops):
        out = lax.ppermute(out, axis, [(i, i ^ bit) for i in range(count)])
        if place == 0:
            out, d_own, att_back = lax.optimization_barrier((out, d_own, att_back))
        if place + 1 < len(hops):
            total = keep + out.astype(F32)
            rows = total.shape[0] // 2
            keep, out = total[:rows], total[rows:].astype(BF16)

    output, dq = finish_queries(att_own, att_back, dq_own, dq_back, w_out)
    dk, dv, total = finish_keys(d_own, far, (home_k, home_v), keep, out)
    return (output[None], dq[None], dk[None], dv[None], total)


def solution(mesh):
    placed = (
        P("dp", "seq", None),
        P("dp", "seq", None),
        P("dp", "seq", None),
        P(),
        P("dp", "seq", None),
        P("dp", "seq", None),
        P("dp", "seq"),
    )
    return jax.shard_map(
        on_device,
        mesh=mesh,
        in_specs=placed,
        out_specs=(
            P("dp", "seq", None),
            P("dp", "seq", None),
            P("dp", "seq", None),
            P("dp", "seq", None),
            P(("seq", "dp"), None),
        ),
        check_vma=False,
    )
```

```python
import functools
import math

import jax
import jax.numpy as jnp
from jax import lax
from jax.experimental import pallas as pl
from jax.experimental.pallas import tpu as pltpu
from jax.sharding import PartitionSpec as P

HD = 128
VMEM_LIMIT = 12 * 1024 * 1024
F32 = jnp.float32
BF16 = jnp.bfloat16
VMEM = pl.BlockSpec(memory_space=pltpu.VMEM)
HBM = pl.BlockSpec(memory_space=pltpu.HBM)
ANY = pl.BlockSpec(memory_space=pl.ANY)
FLAG_ROWS = 16


def dot(a, b, ca, cb):
    return lax.dot_general(a, b, (((ca,), (cb,)), ((), ())), preferred_element_type=F32)


def bit_reversed(index, bits):
    out = 0
    for b in range(bits):
        out = out * 2 + ((index >> b) & 1)
    return out


def shape_of(*dims, dtype=BF16):
    return jax.ShapeDtypeStruct(dims, dtype)


def call(body, out_shape, in_specs, name, scratch=()):
    return pl.pallas_call(
        body,
        out_shape=out_shape,
        in_specs=in_specs,
        out_specs=(VMEM,) * len(out_shape),
        scratch_shapes=list(scratch),
        compiler_params=pltpu.CompilerParams(vmem_limit_bytes=VMEM_LIMIT),
        cost_estimate=pl.CostEstimate(flops=0, bytes_accessed=0, transcendentals=0),
        name=name,
    )


def head_cols(pair, parity):
    return pl.ds(pl.multiple_of((2 * pair + parity) * HD, HD), HD)


def listed_flags(me, listed):
    far_patch = jnp.where(me % 2 == 0, me - 1, me + 1)
    near, far = jnp.int32(0), jnp.int32(0)
    for slot in range(listed.shape[1]):
        near = jnp.where(listed[0, slot] == (me ^ 1), 1, near)
        far = jnp.where(listed[0, slot] == far_patch, 1, far)
    return near, far


def in_hbm(x):
    return pltpu.with_memory_space_constraint(x, pltpu.HBM)


def pack_kernel(listed, q, k, v, kv_send, kv_keep, q_send, q_keep, listed_in, sems):
    mine = lax.axis_index("seq") & 1
    tokens, half = q_keep.shape[0] - FLAG_ROWS, q_keep.shape[1]
    copies = []

    def copy(source, target):
        copies.append(pltpu.make_async_copy(source, target, sems.at[len(copies)]))
        copies[-1].start()

    copy(listed, listed_in)
    for kv, q_to, parity in ((kv_send, q_send, 1 - mine), (kv_keep, q_keep, mine)):
        for source, target, row in ((k, kv, 0), (v, kv, tokens), (q, q_to, 0)):
            for j in range(half // HD):
                copy(
                    source.at[:, head_cols(j, parity)],
                    target.at[row : row + tokens, j * HD : (j + 1) * HD],
                )
    copies[0].wait()
    near, far = listed_flags(lax.axis_index("seq"), listed_in)
    left = lax.broadcasted_iota(jnp.int32, (FLAG_ROWS, half), 1) < half // 2
    flags = jnp.where(left, near, far).astype(F32).astype(BF16)
    q_send[tokens : tokens + FLAG_ROWS, :] = flags
    q_keep[tokens : tokens + FLAG_ROWS, :] = flags
    for item in copies[1:]:
        item.wait()


def pack(listed, q, k, v):
    tokens, features = k.shape
    half = features // 2
    kv = shape_of(2 * tokens, half)
    return call(
        pack_kernel,
        (kv, kv) + (shape_of(tokens + FLAG_ROWS, half),) * 2,
        [HBM] * 4,
        "pack_heads",
        scratch=[
            pltpu.SMEM(listed.shape, jnp.int32),
            pltpu.SemaphoreType.DMA((3 * features // HD + 1,)),
        ],
    )(*[in_hbm(x) for x in (listed, q, k, v)])


def turn_kernel(cot, cot_par, w, ga, cot_in, w_in, sems):
    tokens = cot.shape[0]
    pairs = ga.shape[1] // HD
    copies = [pltpu.make_async_copy(cot, cot_in, sems.at[pairs])]
    for j in range(pairs):
        rows = w.at[head_cols(j, lax.axis_index("seq") & 1), :]
        copies.append(pltpu.make_async_copy(rows, w_in.at[j], sems.at[j]))
    for item in copies:
        item.start()
    copies[0].wait()
    for j in range(pairs):
        cols = slice(j * HD, (j + 1) * HD)
        copies[j + 1].wait()
        ga[:tokens, cols] = dot(cot_in[...], w_in[j], 1, 1).astype(BF16)
        ga[tokens:, cols] = dot(cot_par[...], w_in[j], 1, 1).astype(BF16)


def grad_attended(cot, cot_par, w):
    tokens, width = cot.shape
    pairs = w.shape[0] // (2 * HD)
    return call(
        turn_kernel,
        (shape_of(2 * tokens, pairs * HD),),
        [HBM, VMEM, HBM],
        "grad_attended",
        scratch=[
            pltpu.VMEM((tokens, width), BF16),
            pltpu.VMEM((pairs, HD, width), BF16),
            pltpu.SemaphoreType.DMA((pairs + 1,)),
        ],
    )(in_hbm(cot), cot_par, in_hbm(w))[0]


def far_slot(me):
    return (me & 1) ^ ((me >> 1) & 1)


def forward_kernel(
    direct, n_dp, q_own, q_par, own, par, far_own, far_par, after,
    probs, att_own, att_back, att_t,
):
    rate = math.log2(math.e) / math.sqrt(HD)
    tokens, half = q_own.shape[0] - FLAG_ROWS, q_own.shape[1]
    pairs = half // HD
    me = lax.axis_index("seq")
    left = lax.broadcasted_iota(jnp.int32, (1, 2 * tokens), 1) < tokens

    def barred(x, place):
        flag = x[tokens : tokens + FLAG_ROWS, :].astype(F32)[:1, place : place + 1]
        return jnp.where(jnp.broadcast_to(flag, (1, 2 * tokens)) > 0, 0.0, -jnp.inf)

    bias = (
        jnp.where(left, 0.0, barred(q_par, 0)),
        jnp.where(left, barred(q_own, 0), 0.0),
        jnp.where(left, barred(q_own, half - 1), barred(q_par, half - 1)),
    )
    for j in range(pairs):
        cols = slice(j * HD, (j + 1) * HD)
        qo, qp = q_own[:tokens, cols], q_par[:tokens, cols]
        q = jnp.concatenate([qo, qp], axis=0)
        k = jnp.concatenate([own[:tokens, cols], par[:tokens, cols]], axis=0)
        v = jnp.concatenate([own[tokens:, cols], par[tokens:, cols]], axis=0)
        near = dot(k, q, 1, 1)
        far = jnp.concatenate(
            [dot(far_own[:tokens, cols], qo, 1, 1), dot(far_par[:tokens, cols], qp, 1, 1)], axis=1
        )
        s = [near[:tokens] + bias[0], near[tokens:] + bias[1], far + bias[2]]
        top = jnp.max(jnp.maximum(jnp.maximum(s[0], s[1]), s[2]), axis=0, keepdims=True)
        e = [jnp.exp2((x - top) * rate) for x in s]
        inv = 1.0 / jnp.sum(e[0] + e[1] + e[2], axis=0, keepdims=True)
        low = [(x * inv).astype(BF16) for x in e]
        for i in range(3):
            probs[j, i * tokens : (i + 1) * tokens, :] = low[i]
        vfo, vfp = far_own[tokens:, cols], far_par[tokens:, cols]
        o_t = dot(v, jnp.concatenate(low[:2], axis=0), 0, 0)
        o_t += jnp.concatenate(
            [dot(vfo, low[2][:, :tokens], 0, 0), dot(vfp, low[2][:, tokens:], 0, 0)], axis=1
        )
        o = o_t.T.astype(BF16)
        att_own[:, cols] = o[:tokens]
        att_back[:, cols] = o[tokens:]
        o_low = o_t.astype(BF16)
        if direct:
            rows = HD // n_dp
            place = bit_reversed(j ^ (me >> 1), (pairs - 1).bit_length())
            for d in range(n_dp):
                block = bit_reversed((d ^ lax.axis_index("dp")) >> 1, (n_dp // 2 - 1).bit_length())
                start = pl.multiple_of((block * pairs + place) * rows, rows)
                att_t[(d ^ lax.axis_index("dp")) & 1, pl.ds(start, rows), :] = o_low[d * rows : (d + 1) * rows, :]
        else:
            att_t[cols, :] = o_low


def forward(inputs, after, n_seq, n_dp):
    tokens, half = inputs[0].shape[0] - FLAG_ROWS, inputs[0].shape[1]
    features = 2 * half
    heads, pairs = features // HD, half // HD
    direct = n_seq == heads and HD % n_dp == 0 and (HD // n_dp) % 16 == 0
    one = shape_of(tokens, half)
    turned = shape_of(2, half // 2, 2 * tokens) if direct else shape_of(half, 2 * tokens)
    probs, att_own, att_back, turned = call(
        functools.partial(forward_kernel, direct, n_dp),
        (shape_of(pairs, 3 * tokens, 2 * tokens), one, one, turned),
        [VMEM] * 6 + [ANY],
        "patch_forward",
    )(*inputs, after)
    if not direct:
        here = lax.axis_index("seq")
        bits, d_bits = (n_seq - 1).bit_length(), (n_dp // 2 - 1).bit_length()
        order = jnp.array([bit_reversed(i, bits) for i in range(n_seq)], jnp.int32) ^ here
        d_order = [bit_reversed(i, d_bits) * 2 + c for c in range(2) for i in range(n_dp // 2)]
        full = jnp.zeros((heads // 2, 2, HD, 2 * tokens), BF16)
        full = lax.dynamic_update_slice(
            full, turned.reshape(heads // 2, 1, HD, 2 * tokens), (0, here & 1, 0, 0)
        )
        full = full.reshape(n_seq, n_dp, features // (n_seq * n_dp), 2 * tokens)
        full = jnp.take(full, order, axis=0)
        full = jnp.take(full, jnp.array(d_order, jnp.int32) ^ lax.axis_index("dp"), axis=1).transpose(1, 0, 2, 3)
        turned = full.reshape(2, features // 2, 2 * tokens)
    return probs, att_own, att_back, turned, 2 if direct else 1


def backward_kernel(
    q_own, q_par, own, par, far_own, far_par, ga, probs, grads, edge_a, edge_b
):
    scale = 1.0 / math.sqrt(HD)
    tokens, half = q_own.shape[0] - FLAG_ROWS, q_own.shape[1]
    slot = far_slot(lax.axis_index("seq"))
    last = slice(2 * tokens, 3 * tokens)
    for j in range(half // HD):
        cols = slice(j * HD, (j + 1) * HD)
        g_both = ga[:, cols]
        go, gp = g_both[:tokens], g_both[tokens:]
        qo, qp = q_own[:tokens, cols], q_par[:tokens, cols]
        v = jnp.concatenate([own[tokens:, cols], par[tokens:, cols]], axis=0)
        vfo, vfp = far_own[tokens:, cols], far_par[tokens:, cols]
        gn = dot(v, g_both, 1, 1)
        g = [
            gn[:tokens],
            gn[tokens:],
            jnp.concatenate([dot(vfo, go, 1, 1), dot(vfp, gp, 1, 1)], axis=1),
        ]
        p = [probs[j, i * tokens : (i + 1) * tokens, :].astype(F32) for i in range(3)]
        delta = jnp.sum(p[0] * g[0] + p[1] * g[1] + p[2] * g[2], axis=0, keepdims=True)
        ds = [(p[i] * (g[i] - delta)).astype(BF16) for i in range(3)]
        for i in range(3):
            grads[j, i * tokens : (i + 1) * tokens, :] = ds[i]
        dfo, dfp = ds[2][:, :tokens], ds[2][:, tokens:]
        own_far = jnp.concatenate(
            [dot(dfo, qo, 1, 0) * scale, dot(probs[j, last, :tokens], go, 1, 0)], axis=0
        ).astype(BF16)
        par_far = jnp.concatenate(
            [dot(dfp, qp, 1, 0) * scale, dot(probs[j, last, tokens:], gp, 1, 0)], axis=0
        ).astype(BF16)
        edge_a[:, cols] = jnp.where(slot == 0, own_far, par_far)
        edge_b[:, cols] = jnp.where(slot == 0, par_far, own_far)


def backward(inputs, ga, probs):
    tokens, half = inputs[0].shape[0] - FLAG_ROWS, inputs[0].shape[1]
    return call(
        backward_kernel,
        (shape_of(*probs.shape),) + (shape_of(2 * tokens, half),) * 2,
        [VMEM] * 8,
        "patch_backward",
    )(*inputs, ga, probs)


def gradient_kernel(
    q_own, q_par, own, par, far_own, far_par, ga, probs, grads, dq_own, dq_back, d_own, d_par
):
    scale = 1.0 / math.sqrt(HD)
    tokens, half = q_own.shape[0] - FLAG_ROWS, q_own.shape[1]
    near, last = slice(0, 2 * tokens), slice(2 * tokens, 3 * tokens)
    for j in range(half // HD):
        cols = slice(j * HD, (j + 1) * HD)
        q = jnp.concatenate([q_own[:tokens, cols], q_par[:tokens, cols]], axis=0)
        k = jnp.concatenate([own[:tokens, cols], par[:tokens, cols]], axis=0)
        kfo, kfp = far_own[:tokens, cols], far_par[:tokens, cols]
        low, dsn = probs[j, near, :], grads[j, near, :]
        dfo, dfp = grads[j, last, :tokens], grads[j, last, tokens:]
        dq = dot(dsn, k, 0, 0) + jnp.concatenate([dot(dfo, kfo, 0, 0), dot(dfp, kfp, 0, 0)], axis=0)
        dq = (dq * scale).astype(BF16)
        dq_own[:, cols] = dq[:tokens]
        dq_back[:, cols] = dq[tokens:]
        dk = (dot(dsn, q, 1, 0) * scale).astype(BF16)
        dv = dot(low, ga[:, cols], 1, 0).astype(BF16)
        d_own[:tokens, cols] = dk[:tokens]
        d_par[:tokens, cols] = dk[tokens:]
        d_own[tokens:, cols] = dv[:tokens]
        d_par[tokens:, cols] = dv[tokens:]


def gradients(inputs, ga, probs, grads):
    tokens, half = inputs[0].shape[0] - FLAG_ROWS, inputs[0].shape[1]
    one, kv = shape_of(tokens, half), shape_of(2 * tokens, half)
    return call(
        gradient_kernel, (one, one, kv, kv), [VMEM] * 9, "patch_gradients"
    )(*inputs, ga, probs, grads)


def weight_kernel(kept, att_keep, att_core, own, par, core_own, core_par, _after, target):
    size = target.shape[0]
    tokens = own.shape[0]
    rows = slice(0, size) if kept else slice(size, 2 * size)
    total = dot(att_keep[rows, :tokens], own[...], 1, 0)
    total += dot(att_keep[rows, tokens:], par[...], 1, 0)
    total += dot(att_core[rows, :tokens], core_own[...], 1, 0)
    total += dot(att_core[rows, tokens:], core_par[...], 1, 0)
    target[...] = total.astype(target.dtype)


def weight_terms(kept, operands, after):
    rows, width = operands[0].shape[0] // 2, operands[2].shape[1]
    return call(
        functools.partial(weight_kernel, kept),
        (shape_of(rows, width, dtype=F32 if kept else BF16),),
        [VMEM] * 6 + [ANY],
        "weight_terms_kept" if kept else "weight_terms_sent",
    )(*operands, after)[0]


def query_kernel(att_own, att_back, dq_own, dq_back, w, out, dq, att):
    mine = lax.axis_index("seq") & 1
    for j in range(att_own.shape[1] // HD):
        cols = slice(j * HD, (j + 1) * HD)
        att[:, head_cols(j, mine)] = att_own[:, cols]
        att[:, head_cols(j, 1 - mine)] = att_back[:, cols]
        dq[:, head_cols(j, mine)] = dq_own[:, cols]
        dq[:, head_cols(j, 1 - mine)] = dq_back[:, cols]
    out[...] = dot(att[...], w[...], 1, 0).astype(BF16)


def finish_queries(att_own, att_back, dq_own, dq_back, w):
    tokens = att_own.shape[0]
    return call(
        query_kernel,
        (shape_of(tokens, w.shape[1]), shape_of(tokens, w.shape[0])),
        [VMEM] * 5,
        "finish_queries",
        scratch=[pltpu.VMEM((tokens, w.shape[0]), BF16)],
    )(att_own, att_back, dq_own, dq_back, w)


def returned_kernel(d_par, far_a, far_b, total):
    slot = far_slot(lax.axis_index("seq"))
    returned = jnp.where(slot == 0, far_b[...].astype(F32), far_a[...].astype(F32))
    total[...] = (d_par[...].astype(F32) + returned).astype(BF16)


def add_returned(d_par, far):
    return call(
        returned_kernel, (shape_of(*d_par.shape),), [VMEM] * 3, "add_returned"
    )(d_par, *far)[0]


def column_copies(source, targets, parity, sems):
    tokens = targets[0].shape[0]
    copies = []
    for i, target in enumerate(targets):
        for j in range(source.shape[1] // HD):
            copies.append(
                pltpu.make_async_copy(
                    source.at[i * tokens : (i + 1) * tokens, j * HD : (j + 1) * HD],
                    target.at[:, head_cols(j, parity)],
                    sems.at[len(copies)],
                )
            )
            copies[-1].start()
    return copies


def own_kernel(own, far_a, far_b, dk, dv, total, sems):
    me = lax.axis_index("seq")
    far = jnp.where(far_slot(me) == 0, far_a[...].astype(F32), far_b[...].astype(F32))
    total[...] = (own[...].astype(F32) + far).astype(BF16)
    for item in column_copies(total, (dk, dv), me & 1, sems):
        item.wait()


def home_kernel(_dk, _dv, home, keep, out, dk, dv, total, sems):
    copies = column_copies(home, (dk, dv), 1 - (lax.axis_index("seq") & 1), sems)
    total[...] = keep[...] + out[...].astype(F32)
    for item in copies:
        item.wait()


def finish_keys(own, far, home, keep, out):
    tokens, half = own.shape[0] // 2, own.shape[1]
    params = pltpu.CompilerParams(vmem_limit_bytes=VMEM_LIMIT)
    sems = pltpu.SemaphoreType.DMA((2 * half // HD,))
    shapes = (shape_of(tokens, 2 * half),) * 2
    begun = pl.pallas_call(
        own_kernel,
        out_shape=shapes,
        in_specs=[VMEM] * 3,
        out_specs=(HBM, HBM),
        scratch_shapes=[pltpu.VMEM(own.shape, BF16), sems],
        compiler_params=params,
        name="finish_own_heads",
    )(own, *far)
    return pl.pallas_call(
        home_kernel,
        out_shape=shapes + (shape_of(*keep.shape, dtype=F32),),
        in_specs=[HBM, HBM] + [VMEM] * 3,
        out_specs=(HBM, HBM, VMEM),
        input_output_aliases={0: 0, 1: 1},
        scratch_shapes=[sems],
        compiler_params=params,
        name="finish_home_heads",
    )(*begun, home, keep, out)


def on_device(queries, key_states, values, w_out, cotangent, neighbours, counts):
    n_seq, n_dp = lax.axis_size("seq"), lax.axis_size("dp")
    cot = cotangent[0]

    swap = [(i, i ^ 1) for i in range(n_seq)]
    relay = [(i, i + 2) for i in range(0, n_seq, 2) if i + 2 < n_seq]
    relay += [(i, i - 2) for i in range(1, n_seq, 2) if i - 2 >= 0]
    outer = [(b, a) for a, b in relay]
    edges = [[], []]
    for i in range(n_seq):
        edges[1].append((i, i ^ 2))
        other = i + 2 if (i >> 1) & 1 else i - 2
        if 0 <= other < n_seq:
            edges[0].append((i, other))
    send = lambda x, pairs: lax.ppermute(x, "seq", pairs)
    across = lambda x, k: lax.ppermute(x, "dp", [(i, i ^ k) for i in range(n_dp)])

    kv_send, own, q_send, q_own = pack(
        neighbours[0], queries[0], key_states[0], values[0]
    )
    par = send(kv_send, swap)
    q_par = send(q_send, swap)
    far_par = send(own, outer)
    cot_par = send(cot, swap)
    far_own = send(par, relay)
    core_own, core_par = across(cot, 1), across(cot_par, 1)
    ga = grad_attended(cot, cot_par, w_out)

    inputs = (q_own, q_par, own, par, far_own, far_par)
    probs, att_own, att_back, att_t, step = forward(
        inputs, ga, n_seq, n_dp
    )
    att_core = across(att_t[1], 1)
    att_back = send(att_back, swap)
    grads, *leaving = backward(inputs, ga, probs)
    operands = (att_t[0], att_core, cot, cot_par, core_own, core_par)
    out = weight_terms(False, operands, leaving[0])
    keep = weight_terms(True, operands, out)
    far = [send(leaving[i], edges[i]) for i in range(2)]
    dq_own, dq_back, d_own, d_par = gradients(inputs, ga, probs, grads)
    dq_back = send(dq_back, swap)
    home = send(add_returned(d_par, far), swap)

    hops = []
    bit = 2
    while bit < n_dp:
        hops.append(("dp", n_dp, bit))
        bit *= 2
    while step < n_seq:
        hops.append(("seq", n_seq, step))
        step *= 2
    for place, (axis, count, bit) in enumerate(hops):
        out = lax.ppermute(out, axis, [(i, i ^ bit) for i in range(count)])
        if place == 0:
            out, d_own, att_back = lax.optimization_barrier((out, d_own, att_back))
        if place + 1 < len(hops):
            total = keep + out.astype(F32)
            rows = total.shape[0] // 2
            keep, out = total[:rows], total[rows:].astype(BF16)

    output, dq = finish_queries(att_own, att_back, dq_own, dq_back, w_out)
    dk, dv, total = finish_keys(d_own, far, home, keep, out)
    return (output[None], dq[None], dk[None], dv[None], total)


def solution(mesh):
    placed = (
        P("dp", "seq", None),
        P("dp", "seq", None),
        P("dp", "seq", None),
        P(),
        P("dp", "seq", None),
        P("dp", "seq", None),
        P("dp", "seq"),
    )
    return jax.shard_map(
        on_device,
        mesh=mesh,
        in_specs=placed,
        out_specs=(
            P("dp", "seq", None),
            P("dp", "seq", None),
            P("dp", "seq", None),
            P("dp", "seq", None),
            P(("seq", "dp"), None),
        ),
        check_vma=False,
    )
```

```python
import functools
import math

import jax
import jax.numpy as jnp
from jax import lax
from jax.experimental import pallas as pl
from jax.experimental.pallas import tpu as pltpu
from jax.sharding import PartitionSpec as P

HD = 128
VMEM_LIMIT = 12 * 1024 * 1024
F32 = jnp.float32
BF16 = jnp.bfloat16
VMEM = pl.BlockSpec(memory_space=pltpu.VMEM)
HBM = pl.BlockSpec(memory_space=pltpu.HBM)
ANY = pl.BlockSpec(memory_space=pl.ANY)
FLAG_ROWS = 16


def dot(a, b, ca, cb):
    return lax.dot_general(a, b, (((ca,), (cb,)), ((), ())), preferred_element_type=F32)


def bit_reversed(index, bits):
    out = 0
    for b in range(bits):
        out = out * 2 + ((index >> b) & 1)
    return out


def shape_of(*dims, dtype=BF16):
    return jax.ShapeDtypeStruct(dims, dtype)


def call(body, out_shape, in_specs, name, scratch=()):
    return pl.pallas_call(
        body,
        out_shape=out_shape,
        in_specs=in_specs,
        out_specs=(VMEM,) * len(out_shape),
        scratch_shapes=list(scratch),
        compiler_params=pltpu.CompilerParams(vmem_limit_bytes=VMEM_LIMIT),
        cost_estimate=pl.CostEstimate(flops=0, bytes_accessed=0, transcendentals=0),
        name=name,
    )


def head_cols(pair, parity):
    return pl.ds(pl.multiple_of((2 * pair + parity) * HD, HD), HD)


def listed_flags(me, listed):
    far_patch = jnp.where(me % 2 == 0, me - 1, me + 1)
    near, far = jnp.int32(0), jnp.int32(0)
    for slot in range(listed.shape[1]):
        near = jnp.where(listed[0, slot] == (me ^ 1), 1, near)
        far = jnp.where(listed[0, slot] == far_patch, 1, far)
    return near, far


def in_hbm(x):
    return pltpu.with_memory_space_constraint(x, pltpu.HBM)


def pack_kernel(listed, q, k, v, kv_send, kv_keep, q_send, q_keep, listed_in, sems):
    mine = lax.axis_index("seq") & 1
    tokens, half = q_keep.shape[0] - FLAG_ROWS, q_keep.shape[1]
    copies = []

    def copy(source, target):
        copies.append(pltpu.make_async_copy(source, target, sems.at[len(copies)]))
        copies[-1].start()

    copy(listed, listed_in)
    for kv, q_to, parity in ((kv_send, q_send, 1 - mine), (kv_keep, q_keep, mine)):
        for source, target, row in ((k, kv, 0), (v, kv, tokens), (q, q_to, 0)):
            for j in range(half // HD):
                copy(
                    source.at[:, head_cols(j, parity)],
                    target.at[row : row + tokens, j * HD : (j + 1) * HD],
                )
    copies[0].wait()
    near, far = listed_flags(lax.axis_index("seq"), listed_in)
    left = lax.broadcasted_iota(jnp.int32, (FLAG_ROWS, half), 1) < half // 2
    flags = jnp.where(left, near, far).astype(F32).astype(BF16)
    q_send[tokens : tokens + FLAG_ROWS, :] = flags
    q_keep[tokens : tokens + FLAG_ROWS, :] = flags
    for item in copies[1:]:
        item.wait()


def pack(listed, q, k, v):
    tokens, features = k.shape
    half = features // 2
    kv = shape_of(2 * tokens, half)
    return call(
        pack_kernel,
        (kv, kv) + (shape_of(tokens + FLAG_ROWS, half),) * 2,
        [HBM] * 4,
        "pack_heads",
        scratch=[
            pltpu.SMEM(listed.shape, jnp.int32),
            pltpu.SemaphoreType.DMA((3 * features // HD + 1,)),
        ],
    )(*[in_hbm(x) for x in (listed, q, k, v)])


def turn_kernel(cot, cot_par, w, ga, cot_in, w_in, sems):
    tokens = cot.shape[0]
    pairs = ga.shape[1] // HD
    copies = [pltpu.make_async_copy(cot, cot_in, sems.at[pairs])]
    for j in range(pairs):
        rows = w.at[head_cols(j, lax.axis_index("seq") & 1), :]
        copies.append(pltpu.make_async_copy(rows, w_in.at[j], sems.at[j]))
    for item in copies:
        item.start()
    copies[0].wait()
    for j in range(pairs):
        cols = slice(j * HD, (j + 1) * HD)
        copies[j + 1].wait()
        ga[:tokens, cols] = dot(cot_in[...], w_in[j], 1, 1).astype(BF16)
        ga[tokens:, cols] = dot(cot_par[...], w_in[j], 1, 1).astype(BF16)


def grad_attended(cot, cot_par, w):
    tokens, width = cot.shape
    pairs = w.shape[0] // (2 * HD)
    return call(
        turn_kernel,
        (shape_of(2 * tokens, pairs * HD),),
        [HBM, VMEM, HBM],
        "grad_attended",
        scratch=[
            pltpu.VMEM((tokens, width), BF16),
            pltpu.VMEM((pairs, HD, width), BF16),
            pltpu.SemaphoreType.DMA((pairs + 1,)),
        ],
    )(in_hbm(cot), cot_par, in_hbm(w))[0]


def far_slot(me):
    return (me & 1) ^ ((me >> 1) & 1)


def forward_kernel(
    direct, n_dp, q_own, q_par, own, par, far_own, far_par, after,
    probs, att_own, att_back, att_t,
):
    rate = math.log2(math.e) / math.sqrt(HD)
    tokens, half = q_own.shape[0] - FLAG_ROWS, q_own.shape[1]
    pairs = half // HD
    me = lax.axis_index("seq")
    left = lax.broadcasted_iota(jnp.int32, (1, 2 * tokens), 1) < tokens

    def barred(x, place):
        flag = x[tokens : tokens + FLAG_ROWS, :].astype(F32)[:1, place : place + 1]
        return jnp.where(jnp.broadcast_to(flag, (1, 2 * tokens)) > 0, 0.0, -jnp.inf)

    bias = (
        jnp.where(left, 0.0, barred(q_par, 0)),
        jnp.where(left, barred(q_own, 0), 0.0),
        jnp.where(left, barred(q_own, half - 1), barred(q_par, half - 1)),
    )
    for j in range(pairs):
        cols = slice(j * HD, (j + 1) * HD)
        qo, qp = q_own[:tokens, cols], q_par[:tokens, cols]
        q = jnp.concatenate([qo, qp], axis=0)
        k = jnp.concatenate([own[:tokens, cols], par[:tokens, cols]], axis=0)
        v = jnp.concatenate([own[tokens:, cols], par[tokens:, cols]], axis=0)
        near = dot(k, q, 1, 1)
        far = jnp.concatenate(
            [dot(far_own[:tokens, cols], qo, 1, 1), dot(far_par[:tokens, cols], qp, 1, 1)], axis=1
        )
        s = [near[:tokens] + bias[0], near[tokens:] + bias[1], far + bias[2]]
        top = jnp.max(jnp.maximum(jnp.maximum(s[0], s[1]), s[2]), axis=0, keepdims=True)
        e = [jnp.exp2((x - top) * rate) for x in s]
        inv = 1.0 / jnp.sum(e[0] + e[1] + e[2], axis=0, keepdims=True)
        low = [(x * inv).astype(BF16) for x in e]
        for i in range(3):
            probs[j, i * tokens : (i + 1) * tokens, :] = low[i]
        vfo, vfp = far_own[tokens:, cols], far_par[tokens:, cols]
        o_t = dot(v, jnp.concatenate(low[:2], axis=0), 0, 0)
        o_t += jnp.concatenate(
            [dot(vfo, low[2][:, :tokens], 0, 0), dot(vfp, low[2][:, tokens:], 0, 0)], axis=1
        )
        o = o_t.T.astype(BF16)
        att_own[:, cols] = o[:tokens]
        att_back[:, cols] = o[tokens:]
        o_low = o_t.astype(BF16)
        if direct:
            rows = HD // n_dp
            place = bit_reversed(j ^ (me >> 1), (pairs - 1).bit_length())
            for d in range(n_dp):
                block = bit_reversed((d ^ lax.axis_index("dp")) >> 1, (n_dp // 2 - 1).bit_length())
                start = pl.multiple_of((block * pairs + place) * rows, rows)
                att_t[(d ^ lax.axis_index("dp")) & 1, pl.ds(start, rows), :] = o_low[d * rows : (d + 1) * rows, :]
        else:
            att_t[cols, :] = o_low


def forward(inputs, after, n_seq, n_dp):
    tokens, half = inputs[0].shape[0] - FLAG_ROWS, inputs[0].shape[1]
    features = 2 * half
    heads, pairs = features // HD, half // HD
    direct = n_seq == heads and HD % n_dp == 0 and (HD // n_dp) % 16 == 0
    one = shape_of(tokens, half)
    turned = shape_of(2, half // 2, 2 * tokens) if direct else shape_of(half, 2 * tokens)
    probs, att_own, att_back, turned = call(
        functools.partial(forward_kernel, direct, n_dp),
        (shape_of(pairs, 3 * tokens, 2 * tokens), one, one, turned),
        [VMEM] * 6 + [ANY],
        "patch_forward",
    )(*inputs, after)
    if not direct:
        here = lax.axis_index("seq")
        bits, d_bits = (n_seq - 1).bit_length(), (n_dp // 2 - 1).bit_length()
        order = jnp.array([bit_reversed(i, bits) for i in range(n_seq)], jnp.int32) ^ here
        d_order = [bit_reversed(i, d_bits) * 2 + c for c in range(2) for i in range(n_dp // 2)]
        full = jnp.zeros((heads // 2, 2, HD, 2 * tokens), BF16)
        full = lax.dynamic_update_slice(
            full, turned.reshape(heads // 2, 1, HD, 2 * tokens), (0, here & 1, 0, 0)
        )
        full = full.reshape(n_seq, n_dp, features // (n_seq * n_dp), 2 * tokens)
        full = jnp.take(full, order, axis=0)
        full = jnp.take(full, jnp.array(d_order, jnp.int32) ^ lax.axis_index("dp"), axis=1).transpose(1, 0, 2, 3)
        turned = full.reshape(2, features // 2, 2 * tokens)
    return probs, att_own, att_back, turned, 2 if direct else 1


def backward_kernel(
    q_own, q_par, own, par, far_own, far_par, ga, probs, grads, edge_a, edge_b
):
    scale = 1.0 / math.sqrt(HD)
    tokens, half = q_own.shape[0] - FLAG_ROWS, q_own.shape[1]
    slot = far_slot(lax.axis_index("seq"))
    last = slice(2 * tokens, 3 * tokens)
    for j in range(half // HD):
        cols = slice(j * HD, (j + 1) * HD)
        g_both = ga[:, cols]
        go, gp = g_both[:tokens], g_both[tokens:]
        qo, qp = q_own[:tokens, cols], q_par[:tokens, cols]
        v = jnp.concatenate([own[tokens:, cols], par[tokens:, cols]], axis=0)
        vfo, vfp = far_own[tokens:, cols], far_par[tokens:, cols]
        gn = dot(v, g_both, 1, 1)
        g = [
            gn[:tokens],
            gn[tokens:],
            jnp.concatenate([dot(vfo, go, 1, 1), dot(vfp, gp, 1, 1)], axis=1),
        ]
        p = [probs[j, i * tokens : (i + 1) * tokens, :].astype(F32) for i in range(3)]
        delta = jnp.sum(p[0] * g[0] + p[1] * g[1] + p[2] * g[2], axis=0, keepdims=True)
        ds = [(p[i] * (g[i] - delta)).astype(BF16) for i in range(3)]
        for i in range(3):
            grads[j, i * tokens : (i + 1) * tokens, :] = ds[i]
        dfo, dfp = ds[2][:, :tokens], ds[2][:, tokens:]
        own_far = jnp.concatenate(
            [dot(dfo, qo, 1, 0) * scale, dot(probs[j, last, :tokens], go, 1, 0)], axis=0
        ).astype(BF16)
        par_far = jnp.concatenate(
            [dot(dfp, qp, 1, 0) * scale, dot(probs[j, last, tokens:], gp, 1, 0)], axis=0
        ).astype(BF16)
        edge_a[:, cols] = jnp.where(slot == 0, own_far, par_far)
        edge_b[:, cols] = jnp.where(slot == 0, par_far, own_far)


def backward(inputs, ga, probs):
    tokens, half = inputs[0].shape[0] - FLAG_ROWS, inputs[0].shape[1]
    return call(
        backward_kernel,
        (shape_of(*probs.shape),) + (shape_of(2 * tokens, half),) * 2,
        [VMEM] * 8,
        "patch_backward",
    )(*inputs, ga, probs)


def gradient_kernel(
    q_own, q_par, own, par, far_own, far_par, ga, probs, grads, dq_own, dq_back, d_own, d_par
):
    scale = 1.0 / math.sqrt(HD)
    tokens, half = q_own.shape[0] - FLAG_ROWS, q_own.shape[1]
    near, last = slice(0, 2 * tokens), slice(2 * tokens, 3 * tokens)
    for j in range(half // HD):
        cols = slice(j * HD, (j + 1) * HD)
        q = jnp.concatenate([q_own[:tokens, cols], q_par[:tokens, cols]], axis=0)
        k = jnp.concatenate([own[:tokens, cols], par[:tokens, cols]], axis=0)
        kfo, kfp = far_own[:tokens, cols], far_par[:tokens, cols]
        low, dsn = probs[j, near, :], grads[j, near, :]
        dfo, dfp = grads[j, last, :tokens], grads[j, last, tokens:]
        dq = dot(dsn, k, 0, 0) + jnp.concatenate([dot(dfo, kfo, 0, 0), dot(dfp, kfp, 0, 0)], axis=0)
        dq = (dq * scale).astype(BF16)
        dq_own[:, cols] = dq[:tokens]
        dq_back[:, cols] = dq[tokens:]
        dk = (dot(dsn, q, 1, 0) * scale).astype(BF16)
        dv = dot(low, ga[:, cols], 1, 0).astype(BF16)
        d_own[:tokens, cols] = dk[:tokens]
        d_par[:tokens, cols] = dk[tokens:]
        d_own[tokens:, cols] = dv[:tokens]
        d_par[tokens:, cols] = dv[tokens:]


def gradients(inputs, ga, probs, grads):
    tokens, half = inputs[0].shape[0] - FLAG_ROWS, inputs[0].shape[1]
    one, kv = shape_of(tokens, half), shape_of(2 * tokens, half)
    return call(
        gradient_kernel, (one, one, kv, kv), [VMEM] * 9, "patch_gradients"
    )(*inputs, ga, probs, grads)


def weight_kernel(kept, att_keep, att_core, own, par, core_own, core_par, _after, target):
    size = target.shape[0]
    tokens = own.shape[0]
    rows = slice(0, size) if kept else slice(size, 2 * size)
    total = dot(att_keep[rows, :tokens], own[...], 1, 0)
    total += dot(att_keep[rows, tokens:], par[...], 1, 0)
    total += dot(att_core[rows, :tokens], core_own[...], 1, 0)
    total += dot(att_core[rows, tokens:], core_par[...], 1, 0)
    target[...] = total.astype(target.dtype)


def weight_terms(kept, operands, after):
    rows, width = operands[0].shape[0] // 2, operands[2].shape[1]
    return call(
        functools.partial(weight_kernel, kept),
        (shape_of(rows, width, dtype=F32 if kept else BF16),),
        [VMEM] * 6 + [ANY],
        "weight_terms_kept" if kept else "weight_terms_sent",
    )(*operands, after)[0]


def query_kernel(att_own, att_back, dq_own, dq_back, w, out, dq, att):
    mine = lax.axis_index("seq") & 1
    for j in range(att_own.shape[1] // HD):
        cols = slice(j * HD, (j + 1) * HD)
        att[:, head_cols(j, mine)] = att_own[:, cols]
        att[:, head_cols(j, 1 - mine)] = att_back[:, cols]
        dq[:, head_cols(j, mine)] = dq_own[:, cols]
        dq[:, head_cols(j, 1 - mine)] = dq_back[:, cols]
    out[...] = dot(att[...], w[...], 1, 0).astype(BF16)


def finish_queries(att_own, att_back, dq_own, dq_back, w):
    tokens = att_own.shape[0]
    return call(
        query_kernel,
        (shape_of(tokens, w.shape[1]), shape_of(tokens, w.shape[0])),
        [VMEM] * 5,
        "finish_queries",
        scratch=[pltpu.VMEM((tokens, w.shape[0]), BF16)],
    )(att_own, att_back, dq_own, dq_back, w)


def returned_kernel(d_par, far_a, far_b, total):
    slot = far_slot(lax.axis_index("seq"))
    returned = jnp.where(slot == 0, far_b[...].astype(F32), far_a[...].astype(F32))
    total[...] = (d_par[...].astype(F32) + returned).astype(BF16)


def add_returned(d_par, far):
    return call(
        returned_kernel, (shape_of(*d_par.shape),), [VMEM] * 3, "add_returned"
    )(d_par, *far)[0]


def key_kernel(own, far_a, far_b, home, keep, out, dk, dv, total):
    mine = lax.axis_index("seq") & 1
    slot = far_slot(lax.axis_index("seq"))
    tokens = dk.shape[0]
    for i, target in ((0, dk), (1, dv)):
        rows = slice(i * tokens, (i + 1) * tokens)
        for j in range(own.shape[1] // HD):
            cols = slice(j * HD, (j + 1) * HD)
            far = jnp.where(slot == 0, far_a[rows, cols].astype(F32), far_b[rows, cols].astype(F32))
            target[:, head_cols(j, mine)] = (own[rows, cols].astype(F32) + far).astype(BF16)
            target[:, head_cols(j, 1 - mine)] = home[rows, cols]
    total[...] = keep[...] + out[...].astype(F32)


def finish_keys(own, far, home, keep, out):
    tokens, half = own.shape[0] // 2, own.shape[1]
    return call(
        key_kernel,
        (shape_of(tokens, 2 * half),) * 2 + (shape_of(*keep.shape, dtype=F32),),
        [VMEM] * 6,
        "finish_keys",
    )(own, *far, home, keep, out)


def on_device(queries, key_states, values, w_out, cotangent, neighbours, counts):
    n_seq, n_dp = lax.axis_size("seq"), lax.axis_size("dp")
    cot = cotangent[0]

    swap = [(i, i ^ 1) for i in range(n_seq)]
    relay = [(i, i + 2) for i in range(0, n_seq, 2) if i + 2 < n_seq]
    relay += [(i, i - 2) for i in range(1, n_seq, 2) if i - 2 >= 0]
    outer = [(b, a) for a, b in relay]
    edges = [[], []]
    for i in range(n_seq):
        edges[1].append((i, i ^ 2))
        other = i + 2 if (i >> 1) & 1 else i - 2
        if 0 <= other < n_seq:
            edges[0].append((i, other))
    send = lambda x, pairs: lax.ppermute(x, "seq", pairs)
    across = lambda x, k: lax.ppermute(x, "dp", [(i, i ^ k) for i in range(n_dp)])

    kv_send, own, q_send, q_own = pack(
        neighbours[0], queries[0], key_states[0], values[0]
    )
    par = send(kv_send, swap)
    q_par = send(q_send, swap)
    far_par = send(own, outer)
    cot_par = send(cot, swap)
    far_own = send(par, relay)
    core_own, core_par = across(cot, 1), across(cot_par, 1)
    ga = grad_attended(cot, cot_par, w_out)

    inputs = (q_own, q_par, own, par, far_own, far_par)
    probs, att_own, att_back, att_t, step = forward(
        inputs, ga, n_seq, n_dp
    )
    att_core = across(att_t[1], 1)
    att_back = send(att_back, swap)
    grads, *leaving = backward(inputs, ga, probs)
    operands = (att_t[0], att_core, cot, cot_par, core_own, core_par)
    out = weight_terms(False, operands, leaving[0])
    keep = weight_terms(True, operands, out)
    far = [send(leaving[i], edges[i]) for i in range(2)]
    dq_own, dq_back, d_own, d_par = gradients(inputs, ga, probs, grads)
    dq_back = send(dq_back, swap)
    home = send(add_returned(d_par, far), swap)

    hops = []
    bit = 2
    while bit < n_dp:
        hops.append(("dp", n_dp, bit))
        bit *= 2
    while step < n_seq:
        hops.append(("seq", n_seq, step))
        step *= 2
    for place, (axis, count, bit) in enumerate(hops):
        out = lax.ppermute(out, axis, [(i, i ^ bit) for i in range(count)])
        if place == 0:
            out, d_own = lax.optimization_barrier((out, d_own))
        if place + 1 < len(hops):
            total = keep + out.astype(F32)
            rows = total.shape[0] // 2
            keep, out = total[:rows], total[rows:].astype(BF16)

    output, dq = finish_queries(att_own, att_back, dq_own, dq_back, w_out)
    dk, dv, total = finish_keys(d_own, far, home, keep, out)
    return (output[None], dq[None], dk[None], dv[None], total)


def solution(mesh):
    placed = (
        P("dp", "seq", None),
        P("dp", "seq", None),
        P("dp", "seq", None),
        P(),
        P("dp", "seq", None),
        P("dp", "seq", None),
        P("dp", "seq"),
    )
    return jax.shard_map(
        on_device,
        mesh=mesh,
        in_specs=placed,
        out_specs=(
            P("dp", "seq", None),
            P("dp", "seq", None),
            P("dp", "seq", None),
            P("dp", "seq", None),
            P(("seq", "dp"), None),
        ),
        check_vma=False,
    )
```

```python
import functools
import math

import jax
import jax.numpy as jnp
from jax import lax
from jax.experimental import pallas as pl
from jax.experimental.pallas import tpu as pltpu
from jax.sharding import PartitionSpec as P

HD = 128
VMEM_LIMIT = 12 * 1024 * 1024
F32 = jnp.float32
BF16 = jnp.bfloat16
VMEM = pl.BlockSpec(memory_space=pltpu.VMEM)
HBM = pl.BlockSpec(memory_space=pltpu.HBM)
ANY = pl.BlockSpec(memory_space=pl.ANY)
FLAG_ROWS = 16


def dot(a, b, ca, cb):
    return lax.dot_general(a, b, (((ca,), (cb,)), ((), ())), preferred_element_type=F32)


def bit_reversed(index, bits):
    out = 0
    for b in range(bits):
        out = out * 2 + ((index >> b) & 1)
    return out


def shape_of(*dims, dtype=BF16):
    return jax.ShapeDtypeStruct(dims, dtype)


def call(body, out_shape, in_specs, name, scratch=()):
    return pl.pallas_call(
        body,
        out_shape=out_shape,
        in_specs=in_specs,
        out_specs=(VMEM,) * len(out_shape),
        scratch_shapes=list(scratch),
        compiler_params=pltpu.CompilerParams(vmem_limit_bytes=VMEM_LIMIT),
        cost_estimate=pl.CostEstimate(flops=0, bytes_accessed=0, transcendentals=0),
        name=name,
    )


def head_cols(pair, parity):
    return pl.ds(pl.multiple_of((2 * pair + parity) * HD, HD), HD)


def listed_flags(me, listed):
    far_patch = jnp.where(me % 2 == 0, me - 1, me + 1)
    near, far = jnp.int32(0), jnp.int32(0)
    for slot in range(listed.shape[1]):
        near = jnp.where(listed[0, slot] == (me ^ 1), 1, near)
        far = jnp.where(listed[0, slot] == far_patch, 1, far)
    return near, far


def in_hbm(x):
    return pltpu.with_memory_space_constraint(x, pltpu.HBM)


def pack_kernel(listed, q, k, v, kv_send, kv_keep, q_send, q_keep, listed_in, sems):
    mine = lax.axis_index("seq") & 1
    tokens, half = q_keep.shape[0] - FLAG_ROWS, q_keep.shape[1]
    copies = []

    def copy(source, target):
        copies.append(pltpu.make_async_copy(source, target, sems.at[len(copies)]))
        copies[-1].start()

    copy(listed, listed_in)
    for kv, q_to, parity in ((kv_send, q_send, 1 - mine), (kv_keep, q_keep, mine)):
        for source, target, row in ((k, kv, 0), (v, kv, tokens), (q, q_to, 0)):
            for j in range(half // HD):
                copy(
                    source.at[:, head_cols(j, parity)],
                    target.at[row : row + tokens, j * HD : (j + 1) * HD],
                )
    copies[0].wait()
    near, far = listed_flags(lax.axis_index("seq"), listed_in)
    left = lax.broadcasted_iota(jnp.int32, (FLAG_ROWS, half), 1) < half // 2
    flags = jnp.where(left, near, far).astype(F32).astype(BF16)
    q_send[tokens : tokens + FLAG_ROWS, :] = flags
    q_keep[tokens : tokens + FLAG_ROWS, :] = flags
    for item in copies[1:]:
        item.wait()


def pack(listed, q, k, v):
    tokens, features = k.shape
    half = features // 2
    kv = shape_of(2 * tokens, half)
    return call(
        pack_kernel,
        (kv, kv) + (shape_of(tokens + FLAG_ROWS, half),) * 2,
        [HBM] * 4,
        "pack_heads",
        scratch=[
            pltpu.SMEM(listed.shape, jnp.int32),
            pltpu.SemaphoreType.DMA((3 * features // HD + 1,)),
        ],
    )(*[in_hbm(x) for x in (listed, q, k, v)])


def turn_kernel(cot, cot_par, w, ga, cot_in, w_in, sems):
    tokens = cot.shape[0]
    pairs = ga.shape[1] // HD
    copies = [pltpu.make_async_copy(cot, cot_in, sems.at[pairs])]
    for j in range(pairs):
        rows = w.at[head_cols(j, lax.axis_index("seq") & 1), :]
        copies.append(pltpu.make_async_copy(rows, w_in.at[j], sems.at[j]))
    for item in copies:
        item.start()
    copies[0].wait()
    for j in range(pairs):
        cols = slice(j * HD, (j + 1) * HD)
        copies[j + 1].wait()
        ga[:tokens, cols] = dot(cot_in[...], w_in[j], 1, 1).astype(BF16)
        ga[tokens:, cols] = dot(cot_par[...], w_in[j], 1, 1).astype(BF16)


def grad_attended(cot, cot_par, w):
    tokens, width = cot.shape
    pairs = w.shape[0] // (2 * HD)
    return call(
        turn_kernel,
        (shape_of(2 * tokens, pairs * HD),),
        [HBM, VMEM, HBM],
        "grad_attended",
        scratch=[
            pltpu.VMEM((tokens, width), BF16),
            pltpu.VMEM((pairs, HD, width), BF16),
            pltpu.SemaphoreType.DMA((pairs + 1,)),
        ],
    )(in_hbm(cot), cot_par, in_hbm(w))[0]


def far_slot(me):
    return (me & 1) ^ ((me >> 1) & 1)


def forward_kernel(
    direct, n_dp, q_own, q_par, own, par, far_own, far_par, after,
    probs, att_own, att_back, att_t,
):
    rate = math.log2(math.e) / math.sqrt(HD)
    tokens, half = q_own.shape[0] - FLAG_ROWS, q_own.shape[1]
    pairs = half // HD
    me = lax.axis_index("seq")
    left = lax.broadcasted_iota(jnp.int32, (1, 2 * tokens), 1) < tokens

    def barred(x, place):
        flag = x[tokens : tokens + FLAG_ROWS, :].astype(F32)[:1, place : place + 1]
        return jnp.where(jnp.broadcast_to(flag, (1, 2 * tokens)) > 0, 0.0, -jnp.inf)

    bias = (
        jnp.where(left, 0.0, barred(q_par, 0)),
        jnp.where(left, barred(q_own, 0), 0.0),
        jnp.where(left, barred(q_own, half - 1), barred(q_par, half - 1)),
    )
    for j in range(pairs):
        cols = slice(j * HD, (j + 1) * HD)
        qo, qp = q_own[:tokens, cols], q_par[:tokens, cols]
        q = jnp.concatenate([qo, qp], axis=0)
        k = jnp.concatenate([own[:tokens, cols], par[:tokens, cols]], axis=0)
        v = jnp.concatenate([own[tokens:, cols], par[tokens:, cols]], axis=0)
        near = dot(k, q, 1, 1)
        far = jnp.concatenate(
            [dot(far_own[:tokens, cols], qo, 1, 1), dot(far_par[:tokens, cols], qp, 1, 1)], axis=1
        )
        s = [near[:tokens] + bias[0], near[tokens:] + bias[1], far + bias[2]]
        top = jnp.max(jnp.maximum(jnp.maximum(s[0], s[1]), s[2]), axis=0, keepdims=True)
        e = [jnp.exp2((x - top) * rate) for x in s]
        inv = 1.0 / jnp.sum(e[0] + e[1] + e[2], axis=0, keepdims=True)
        low = [(x * inv).astype(BF16) for x in e]
        for i in range(3):
            probs[j, i * tokens : (i + 1) * tokens, :] = low[i]
        vfo, vfp = far_own[tokens:, cols], far_par[tokens:, cols]
        o_t = dot(v, jnp.concatenate(low[:2], axis=0), 0, 0)
        o_t += jnp.concatenate(
            [dot(vfo, low[2][:, :tokens], 0, 0), dot(vfp, low[2][:, tokens:], 0, 0)], axis=1
        )
        o_low = o_t.astype(BF16)
        o = o_low.T
        att_own[:, cols] = o[:tokens]
        att_back[:, cols] = o[tokens:]
        if direct:
            rows = HD // n_dp
            place = bit_reversed(j ^ (me >> 1), (pairs - 1).bit_length())
            for d in range(n_dp):
                block = bit_reversed((d ^ lax.axis_index("dp")) >> 1, (n_dp // 2 - 1).bit_length())
                start = pl.multiple_of((block * pairs + place) * rows, rows)
                att_t[(d ^ lax.axis_index("dp")) & 1, pl.ds(start, rows), :] = o_low[d * rows : (d + 1) * rows, :]
        else:
            att_t[cols, :] = o_low


def forward(inputs, after, n_seq, n_dp):
    tokens, half = inputs[0].shape[0] - FLAG_ROWS, inputs[0].shape[1]
    features = 2 * half
    heads, pairs = features // HD, half // HD
    direct = n_seq == heads and HD % n_dp == 0 and (HD // n_dp) % 16 == 0
    one = shape_of(tokens, half)
    turned = shape_of(2, half // 2, 2 * tokens) if direct else shape_of(half, 2 * tokens)
    probs, att_own, att_back, turned = call(
        functools.partial(forward_kernel, direct, n_dp),
        (shape_of(pairs, 3 * tokens, 2 * tokens), one, one, turned),
        [VMEM] * 6 + [ANY],
        "patch_forward",
    )(*inputs, after)
    if not direct:
        here = lax.axis_index("seq")
        bits, d_bits = (n_seq - 1).bit_length(), (n_dp // 2 - 1).bit_length()
        order = jnp.array([bit_reversed(i, bits) for i in range(n_seq)], jnp.int32) ^ here
        d_order = [bit_reversed(i, d_bits) * 2 + c for c in range(2) for i in range(n_dp // 2)]
        full = jnp.zeros((heads // 2, 2, HD, 2 * tokens), BF16)
        full = lax.dynamic_update_slice(
            full, turned.reshape(heads // 2, 1, HD, 2 * tokens), (0, here & 1, 0, 0)
        )
        full = full.reshape(n_seq, n_dp, features // (n_seq * n_dp), 2 * tokens)
        full = jnp.take(full, order, axis=0)
        full = jnp.take(full, jnp.array(d_order, jnp.int32) ^ lax.axis_index("dp"), axis=1).transpose(1, 0, 2, 3)
        turned = full.reshape(2, features // 2, 2 * tokens)
    return probs, att_own, att_back, turned, 2 if direct else 1


def backward_kernel(
    q_own, q_par, own, par, far_own, far_par, ga, probs, grads, edge_a, edge_b
):
    scale = 1.0 / math.sqrt(HD)
    tokens, half = q_own.shape[0] - FLAG_ROWS, q_own.shape[1]
    slot = far_slot(lax.axis_index("seq"))
    last = slice(2 * tokens, 3 * tokens)
    for j in range(half // HD):
        cols = slice(j * HD, (j + 1) * HD)
        g_both = ga[:, cols]
        go, gp = g_both[:tokens], g_both[tokens:]
        qo, qp = q_own[:tokens, cols], q_par[:tokens, cols]
        v = jnp.concatenate([own[tokens:, cols], par[tokens:, cols]], axis=0)
        vfo, vfp = far_own[tokens:, cols], far_par[tokens:, cols]
        gn = dot(v, g_both, 1, 1)
        g = [
            gn[:tokens],
            gn[tokens:],
            jnp.concatenate([dot(vfo, go, 1, 1), dot(vfp, gp, 1, 1)], axis=1),
        ]
        p = [probs[j, i * tokens : (i + 1) * tokens, :].astype(F32) for i in range(3)]
        delta = jnp.sum(p[0] * g[0] + p[1] * g[1] + p[2] * g[2], axis=0, keepdims=True)
        ds = [(p[i] * (g[i] - delta)).astype(BF16) for i in range(3)]
        for i in range(3):
            grads[j, i * tokens : (i + 1) * tokens, :] = ds[i]
        dfo, dfp = ds[2][:, :tokens], ds[2][:, tokens:]
        own_far = jnp.concatenate(
            [dot(dfo, qo, 1, 0) * scale, dot(probs[j, last, :tokens], go, 1, 0)], axis=0
        ).astype(BF16)
        par_far = jnp.concatenate(
            [dot(dfp, qp, 1, 0) * scale, dot(probs[j, last, tokens:], gp, 1, 0)], axis=0
        ).astype(BF16)
        edge_a[:, cols] = jnp.where(slot == 0, own_far, par_far)
        edge_b[:, cols] = jnp.where(slot == 0, par_far, own_far)


def backward(inputs, ga, probs):
    tokens, half = inputs[0].shape[0] - FLAG_ROWS, inputs[0].shape[1]
    return call(
        backward_kernel,
        (shape_of(*probs.shape),) + (shape_of(2 * tokens, half),) * 2,
        [VMEM] * 8,
        "patch_backward",
    )(*inputs, ga, probs)


def gradient_kernel(
    q_own, q_par, own, par, far_own, far_par, ga, probs, grads, dq_own, dq_back, d_own, d_par
):
    scale = 1.0 / math.sqrt(HD)
    tokens, half = q_own.shape[0] - FLAG_ROWS, q_own.shape[1]
    near, last = slice(0, 2 * tokens), slice(2 * tokens, 3 * tokens)
    for j in range(half // HD):
        cols = slice(j * HD, (j + 1) * HD)
        q = jnp.concatenate([q_own[:tokens, cols], q_par[:tokens, cols]], axis=0)
        k = jnp.concatenate([own[:tokens, cols], par[:tokens, cols]], axis=0)
        kfo, kfp = far_own[:tokens, cols], far_par[:tokens, cols]
        low, dsn = probs[j, near, :], grads[j, near, :]
        dfo, dfp = grads[j, last, :tokens], grads[j, last, tokens:]
        dq = dot(dsn, k, 0, 0) + jnp.concatenate([dot(dfo, kfo, 0, 0), dot(dfp, kfp, 0, 0)], axis=0)
        dq = (dq * scale).astype(BF16)
        dq_own[:, cols] = dq[:tokens]
        dq_back[:, cols] = dq[tokens:]
        dk = (dot(dsn, q, 1, 0) * scale).astype(BF16)
        dv = dot(low, ga[:, cols], 1, 0).astype(BF16)
        d_own[:tokens, cols] = dk[:tokens]
        d_par[:tokens, cols] = dk[tokens:]
        d_own[tokens:, cols] = dv[:tokens]
        d_par[tokens:, cols] = dv[tokens:]


def gradients(inputs, ga, probs, grads):
    tokens, half = inputs[0].shape[0] - FLAG_ROWS, inputs[0].shape[1]
    one, kv = shape_of(tokens, half), shape_of(2 * tokens, half)
    return call(
        gradient_kernel, (one, one, kv, kv), [VMEM] * 9, "patch_gradients"
    )(*inputs, ga, probs, grads)


def weight_kernel(kept, att_keep, att_core, own, par, core_own, core_par, _after, target):
    size = target.shape[0]
    tokens = own.shape[0]
    rows = slice(0, size) if kept else slice(size, 2 * size)
    total = dot(att_keep[rows, :tokens], own[...], 1, 0)
    total += dot(att_keep[rows, tokens:], par[...], 1, 0)
    total += dot(att_core[rows, :tokens], core_own[...], 1, 0)
    total += dot(att_core[rows, tokens:], core_par[...], 1, 0)
    target[...] = total.astype(target.dtype)


def weight_terms(kept, operands, after):
    rows, width = operands[0].shape[0] // 2, operands[2].shape[1]
    return call(
        functools.partial(weight_kernel, kept),
        (shape_of(rows, width, dtype=F32 if kept else BF16),),
        [VMEM] * 6 + [ANY],
        "weight_terms_kept" if kept else "weight_terms_sent",
    )(*operands, after)[0]


def query_kernel(att_own, att_back, dq_own, dq_back, w, out, dq, att):
    mine = lax.axis_index("seq") & 1
    for j in range(att_own.shape[1] // HD):
        cols = slice(j * HD, (j + 1) * HD)
        att[:, head_cols(j, mine)] = att_own[:, cols]
        att[:, head_cols(j, 1 - mine)] = att_back[:, cols]
        dq[:, head_cols(j, mine)] = dq_own[:, cols]
        dq[:, head_cols(j, 1 - mine)] = dq_back[:, cols]
    out[...] = dot(att[...], w[...], 1, 0).astype(BF16)


def finish_queries(att_own, att_back, dq_own, dq_back, w):
    tokens = att_own.shape[0]
    return call(
        query_kernel,
        (shape_of(tokens, w.shape[1]), shape_of(tokens, w.shape[0])),
        [VMEM] * 5,
        "finish_queries",
        scratch=[pltpu.VMEM((tokens, w.shape[0]), BF16)],
    )(att_own, att_back, dq_own, dq_back, w)


def returned_kernel(d_par, far_a, far_b, total):
    slot = far_slot(lax.axis_index("seq"))
    returned = jnp.where(slot == 0, far_b[...].astype(F32), far_a[...].astype(F32))
    total[...] = (d_par[...].astype(F32) + returned).astype(BF16)


def add_returned(d_par, far):
    return call(
        returned_kernel, (shape_of(*d_par.shape),), [VMEM] * 3, "add_returned"
    )(d_par, *far)[0]


def key_kernel(own, far_a, far_b, home, keep, out, dk, dv, total):
    mine = lax.axis_index("seq") & 1
    slot = far_slot(lax.axis_index("seq"))
    tokens = dk.shape[0]
    for i, target in ((0, dk), (1, dv)):
        rows = slice(i * tokens, (i + 1) * tokens)
        for j in range(own.shape[1] // HD):
            cols = slice(j * HD, (j + 1) * HD)
            far = jnp.where(slot == 0, far_a[rows, cols].astype(F32), far_b[rows, cols].astype(F32))
            target[:, head_cols(j, mine)] = (own[rows, cols].astype(F32) + far).astype(BF16)
            target[:, head_cols(j, 1 - mine)] = home[rows, cols]
    total[...] = keep[...] + out[...].astype(F32)


def finish_keys(own, far, home, keep, out):
    tokens, half = own.shape[0] // 2, own.shape[1]
    return call(
        key_kernel,
        (shape_of(tokens, 2 * half),) * 2 + (shape_of(*keep.shape, dtype=F32),),
        [VMEM] * 6,
        "finish_keys",
    )(own, *far, home, keep, out)


def on_device(queries, key_states, values, w_out, cotangent, neighbours, counts):
    n_seq, n_dp = lax.axis_size("seq"), lax.axis_size("dp")
    cot = cotangent[0]

    swap = [(i, i ^ 1) for i in range(n_seq)]
    relay = [(i, i + 2) for i in range(0, n_seq, 2) if i + 2 < n_seq]
    relay += [(i, i - 2) for i in range(1, n_seq, 2) if i - 2 >= 0]
    outer = [(b, a) for a, b in relay]
    edges = [[], []]
    for i in range(n_seq):
        edges[1].append((i, i ^ 2))
        other = i + 2 if (i >> 1) & 1 else i - 2
        if 0 <= other < n_seq:
            edges[0].append((i, other))
    send = lambda x, pairs: lax.ppermute(x, "seq", pairs)
    across = lambda x, k: lax.ppermute(x, "dp", [(i, i ^ k) for i in range(n_dp)])

    kv_send, own, q_send, q_own = pack(
        neighbours[0], queries[0], key_states[0], values[0]
    )
    par = send(kv_send, swap)
    q_par = send(q_send, swap)
    far_par = send(own, outer)
    cot_par = send(cot, swap)
    far_own = send(par, relay)
    core_own, core_par = across(cot, 1), across(cot_par, 1)
    ga = grad_attended(cot, cot_par, w_out)

    inputs = (q_own, q_par, own, par, far_own, far_par)
    probs, att_own, att_back, att_t, step = forward(
        inputs, ga, n_seq, n_dp
    )
    att_core = across(att_t[1], 1)
    att_back = send(att_back, swap)
    grads, *leaving = backward(inputs, ga, probs)
    operands = (att_t[0], att_core, cot, cot_par, core_own, core_par)
    out = weight_terms(False, operands, leaving[0])
    keep = weight_terms(True, operands, out)
    far = [send(leaving[i], edges[i]) for i in range(2)]
    dq_own, dq_back, d_own, d_par = gradients(inputs, ga, probs, grads)
    dq_back = send(dq_back, swap)
    home = send(add_returned(d_par, far), swap)

    hops = []
    bit = 2
    while bit < n_dp:
        hops.append(("dp", n_dp, bit))
        bit *= 2
    while step < n_seq:
        hops.append(("seq", n_seq, step))
        step *= 2
    for place, (axis, count, bit) in enumerate(hops):
        out = lax.ppermute(out, axis, [(i, i ^ bit) for i in range(count)])
        if place == 0:
            out, d_own, att_back = lax.optimization_barrier((out, d_own, att_back))
        if place + 1 < len(hops):
            total = keep + out.astype(F32)
            rows = total.shape[0] // 2
            keep, out = total[:rows], total[rows:].astype(BF16)

    output, dq = finish_queries(att_own, att_back, dq_own, dq_back, w_out)
    dk, dv, total = finish_keys(d_own, far, home, keep, out)
    return (output[None], dq[None], dk[None], dv[None], total)


def solution(mesh):
    placed = (
        P("dp", "seq", None),
        P("dp", "seq", None),
        P("dp", "seq", None),
        P(),
        P("dp", "seq", None),
        P("dp", "seq", None),
        P("dp", "seq"),
    )
    return jax.shard_map(
        on_device,
        mesh=mesh,
        in_specs=placed,
        out_specs=(
            P("dp", "seq", None),
            P("dp", "seq", None),
            P("dp", "seq", None),
            P("dp", "seq", None),
            P(("seq", "dp"), None),
        ),
        check_vma=False,
    )
```

```python
import functools
import math

import jax
import jax.numpy as jnp
from jax import lax
from jax.experimental import pallas as pl
from jax.experimental.pallas import tpu as pltpu
from jax.sharding import PartitionSpec as P

HD = 128
VMEM_LIMIT = 12 * 1024 * 1024
F32 = jnp.float32
BF16 = jnp.bfloat16
VMEM = pl.BlockSpec(memory_space=pltpu.VMEM)
HBM = pl.BlockSpec(memory_space=pltpu.HBM)
ANY = pl.BlockSpec(memory_space=pl.ANY)
FLAG_ROWS = 16


def dot(a, b, ca, cb):
    return lax.dot_general(a, b, (((ca,), (cb,)), ((), ())), preferred_element_type=F32)


def bit_reversed(index, bits):
    out = 0
    for b in range(bits):
        out = out * 2 + ((index >> b) & 1)
    return out


def shape_of(*dims, dtype=BF16):
    return jax.ShapeDtypeStruct(dims, dtype)


def call(body, out_shape, in_specs, name, scratch=()):
    return pl.pallas_call(
        body,
        out_shape=out_shape,
        in_specs=in_specs,
        out_specs=(VMEM,) * len(out_shape),
        scratch_shapes=list(scratch),
        compiler_params=pltpu.CompilerParams(vmem_limit_bytes=VMEM_LIMIT),
        cost_estimate=pl.CostEstimate(flops=0, bytes_accessed=0, transcendentals=0),
        name=name,
    )


def head_cols(pair, parity):
    return pl.ds(pl.multiple_of((2 * pair + parity) * HD, HD), HD)


def listed_flags(me, listed):
    far_patch = jnp.where(me % 2 == 0, me - 1, me + 1)
    near, far = jnp.int32(0), jnp.int32(0)
    for slot in range(listed.shape[1]):
        near = jnp.where(listed[0, slot] == (me ^ 1), 1, near)
        far = jnp.where(listed[0, slot] == far_patch, 1, far)
    return near, far


def in_hbm(x):
    return pltpu.with_memory_space_constraint(x, pltpu.HBM)


def pack_kernel(listed, q, k, v, kv_send, kv_keep, q_send, q_keep, listed_in, sems):
    mine = lax.axis_index("seq") & 1
    tokens, half = q_keep.shape[0] - FLAG_ROWS, q_keep.shape[1]
    copies = []

    def copy(source, target):
        copies.append(pltpu.make_async_copy(source, target, sems.at[len(copies)]))
        copies[-1].start()

    copy(listed, listed_in)
    for kv, q_to, parity in ((kv_send, q_send, 1 - mine), (kv_keep, q_keep, mine)):
        for source, target, row in ((k, kv, 0), (v, kv, tokens), (q, q_to, 0)):
            for j in range(half // HD):
                copy(
                    source.at[:, head_cols(j, parity)],
                    target.at[row : row + tokens, j * HD : (j + 1) * HD],
                )
    copies[0].wait()
    near, far = listed_flags(lax.axis_index("seq"), listed_in)
    left = lax.broadcasted_iota(jnp.int32, (FLAG_ROWS, half), 1) < half // 2
    flags = jnp.where(left, near, far).astype(F32).astype(BF16)
    q_send[tokens : tokens + FLAG_ROWS, :] = flags
    q_keep[tokens : tokens + FLAG_ROWS, :] = flags
    for item in copies[1:]:
        item.wait()


def pack(listed, q, k, v):
    tokens, features = k.shape
    half = features // 2
    kv = shape_of(2 * tokens, half)
    return call(
        pack_kernel,
        (kv, kv) + (shape_of(tokens + FLAG_ROWS, half),) * 2,
        [HBM] * 4,
        "pack_heads",
        scratch=[
            pltpu.SMEM(listed.shape, jnp.int32),
            pltpu.SemaphoreType.DMA((3 * features // HD + 1,)),
        ],
    )(*[in_hbm(x) for x in (listed, q, k, v)])


def turn_kernel(cot, cot_par, w, ga, cot_in, w_in, sems):
    tokens = cot.shape[0]
    pairs = ga.shape[1] // HD
    copies = [pltpu.make_async_copy(cot, cot_in, sems.at[pairs])]
    for j in range(pairs):
        rows = w.at[head_cols(j, lax.axis_index("seq") & 1), :]
        copies.append(pltpu.make_async_copy(rows, w_in.at[j], sems.at[j]))
    for item in copies:
        item.start()
    copies[0].wait()
    for j in range(pairs):
        cols = slice(j * HD, (j + 1) * HD)
        copies[j + 1].wait()
        ga[:tokens, cols] = dot(cot_in[...], w_in[j], 1, 1).astype(BF16)
        ga[tokens:, cols] = dot(cot_par[...], w_in[j], 1, 1).astype(BF16)


def grad_attended(cot, cot_par, w):
    tokens, width = cot.shape
    pairs = w.shape[0] // (2 * HD)
    return call(
        turn_kernel,
        (shape_of(2 * tokens, pairs * HD),),
        [HBM, VMEM, HBM],
        "grad_attended",
        scratch=[
            pltpu.VMEM((tokens, width), BF16),
            pltpu.VMEM((pairs, HD, width), BF16),
            pltpu.SemaphoreType.DMA((pairs + 1,)),
        ],
    )(in_hbm(cot), cot_par, in_hbm(w))[0]


def far_slot(me):
    return (me & 1) ^ ((me >> 1) & 1)


def forward_kernel(
    direct, n_dp, q_own, q_par, own, par, far_own, far_par, after,
    probs, att_own, att_back, att_t,
):
    rate = math.log2(math.e) / math.sqrt(HD)
    tokens, half = q_own.shape[0] - FLAG_ROWS, q_own.shape[1]
    pairs = half // HD
    me = lax.axis_index("seq")
    left = lax.broadcasted_iota(jnp.int32, (1, 2 * tokens), 1) < tokens

    def barred(x, place):
        flag = x[tokens : tokens + FLAG_ROWS, :].astype(F32)[:1, place : place + 1]
        return jnp.where(jnp.broadcast_to(flag, (1, 2 * tokens)) > 0, 0.0, -jnp.inf)

    bias = (
        jnp.where(left, 0.0, barred(q_par, 0)),
        jnp.where(left, barred(q_own, 0), 0.0),
        jnp.where(left, barred(q_own, half - 1), barred(q_par, half - 1)),
    )
    for j in range(pairs):
        cols = slice(j * HD, (j + 1) * HD)
        qo, qp = q_own[:tokens, cols], q_par[:tokens, cols]
        q = jnp.concatenate([qo, qp], axis=0)
        k = jnp.concatenate([own[:tokens, cols], par[:tokens, cols]], axis=0)
        v = jnp.concatenate([own[tokens:, cols], par[tokens:, cols]], axis=0)
        near = dot(k, q, 1, 1)
        far = jnp.concatenate(
            [dot(far_own[:tokens, cols], qo, 1, 1), dot(far_par[:tokens, cols], qp, 1, 1)], axis=1
        )
        s = [near[:tokens] + bias[0], near[tokens:] + bias[1], far + bias[2]]
        top = jnp.max(jnp.maximum(jnp.maximum(s[0], s[1]), s[2]), axis=0, keepdims=True)
        e = [jnp.exp2((x - top) * rate) for x in s]
        inv = 1.0 / jnp.sum(e[0] + e[1] + e[2], axis=0, keepdims=True)
        low = [(x * inv).astype(BF16) for x in e]
        for i in range(3):
            probs[j, i * tokens : (i + 1) * tokens, :] = low[i]
        vfo, vfp = far_own[tokens:, cols], far_par[tokens:, cols]
        o_t = dot(v, jnp.concatenate(low[:2], axis=0), 0, 0)
        o_t += jnp.concatenate(
            [dot(vfo, low[2][:, :tokens], 0, 0), dot(vfp, low[2][:, tokens:], 0, 0)], axis=1
        )
        o_low = o_t.astype(BF16)
        o = o_low.T
        att_own[:, cols] = o[:tokens]
        att_back[:, cols] = o[tokens:]
        if direct:
            rows = HD // n_dp
            place = bit_reversed(j ^ (me >> 1), (pairs - 1).bit_length())
            for d in range(n_dp):
                block = bit_reversed((d ^ lax.axis_index("dp")) >> 1, (n_dp // 2 - 1).bit_length())
                start = pl.multiple_of((block * pairs + place) * rows, rows)
                att_t[(d ^ lax.axis_index("dp")) & 1, pl.ds(start, rows), :] = o_low[d * rows : (d + 1) * rows, :]
        else:
            att_t[cols, :] = o_low


def forward(inputs, after, n_seq, n_dp):
    tokens, half = inputs[0].shape[0] - FLAG_ROWS, inputs[0].shape[1]
    features = 2 * half
    heads, pairs = features // HD, half // HD
    direct = n_seq == heads and HD % n_dp == 0 and (HD // n_dp) % 16 == 0
    one = shape_of(tokens, half)
    turned = shape_of(2, half // 2, 2 * tokens) if direct else shape_of(half, 2 * tokens)
    probs, att_own, att_back, turned = call(
        functools.partial(forward_kernel, direct, n_dp),
        (shape_of(pairs, 3 * tokens, 2 * tokens), one, one, turned),
        [VMEM] * 6 + [ANY],
        "patch_forward",
    )(*inputs, after)
    if not direct:
        here = lax.axis_index("seq")
        bits, d_bits = (n_seq - 1).bit_length(), (n_dp // 2 - 1).bit_length()
        order = jnp.array([bit_reversed(i, bits) for i in range(n_seq)], jnp.int32) ^ here
        d_order = [bit_reversed(i, d_bits) * 2 + c for c in range(2) for i in range(n_dp // 2)]
        full = jnp.zeros((heads // 2, 2, HD, 2 * tokens), BF16)
        full = lax.dynamic_update_slice(
            full, turned.reshape(heads // 2, 1, HD, 2 * tokens), (0, here & 1, 0, 0)
        )
        full = full.reshape(n_seq, n_dp, features // (n_seq * n_dp), 2 * tokens)
        full = jnp.take(full, order, axis=0)
        full = jnp.take(full, jnp.array(d_order, jnp.int32) ^ lax.axis_index("dp"), axis=1).transpose(1, 0, 2, 3)
        turned = full.reshape(2, features // 2, 2 * tokens)
    return probs, att_own, att_back, turned, 2 if direct else 1


def backward_kernel(
    q_own, q_par, own, par, far_own, far_par, ga, probs, grads, edge_a, edge_b
):
    scale = 1.0 / math.sqrt(HD)
    tokens, half = q_own.shape[0] - FLAG_ROWS, q_own.shape[1]
    slot = far_slot(lax.axis_index("seq"))
    last = slice(2 * tokens, 3 * tokens)
    for j in range(half // HD):
        cols = slice(j * HD, (j + 1) * HD)
        g_both = ga[:, cols]
        go, gp = g_both[:tokens], g_both[tokens:]
        qo, qp = q_own[:tokens, cols], q_par[:tokens, cols]
        v = jnp.concatenate([own[tokens:, cols], par[tokens:, cols]], axis=0)
        vfo, vfp = far_own[tokens:, cols], far_par[tokens:, cols]
        gn = dot(v, g_both, 1, 1)
        g = [
            gn[:tokens],
            gn[tokens:],
            jnp.concatenate([dot(vfo, go, 1, 1), dot(vfp, gp, 1, 1)], axis=1),
        ]
        p = [probs[j, i * tokens : (i + 1) * tokens, :].astype(F32) for i in range(3)]
        delta = jnp.sum(p[0] * g[0] + p[1] * g[1] + p[2] * g[2], axis=0, keepdims=True)
        ds = [(p[i] * (g[i] - delta)).astype(BF16) for i in range(3)]
        for i in range(3):
            grads[j, i * tokens : (i + 1) * tokens, :] = ds[i]
        dfo, dfp = ds[2][:, :tokens], ds[2][:, tokens:]
        own_far = jnp.concatenate(
            [dot(dfo, qo, 1, 0) * scale, dot(probs[j, last, :tokens], go, 1, 0)], axis=0
        ).astype(BF16)
        par_far = jnp.concatenate(
            [dot(dfp, qp, 1, 0) * scale, dot(probs[j, last, tokens:], gp, 1, 0)], axis=0
        ).astype(BF16)
        edge_a[:, cols] = jnp.where(slot == 0, own_far, par_far)
        edge_b[:, cols] = jnp.where(slot == 0, par_far, own_far)


def backward(inputs, ga, probs):
    tokens, half = inputs[0].shape[0] - FLAG_ROWS, inputs[0].shape[1]
    return call(
        backward_kernel,
        (shape_of(*probs.shape),) + (shape_of(2 * tokens, half),) * 2,
        [VMEM] * 8,
        "patch_backward",
    )(*inputs, ga, probs)


def gradient_kernel(
    q_own, q_par, own, par, far_own, far_par, ga, probs, grads, dq_own, dq_back, d_own, d_par
):
    scale = 1.0 / math.sqrt(HD)
    tokens, half = q_own.shape[0] - FLAG_ROWS, q_own.shape[1]
    near, last = slice(0, 2 * tokens), slice(2 * tokens, 3 * tokens)
    for j in range(half // HD):
        cols = slice(j * HD, (j + 1) * HD)
        q = jnp.concatenate([q_own[:tokens, cols], q_par[:tokens, cols]], axis=0)
        k = jnp.concatenate([own[:tokens, cols], par[:tokens, cols]], axis=0)
        kfo, kfp = far_own[:tokens, cols], far_par[:tokens, cols]
        low, dsn = probs[j, near, :], grads[j, near, :]
        dfo, dfp = grads[j, last, :tokens], grads[j, last, tokens:]
        dq = dot(dsn, k, 0, 0) + jnp.concatenate([dot(dfo, kfo, 0, 0), dot(dfp, kfp, 0, 0)], axis=0)
        dq = (dq * scale).astype(BF16)
        dq_own[:, cols] = dq[:tokens]
        dq_back[:, cols] = dq[tokens:]
        dk = (dot(dsn, q, 1, 0) * scale).astype(BF16)
        dv = dot(low, ga[:, cols], 1, 0).astype(BF16)
        d_own[:tokens, cols] = dk[:tokens]
        d_par[:tokens, cols] = dk[tokens:]
        d_own[tokens:, cols] = dv[:tokens]
        d_par[tokens:, cols] = dv[tokens:]


def gradients(inputs, ga, probs, grads):
    tokens, half = inputs[0].shape[0] - FLAG_ROWS, inputs[0].shape[1]
    one, kv = shape_of(tokens, half), shape_of(2 * tokens, half)
    return call(
        gradient_kernel, (one, one, kv, kv), [VMEM] * 9, "patch_gradients"
    )(*inputs, ga, probs, grads)


def weight_kernel(kept, att_keep, att_core, own, par, core_own, core_par, _after, target):
    size = target.shape[0]
    tokens = own.shape[0]
    rows = slice(0, size) if kept else slice(size, 2 * size)
    total = dot(att_keep[rows, :tokens], own[...], 1, 0)
    total += dot(att_keep[rows, tokens:], par[...], 1, 0)
    total += dot(att_core[rows, :tokens], core_own[...], 1, 0)
    total += dot(att_core[rows, tokens:], core_par[...], 1, 0)
    target[...] = total.astype(target.dtype)


def weight_terms(kept, operands, after):
    rows, width = operands[0].shape[0] // 2, operands[2].shape[1]
    return call(
        functools.partial(weight_kernel, kept),
        (shape_of(rows, width, dtype=F32 if kept else BF16),),
        [VMEM] * 6 + [ANY],
        "weight_terms_kept" if kept else "weight_terms_sent",
    )(*operands, after)[0]


def query_kernel(att_own, att_back, dq_own, dq_back, w, out, dq, att):
    mine = lax.axis_index("seq") & 1
    for j in range(att_own.shape[1] // HD):
        cols = slice(j * HD, (j + 1) * HD)
        att[:, head_cols(j, mine)] = att_own[:, cols]
        att[:, head_cols(j, 1 - mine)] = att_back[:, cols]
        dq[:, head_cols(j, mine)] = dq_own[:, cols]
        dq[:, head_cols(j, 1 - mine)] = dq_back[:, cols]
    out[...] = dot(att[...], w[...], 1, 0).astype(BF16)


def finish_queries(att_own, att_back, dq_own, dq_back, w):
    tokens = att_own.shape[0]
    return call(
        query_kernel,
        (shape_of(tokens, w.shape[1]), shape_of(tokens, w.shape[0])),
        [VMEM] * 5,
        "finish_queries",
        scratch=[pltpu.VMEM((tokens, w.shape[0]), BF16)],
    )(att_own, att_back, dq_own, dq_back, w)


def returned_kernel(d_par, far_a, far_b, total):
    slot = far_slot(lax.axis_index("seq"))
    returned = jnp.where(slot == 0, far_b[...].astype(F32), far_a[...].astype(F32))
    total[...] = (d_par[...].astype(F32) + returned).astype(BF16)


def add_returned(d_par, far):
    return call(
        returned_kernel, (shape_of(*d_par.shape),), [VMEM] * 3, "add_returned"
    )(d_par, *far)[0]


def key_kernel(own, far_a, far_b, home, keep, out, dk, dv, total):
    mine = lax.axis_index("seq") & 1
    slot = far_slot(lax.axis_index("seq"))
    tokens = dk.shape[0]
    for i, target in ((0, dk), (1, dv)):
        rows = slice(i * tokens, (i + 1) * tokens)
        for j in range(own.shape[1] // HD):
            cols = slice(j * HD, (j + 1) * HD)
            far = jnp.where(slot == 0, far_a[rows, cols].astype(F32), far_b[rows, cols].astype(F32))
            target[:, head_cols(j, mine)] = (own[rows, cols].astype(F32) + far).astype(BF16)
            target[:, head_cols(j, 1 - mine)] = home[rows, cols]
    total[...] = keep[...] + out[...].astype(F32)


def finish_keys(own, far, home, keep, out):
    tokens, half = own.shape[0] // 2, own.shape[1]
    return call(
        key_kernel,
        (shape_of(tokens, 2 * half),) * 2 + (shape_of(*keep.shape, dtype=F32),),
        [VMEM] * 6,
        "finish_keys",
    )(own, *far, home, keep, out)


def on_device(queries, key_states, values, w_out, cotangent, neighbours, counts):
    n_seq, n_dp = lax.axis_size("seq"), lax.axis_size("dp")
    cot = cotangent[0]

    swap = [(i, i ^ 1) for i in range(n_seq)]
    relay = [(i, i + 2) for i in range(0, n_seq, 2) if i + 2 < n_seq]
    relay += [(i, i - 2) for i in range(1, n_seq, 2) if i - 2 >= 0]
    outer = [(b, a) for a, b in relay]
    edges = [[], []]
    for i in range(n_seq):
        edges[1].append((i, i ^ 2))
        other = i + 2 if (i >> 1) & 1 else i - 2
        if 0 <= other < n_seq:
            edges[0].append((i, other))
    send = lambda x, pairs: lax.ppermute(x, "seq", pairs)
    across = lambda x, k: lax.ppermute(x, "dp", [(i, i ^ k) for i in range(n_dp)])

    kv_send, own, q_send, q_own = pack(
        neighbours[0], queries[0], key_states[0], values[0]
    )
    par = send(kv_send, swap)
    q_par = send(q_send, swap)
    far_par = send(own, outer)
    cot_par = send(cot, swap)
    far_own = send(par, relay)
    core_own, core_par = across(cot, 1), across(cot_par, 1)
    ga = grad_attended(cot, cot_par, w_out)

    inputs = (q_own, q_par, own, par, far_own, far_par)
    probs, att_own, att_back, att_t, step = forward(
        inputs, ga, n_seq, n_dp
    )
    att_core = across(att_t[1], 1)
    att_back = send(att_back, swap)
    grads, *leaving = backward(inputs, ga, probs)
    operands = (att_t[0], att_core, cot, cot_par, core_own, core_par)
    out = weight_terms(False, operands, leaving[0])
    keep = weight_terms(True, operands, out)
    far = [send(leaving[i], edges[i]) for i in range(2)]
    dq_own, dq_back, d_own, d_par = gradients(inputs, ga, probs, grads)
    dq_back = send(dq_back, swap)
    home = send(add_returned(d_par, far), swap)

    hops = []
    bit = 2
    while bit < n_dp:
        hops.append(("dp", n_dp, bit))
        bit *= 2
    while step < n_seq:
        hops.append(("seq", n_seq, step))
        step *= 2
    for place, (axis, count, bit) in enumerate(hops):
        out = lax.ppermute(out, axis, [(i, i ^ bit) for i in range(count)])
        if place == 0:
            out, att_back = lax.optimization_barrier((out, att_back))
        if place + 1 < len(hops):
            total = keep + out.astype(F32)
            rows = total.shape[0] // 2
            keep, out = total[:rows], total[rows:].astype(BF16)

    output, dq = finish_queries(att_own, att_back, dq_own, dq_back, w_out)
    dk, dv, total = finish_keys(d_own, far, home, keep, out)
    return (output[None], dq[None], dk[None], dv[None], total)


def solution(mesh):
    placed = (
        P("dp", "seq", None),
        P("dp", "seq", None),
        P("dp", "seq", None),
        P(),
        P("dp", "seq", None),
        P("dp", "seq", None),
        P("dp", "seq"),
    )
    return jax.shard_map(
        on_device,
        mesh=mesh,
        in_specs=placed,
        out_specs=(
            P("dp", "seq", None),
            P("dp", "seq", None),
            P("dp", "seq", None),
            P("dp", "seq", None),
            P(("seq", "dp"), None),
        ),
        check_vma=False,
    )
```

```python
import functools
import math

import jax
import jax.numpy as jnp
from jax import lax
from jax.experimental import pallas as pl
from jax.experimental.pallas import tpu as pltpu
from jax.sharding import PartitionSpec as P

HD = 128
VMEM_LIMIT = 12 * 1024 * 1024
F32 = jnp.float32
BF16 = jnp.bfloat16
VMEM = pl.BlockSpec(memory_space=pltpu.VMEM)
HBM = pl.BlockSpec(memory_space=pltpu.HBM)
ANY = pl.BlockSpec(memory_space=pl.ANY)
FLAG_ROWS = 16


def dot(a, b, ca, cb):
    return lax.dot_general(a, b, (((ca,), (cb,)), ((), ())), preferred_element_type=F32)


def bit_reversed(index, bits):
    out = 0
    for b in range(bits):
        out = out * 2 + ((index >> b) & 1)
    return out


def shape_of(*dims, dtype=BF16):
    return jax.ShapeDtypeStruct(dims, dtype)


def call(body, out_shape, in_specs, name, scratch=()):
    return pl.pallas_call(
        body,
        out_shape=out_shape,
        in_specs=in_specs,
        out_specs=(VMEM,) * len(out_shape),
        scratch_shapes=list(scratch),
        compiler_params=pltpu.CompilerParams(vmem_limit_bytes=VMEM_LIMIT),
        cost_estimate=pl.CostEstimate(flops=0, bytes_accessed=0, transcendentals=0),
        name=name,
    )


def head_cols(pair, parity):
    return pl.ds(pl.multiple_of((2 * pair + parity) * HD, HD), HD)


def listed_flags(me, listed):
    far_patch = jnp.where(me % 2 == 0, me - 1, me + 1)
    near, far = jnp.int32(0), jnp.int32(0)
    for slot in range(listed.shape[1]):
        near = jnp.where(listed[0, slot] == (me ^ 1), 1, near)
        far = jnp.where(listed[0, slot] == far_patch, 1, far)
    return near, far


def in_hbm(x):
    return pltpu.with_memory_space_constraint(x, pltpu.HBM)


def pack_kernel(listed, q, k, v, kv_send, kv_keep, q_send, q_keep, listed_in, sems):
    mine = lax.axis_index("seq") & 1
    tokens, half = q_keep.shape[0] - FLAG_ROWS, q_keep.shape[1]
    copies = []

    def copy(source, target):
        copies.append(pltpu.make_async_copy(source, target, sems.at[len(copies)]))
        copies[-1].start()

    copy(listed, listed_in)
    for kv, q_to, parity in ((kv_send, q_send, 1 - mine), (kv_keep, q_keep, mine)):
        for source, target, row in ((k, kv, 0), (v, kv, tokens), (q, q_to, 0)):
            for j in range(half // HD):
                copy(
                    source.at[:, head_cols(j, parity)],
                    target.at[row : row + tokens, j * HD : (j + 1) * HD],
                )
    copies[0].wait()
    near, far = listed_flags(lax.axis_index("seq"), listed_in)
    left = lax.broadcasted_iota(jnp.int32, (FLAG_ROWS, half), 1) < half // 2
    flags = jnp.where(left, near, far).astype(F32).astype(BF16)
    q_send[tokens : tokens + FLAG_ROWS, :] = flags
    q_keep[tokens : tokens + FLAG_ROWS, :] = flags
    for item in copies[1:]:
        item.wait()


def pack(listed, q, k, v):
    tokens, features = k.shape
    half = features // 2
    kv = shape_of(2 * tokens, half)
    return call(
        pack_kernel,
        (kv, kv) + (shape_of(tokens + FLAG_ROWS, half),) * 2,
        [HBM] * 4,
        "pack_heads",
        scratch=[
            pltpu.SMEM(listed.shape, jnp.int32),
            pltpu.SemaphoreType.DMA((3 * features // HD + 1,)),
        ],
    )(*[in_hbm(x) for x in (listed, q, k, v)])


def turn_kernel(cot, cot_par, w, ga, cot_in, w_in, sems):
    tokens = cot.shape[0]
    pairs = ga.shape[1] // HD
    copies = [pltpu.make_async_copy(cot, cot_in, sems.at[pairs])]
    for j in range(pairs):
        rows = w.at[head_cols(j, lax.axis_index("seq") & 1), :]
        copies.append(pltpu.make_async_copy(rows, w_in.at[j], sems.at[j]))
    for item in copies:
        item.start()
    copies[0].wait()
    for j in range(pairs):
        cols = slice(j * HD, (j + 1) * HD)
        copies[j + 1].wait()
        ga[:tokens, cols] = dot(cot_in[...], w_in[j], 1, 1).astype(BF16)
        ga[tokens:, cols] = dot(cot_par[...], w_in[j], 1, 1).astype(BF16)


def grad_attended(cot, cot_par, w):
    tokens, width = cot.shape
    pairs = w.shape[0] // (2 * HD)
    return call(
        turn_kernel,
        (shape_of(2 * tokens, pairs * HD),),
        [HBM, VMEM, HBM],
        "grad_attended",
        scratch=[
            pltpu.VMEM((tokens, width), BF16),
            pltpu.VMEM((pairs, HD, width), BF16),
            pltpu.SemaphoreType.DMA((pairs + 1,)),
        ],
    )(in_hbm(cot), cot_par, in_hbm(w))[0]


def far_slot(me):
    return (me & 1) ^ ((me >> 1) & 1)


def forward_kernel(
    direct, n_dp, q_own, q_par, own, par, far_own, far_par, after,
    probs, att_own, att_back, att_t,
):
    rate = math.log2(math.e) / math.sqrt(HD)
    tokens, half = q_own.shape[0] - FLAG_ROWS, q_own.shape[1]
    pairs = half // HD
    me = lax.axis_index("seq")
    left = lax.broadcasted_iota(jnp.int32, (1, 2 * tokens), 1) < tokens

    def barred(x, place):
        flag = x[tokens : tokens + FLAG_ROWS, :].astype(F32)[:1, place : place + 1]
        return jnp.where(jnp.broadcast_to(flag, (1, 2 * tokens)) > 0, 0.0, -jnp.inf)

    bias = (
        jnp.where(left, 0.0, barred(q_par, 0)),
        jnp.where(left, barred(q_own, 0), 0.0),
        jnp.where(left, barred(q_own, half - 1), barred(q_par, half - 1)),
    )
    for j in range(pairs):
        cols = slice(j * HD, (j + 1) * HD)
        qo, qp = q_own[:tokens, cols], q_par[:tokens, cols]
        q = jnp.concatenate([qo, qp], axis=0)
        k = jnp.concatenate([own[:tokens, cols], par[:tokens, cols]], axis=0)
        v = jnp.concatenate([own[tokens:, cols], par[tokens:, cols]], axis=0)
        near = dot(k, q, 1, 1)
        far = jnp.concatenate(
            [dot(far_own[:tokens, cols], qo, 1, 1), dot(far_par[:tokens, cols], qp, 1, 1)], axis=1
        )
        s = [near[:tokens] + bias[0], near[tokens:] + bias[1], far + bias[2]]
        top = jnp.max(jnp.maximum(jnp.maximum(s[0], s[1]), s[2]), axis=0, keepdims=True)
        e = [jnp.exp2((x - top) * rate) for x in s]
        inv = 1.0 / jnp.sum(e[0] + e[1] + e[2], axis=0, keepdims=True)
        low = [(x * inv).astype(BF16) for x in e]
        for i in range(3):
            probs[j, i * tokens : (i + 1) * tokens, :] = low[i]
        vfo, vfp = far_own[tokens:, cols], far_par[tokens:, cols]
        o_t = dot(v, jnp.concatenate(low[:2], axis=0), 0, 0)
        o_t += jnp.concatenate(
            [dot(vfo, low[2][:, :tokens], 0, 0), dot(vfp, low[2][:, tokens:], 0, 0)], axis=1
        )
        o_low = o_t.astype(BF16)
        o = o_low.T
        att_own[:, cols] = o[:tokens]
        att_back[:, cols] = o[tokens:]
        if direct:
            rows = HD // n_dp
            place = bit_reversed(j ^ (me >> 1), (pairs - 1).bit_length())
            for d in range(n_dp):
                block = bit_reversed((d ^ lax.axis_index("dp")) >> 1, (n_dp // 2 - 1).bit_length())
                start = pl.multiple_of((block * pairs + place) * rows, rows)
                att_t[(d ^ lax.axis_index("dp")) & 1, pl.ds(start, rows), :] = o_low[d * rows : (d + 1) * rows, :]
        else:
            att_t[cols, :] = o_low


def forward(inputs, after, n_seq, n_dp):
    tokens, half = inputs[0].shape[0] - FLAG_ROWS, inputs[0].shape[1]
    features = 2 * half
    heads, pairs = features // HD, half // HD
    direct = n_seq == heads and HD % n_dp == 0 and (HD // n_dp) % 16 == 0
    one = shape_of(tokens, half)
    turned = shape_of(2, half // 2, 2 * tokens) if direct else shape_of(half, 2 * tokens)
    probs, att_own, att_back, turned = call(
        functools.partial(forward_kernel, direct, n_dp),
        (shape_of(pairs, 3 * tokens, 2 * tokens), one, one, turned),
        [VMEM] * 6 + [ANY],
        "patch_forward",
    )(*inputs, after)
    if not direct:
        here = lax.axis_index("seq")
        bits, d_bits = (n_seq - 1).bit_length(), (n_dp // 2 - 1).bit_length()
        order = jnp.array([bit_reversed(i, bits) for i in range(n_seq)], jnp.int32) ^ here
        d_order = [bit_reversed(i, d_bits) * 2 + c for c in range(2) for i in range(n_dp // 2)]
        full = jnp.zeros((heads // 2, 2, HD, 2 * tokens), BF16)
        full = lax.dynamic_update_slice(
            full, turned.reshape(heads // 2, 1, HD, 2 * tokens), (0, here & 1, 0, 0)
        )
        full = full.reshape(n_seq, n_dp, features // (n_seq * n_dp), 2 * tokens)
        full = jnp.take(full, order, axis=0)
        full = jnp.take(full, jnp.array(d_order, jnp.int32) ^ lax.axis_index("dp"), axis=1).transpose(1, 0, 2, 3)
        turned = full.reshape(2, features // 2, 2 * tokens)
    return probs, att_own, att_back, turned, 2 if direct else 1


def backward_kernel(
    q_own, q_par, own, par, far_own, far_par, ga, probs, grads, edge_a, edge_b
):
    scale = 1.0 / math.sqrt(HD)
    tokens, half = q_own.shape[0] - FLAG_ROWS, q_own.shape[1]
    slot = far_slot(lax.axis_index("seq"))
    last = slice(2 * tokens, 3 * tokens)
    for j in range(half // HD):
        cols = slice(j * HD, (j + 1) * HD)
        g_both = ga[:, cols]
        go, gp = g_both[:tokens], g_both[tokens:]
        qo, qp = q_own[:tokens, cols], q_par[:tokens, cols]
        v = jnp.concatenate([own[tokens:, cols], par[tokens:, cols]], axis=0)
        vfo, vfp = far_own[tokens:, cols], far_par[tokens:, cols]
        gn = dot(v, g_both, 1, 1)
        g = [
            gn[:tokens],
            gn[tokens:],
            jnp.concatenate([dot(vfo, go, 1, 1), dot(vfp, gp, 1, 1)], axis=1),
        ]
        p = [probs[j, i * tokens : (i + 1) * tokens, :].astype(F32) for i in range(3)]
        delta = jnp.sum(p[0] * g[0] + p[1] * g[1] + p[2] * g[2], axis=0, keepdims=True)
        ds = [(p[i] * (g[i] - delta)).astype(BF16) for i in range(3)]
        for i in range(3):
            grads[j, i * tokens : (i + 1) * tokens, :] = ds[i]
        dfo, dfp = ds[2][:, :tokens], ds[2][:, tokens:]
        own_far = jnp.concatenate(
            [dot(dfo, qo, 1, 0) * scale, dot(probs[j, last, :tokens], go, 1, 0)], axis=0
        ).astype(BF16)
        par_far = jnp.concatenate(
            [dot(dfp, qp, 1, 0) * scale, dot(probs[j, last, tokens:], gp, 1, 0)], axis=0
        ).astype(BF16)
        edge_a[:, cols] = jnp.where(slot == 0, own_far, par_far)
        edge_b[:, cols] = jnp.where(slot == 0, par_far, own_far)


def backward(inputs, ga, probs):
    tokens, half = inputs[0].shape[0] - FLAG_ROWS, inputs[0].shape[1]
    return call(
        backward_kernel,
        (shape_of(*probs.shape),) + (shape_of(2 * tokens, half),) * 2,
        [VMEM] * 8,
        "patch_backward",
    )(*inputs, ga, probs)


def gradient_kernel(
    q_own, q_par, own, par, far_own, far_par, ga, probs, grads, dq_own, dq_back, d_own, d_par
):
    scale = 1.0 / math.sqrt(HD)
    tokens, half = q_own.shape[0] - FLAG_ROWS, q_own.shape[1]
    near, last = slice(0, 2 * tokens), slice(2 * tokens, 3 * tokens)
    for j in range(half // HD):
        cols = slice(j * HD, (j + 1) * HD)
        q = jnp.concatenate([q_own[:tokens, cols], q_par[:tokens, cols]], axis=0)
        k = jnp.concatenate([own[:tokens, cols], par[:tokens, cols]], axis=0)
        kfo, kfp = far_own[:tokens, cols], far_par[:tokens, cols]
        low, dsn = probs[j, near, :], grads[j, near, :]
        dfo, dfp = grads[j, last, :tokens], grads[j, last, tokens:]
        dq = dot(dsn, k, 0, 0) + jnp.concatenate([dot(dfo, kfo, 0, 0), dot(dfp, kfp, 0, 0)], axis=0)
        dq = (dq * scale).astype(BF16)
        dq_own[:, cols] = dq[:tokens]
        dq_back[:, cols] = dq[tokens:]
        dk = (dot(dsn, q, 1, 0) * scale).astype(BF16)
        dv = dot(low, ga[:, cols], 1, 0).astype(BF16)
        d_own[:tokens, cols] = dk[:tokens]
        d_par[:tokens, cols] = dk[tokens:]
        d_own[tokens:, cols] = dv[:tokens]
        d_par[tokens:, cols] = dv[tokens:]


def gradients(inputs, ga, probs, grads):
    tokens, half = inputs[0].shape[0] - FLAG_ROWS, inputs[0].shape[1]
    one, kv = shape_of(tokens, half), shape_of(2 * tokens, half)
    return call(
        gradient_kernel, (one, one, kv, kv), [VMEM] * 9, "patch_gradients"
    )(*inputs, ga, probs, grads)


def weight_kernel(kept, att_keep, att_core, own, par, core_own, core_par, _after, target):
    size = target.shape[0]
    tokens = own.shape[0]
    rows = slice(0, size) if kept else slice(size, 2 * size)
    total = dot(att_keep[rows, :tokens], own[...], 1, 0)
    total += dot(att_keep[rows, tokens:], par[...], 1, 0)
    total += dot(att_core[rows, :tokens], core_own[...], 1, 0)
    total += dot(att_core[rows, tokens:], core_par[...], 1, 0)
    target[...] = total.astype(target.dtype)


def weight_terms(kept, operands, after):
    rows, width = operands[0].shape[0] // 2, operands[2].shape[1]
    return call(
        functools.partial(weight_kernel, kept),
        (shape_of(rows, width, dtype=F32 if kept else BF16),),
        [VMEM] * 6 + [ANY],
        "weight_terms_kept" if kept else "weight_terms_sent",
    )(*operands, after)[0]


def query_kernel(att_own, att_back, dq_own, dq_back, w, out, dq, att):
    mine = lax.axis_index("seq") & 1
    for j in range(att_own.shape[1] // HD):
        cols = slice(j * HD, (j + 1) * HD)
        att[:, head_cols(j, mine)] = att_own[:, cols]
        att[:, head_cols(j, 1 - mine)] = att_back[:, cols]
        dq[:, head_cols(j, mine)] = dq_own[:, cols]
        dq[:, head_cols(j, 1 - mine)] = dq_back[:, cols]
    out[...] = dot(att[...], w[...], 1, 0).astype(BF16)


def finish_queries(att_own, att_back, dq_own, dq_back, w):
    tokens = att_own.shape[0]
    return call(
        query_kernel,
        (shape_of(tokens, w.shape[1]), shape_of(tokens, w.shape[0])),
        [VMEM] * 5,
        "finish_queries",
        scratch=[pltpu.VMEM((tokens, w.shape[0]), BF16)],
    )(att_own, att_back, dq_own, dq_back, w)


def returned_kernel(d_par, far_a, far_b, total):
    slot = far_slot(lax.axis_index("seq"))
    returned = jnp.where(slot == 0, far_b[...], far_a[...]).astype(F32)
    total[...] = (d_par[...].astype(F32) + returned).astype(BF16)


def add_returned(d_par, far):
    return call(
        returned_kernel, (shape_of(*d_par.shape),), [VMEM] * 3, "add_returned"
    )(d_par, *far)[0]


def key_kernel(own, far_a, far_b, home, keep, out, dk, dv, total):
    mine = lax.axis_index("seq") & 1
    slot = far_slot(lax.axis_index("seq"))
    tokens = dk.shape[0]
    for i, target in ((0, dk), (1, dv)):
        rows = slice(i * tokens, (i + 1) * tokens)
        for j in range(own.shape[1] // HD):
            cols = slice(j * HD, (j + 1) * HD)
            far = jnp.where(slot == 0, far_a[rows, cols], far_b[rows, cols]).astype(F32)
            target[:, head_cols(j, mine)] = (own[rows, cols].astype(F32) + far).astype(BF16)
            target[:, head_cols(j, 1 - mine)] = home[rows, cols]
    total[...] = keep[...] + out[...].astype(F32)


def finish_keys(own, far, home, keep, out):
    tokens, half = own.shape[0] // 2, own.shape[1]
    return call(
        key_kernel,
        (shape_of(tokens, 2 * half),) * 2 + (shape_of(*keep.shape, dtype=F32),),
        [VMEM] * 6,
        "finish_keys",
    )(own, *far, home, keep, out)


def on_device(queries, key_states, values, w_out, cotangent, neighbours, counts):
    n_seq, n_dp = lax.axis_size("seq"), lax.axis_size("dp")
    cot = cotangent[0]

    swap = [(i, i ^ 1) for i in range(n_seq)]
    relay = [(i, i + 2) for i in range(0, n_seq, 2) if i + 2 < n_seq]
    relay += [(i, i - 2) for i in range(1, n_seq, 2) if i - 2 >= 0]
    outer = [(b, a) for a, b in relay]
    edges = [[], []]
    for i in range(n_seq):
        edges[1].append((i, i ^ 2))
        other = i + 2 if (i >> 1) & 1 else i - 2
        if 0 <= other < n_seq:
            edges[0].append((i, other))
    send = lambda x, pairs: lax.ppermute(x, "seq", pairs)
    across = lambda x, k: lax.ppermute(x, "dp", [(i, i ^ k) for i in range(n_dp)])

    kv_send, own, q_send, q_own = pack(
        neighbours[0], queries[0], key_states[0], values[0]
    )
    par = send(kv_send, swap)
    q_par = send(q_send, swap)
    far_par = send(own, outer)
    cot_par = send(cot, swap)
    far_own = send(par, relay)
    core_own, core_par = across(cot, 1), across(cot_par, 1)
    ga = grad_attended(cot, cot_par, w_out)

    inputs = (q_own, q_par, own, par, far_own, far_par)
    probs, att_own, att_back, att_t, step = forward(
        inputs, ga, n_seq, n_dp
    )
    att_core = across(att_t[1], 1)
    att_back = send(att_back, swap)
    grads, *leaving = backward(inputs, ga, probs)
    operands = (att_t[0], att_core, cot, cot_par, core_own, core_par)
    out = weight_terms(False, operands, leaving[0])
    keep = weight_terms(True, operands, out)
    far = [send(leaving[i], edges[i]) for i in range(2)]
    dq_own, dq_back, d_own, d_par = gradients(inputs, ga, probs, grads)
    dq_back = send(dq_back, swap)
    home = send(add_returned(d_par, far), swap)

    hops = []
    bit = 2
    while bit < n_dp:
        hops.append(("dp", n_dp, bit))
        bit *= 2
    while step < n_seq:
        hops.append(("seq", n_seq, step))
        step *= 2
    for place, (axis, count, bit) in enumerate(hops):
        out = lax.ppermute(out, axis, [(i, i ^ bit) for i in range(count)])
        if place == 0:
            out, att_back = lax.optimization_barrier((out, att_back))
        if place + 1 < len(hops):
            total = keep + out.astype(F32)
            rows = total.shape[0] // 2
            keep, out = total[:rows], total[rows:].astype(BF16)

    output, dq = finish_queries(att_own, att_back, dq_own, dq_back, w_out)
    dk, dv, total = finish_keys(d_own, far, home, keep, out)
    return (output[None], dq[None], dk[None], dv[None], total)


def solution(mesh):
    placed = (
        P("dp", "seq", None),
        P("dp", "seq", None),
        P("dp", "seq", None),
        P(),
        P("dp", "seq", None),
        P("dp", "seq", None),
        P("dp", "seq"),
    )
    return jax.shard_map(
        on_device,
        mesh=mesh,
        in_specs=placed,
        out_specs=(
            P("dp", "seq", None),
            P("dp", "seq", None),
            P("dp", "seq", None),
            P("dp", "seq", None),
            P(("seq", "dp"), None),
        ),
        check_vma=False,
    )
```
